32 devices in a mesh: tok: 8 (over z, y), head: 4 (over x, core).
Axes of the slice: x: 2, y: 2, z: 4, core: 2. Of those that a mesh axis runs over, the one named last changes fastest.
Arguments:
- tokens: bfloat16 [16384, 768], P('tok'), may hold values from -6 to 6
- latents: bfloat16 [512, 768], P('tok'), may hold values from -6 to 6
- image_groups: int32 [5], replicated, may hold values from 1 to 58, as said below
- read_query: bfloat16 [768, 768], P(None, 'head'), may hold values from -0.4375 to 0.4375
- read_key: bfloat16 [768, 768], P(None, 'head'), may hold values from -0.21875 to 0.21875
- read_value: bfloat16 [768, 768], P(None, 'head'), may hold values from -0.21875 to 0.21875
- read_out: bfloat16 [768, 768], P('head'), may hold values from -1.25 to 1.25
- write_query: bfloat16 [768, 768], P(None, 'head'), may hold values from -0.4375 to 0.4375
- write_key: bfloat16 [768, 768], P(None, 'head'), may hold values from -0.21875 to 0.21875
- write_value: bfloat16 [768, 768], P(None, 'head'), may hold values from -0.21875 to 0.21875
- write_out: bfloat16 [768, 768], P('head'), may hold values from -1.25 to 1.25
- mlp_in: bfloat16 [768, 3072], P(None, 'head'), may hold values from -0.21875 to 0.21875
- mlp_out: bfloat16 [3072, 768], P('head'), may hold values from -0.109375 to 0.109375
- cotangent: bfloat16 [16384, 768], P('tok'), may hold values from -6 to 6
Outputs:
- layer_out: bfloat16 [16384, 768], P(('tok', 'head'))
- input_grad: float32 [16384, 768], P(('tok', 'head'))
- latent_grad: float32 [512, 768], P(('tok', 'head'))
- grad_read_query: float32 [768, 768], P('tok', 'head')
- grad_read_key: float32 [768, 768], P('tok', 'head')
- grad_read_value: float32 [768, 768], P('tok', 'head')
- grad_read_out: float32 [768, 768], P('head', 'tok')
- grad_write_query: float32 [768, 768], P('tok', 'head')
- grad_write_key: float32 [768, 768], P('tok', 'head')
- grad_write_value: float32 [768, 768], P('tok', 'head')
- grad_write_out: float32 [768, 768], P('head', 'tok')
- grad_mlp_in: float32 [768, 3072], P('tok', 'head')
- grad_mlp_out: float32 [3072, 768], P('head', 'tok')
The draws below stay inside these ranges and needn't reach their ends.
Inputs may be any that keep to these rules, and one draw needn't show every extreme that they name: `image_groups`: groups of each image; the counts add up to 64; the middle image is the largest, every other image has 1 or 2 groups.
All inputs are finite; a program needn't handle non-finite values.
Results may differ from the reference program's by a relative error of at most 0.025.
The reference program's roundings to bfloat16 on the way count: a program that leaves them out, or rounds other values in their place, can miss the bound.
Values may be sent and summed in bfloat16 or wider, within the bound.
A program may use at most 256 MiB of HBM per device.

```python
from functools import partial
import jax
import jax.numpy as jnp
from jax import lax

D = 768
HEADS = 12
HD = 64
FF = 3072
GROUP = 256
LPG = 8
SMALL = 2
NGROUPS = 64
TOKENS = 16384
NLAT = 512


def draw_image_groups(key, part):
    key = jax.random.fold_in(key, 17)
    flips = jax.random.randint(key, (SMALL,), 0, 2, dtype=jnp.int32)
    before = (1 + flips).astype(jnp.int32)
    after = (2 - flips).astype(jnp.int32)
    largest = jnp.full((1,), NGROUPS - 3 * SMALL, dtype=jnp.int32)
    return jnp.concatenate([before, largest, after]).astype(jnp.int32)


def block_levels(rng, extent, split, least, top_value):
    def one(position, blocks):
        draws = jax.random.uniform(jax.random.fold_in(jax.random.fold_in(rng, 6), position), (blocks,), jnp.float32, least / len(split), top_value / len(split))
        return jnp.repeat(jnp.exp(draws), extent[position] // blocks).reshape((-1,) + (1,) * (len(extent) - position - 1))

    level = one(*split[0])
    for cut in split[1:]:
        level = level * one(*cut)
    return level


def scatter_about(own_key, shape, width, limit, pieces=(), held_as=jnp.bfloat16):
    entries = jax.random.normal(own_key, shape, jnp.float32) * width
    if len(pieces) > 0:
        entries = block_levels(own_key, shape, pieces, -0.22, 0.18) * entries
    return jnp.clip(entries, min=-limit, max=limit).astype(held_as)


def setup_inputs(seed: int = 0) -> dict:
    seeds = jax.random.split(jax.random.key(seed), 15)
    tokens = scatter_about(seeds[0], (TOKENS, D), 1.0, 6.0, ((0, 8),))
    latents = scatter_about(seeds[1], (NLAT, D), 1.0, 6.0, ((0, 8),))
    image_groups = draw_image_groups(jax.random.fold_in(seeds[14], 71), 0)
    read_query = scatter_about(seeds[3], (D, D), (D // 4) ** -0.5, 0.4375, ((1, 4),))
    read_key = scatter_about(seeds[4], (D, D), D ** -0.5, 0.21875, ((1, 4),))
    read_value = scatter_about(seeds[5], (D, D), D ** -0.5, 0.21875, ((1, 4),))
    read_out = scatter_about(seeds[6], (D, D), (D // 32) ** -0.5, 1.25, ((0, 4),))
    write_query = scatter_about(seeds[7], (D, D), (D // 4) ** -0.5, 0.4375, ((1, 4),))
    write_key = scatter_about(seeds[8], (D, D), D ** -0.5, 0.21875, ((1, 4),))
    write_value = scatter_about(seeds[9], (D, D), D ** -0.5, 0.21875, ((1, 4),))
    write_out = scatter_about(seeds[10], (D, D), (D // 32) ** -0.5, 1.25, ((0, 4),))
    mlp_in = scatter_about(seeds[11], (D, FF), D ** -0.5, 0.21875, ((1, 4),))
    mlp_out = scatter_about(seeds[12], (FF, D), FF ** -0.5, 0.109375, ((0, 4),))
    cotangent = scatter_about(seeds[13], (TOKENS, D), 1.0, 6.0, ((0, 8),))
    return {"tokens": tokens, "latents": latents, "image_groups": image_groups, "read_query": read_query, "read_key": read_key, "read_value": read_value, "read_out": read_out, "write_query": write_query, "write_key": write_key, "write_value": write_value, "write_out": write_out, "mlp_in": mlp_in, "mlp_out": mlp_out, "cotangent": cotangent}


epsilon = 1e-05
highest = lax.Precision.HIGHEST

@jax.custom_vjp
def low(v):
    return lax.optimization_barrier(v.astype(jnp.bfloat16)).astype(jnp.float32)

@jax.custom_vjp
def low_back(v):
    return v

def low_keep(v):
    return (low(v), None)

def low_pass(kept, grad):
    return (grad,)

def back_keep(v):
    return (v, None)

def back_low(kept, grad):
    return (low(grad),)
low.defvjp(low_keep, low_pass)
low_back.defvjp(back_keep, back_low)

def norm_rows(values):
    center = values - lax.optimization_barrier(jnp.mean(values, axis=-1, keepdims=True))
    return center * lax.rsqrt(lax.optimization_barrier(jnp.mean(center * center, axis=-1, keepdims=True)) + epsilon)

def project(inputs, weight):
    return low(low_back(jnp.dot(inputs, weight, precision=highest)))

def split_heads(values):
    return values.reshape(values.shape[0], HEADS, HD).transpose(1, 0, 2)

def attend(queries, keys, values, query_image, key_image, round_weights):
    count = queries.shape[0]
    mask = query_image[:, None] == key_image[None, :]

    def one_head(operands):
        query_head, key_head, value_head = operands
        scores = low_back(jnp.dot(query_head, key_head.T, precision=highest) * 0.125)
        weights = jnp.where(mask, jnp.exp(scores), 0.0)
        weights = weights / lax.optimization_barrier(jnp.sum(weights, axis=-1, keepdims=True))
        if round_weights:
            weights = low(weights)
        return jnp.dot(weights, value_head, precision=highest)
    heads_out = lax.map(jax.checkpoint(one_head), (split_heads(queries), split_heads(keys), split_heads(values)))
    return heads_out.transpose(1, 0, 2).reshape(count, D)

def layer(tokens, latents, read_query, read_key, read_value, read_out, write_query, write_key, write_value, write_out, mlp_in, mlp_out, token_image, latent_image):
    normed_x = low(norm_rows(tokens))
    normed_lat = low(norm_rows(latents))
    query_read = project(normed_lat, read_query)
    keys_read = jnp.concatenate([project(normed_x, read_key), project(normed_lat, read_key)], axis=0)
    values_read = jnp.concatenate([project(normed_x, read_value), project(normed_lat, read_value)], axis=0)
    key_image = jnp.concatenate([token_image, latent_image], axis=0)
    read_mixed = low(low_back(attend(query_read, keys_read, values_read, latent_image, key_image, False)))
    latents_one = latents + low_back(jnp.dot(read_mixed, read_out, precision=highest))
    normed_one = low(norm_rows(latents_one))
    keys_write = project(normed_one, write_key)
    values_write = project(normed_one, write_value)
    query_write = project(normed_x, write_query)
    write_mixed = low(low_back(attend(query_write, keys_write, values_write, token_image, latent_image, True)))
    tokens_one = tokens + low_back(jnp.dot(write_mixed, write_out, precision=highest))
    normed_two = low(norm_rows(tokens_one))
    inner = low_back(jnp.dot(normed_two, mlp_in, precision=highest))
    activated = low(jax.nn.gelu(inner))
    return tokens_one + low_back(jnp.dot(activated, mlp_out, precision=highest))

def reference(tokens, latents, image_groups, read_query, read_key, read_value, read_out, write_query, write_key, write_value, write_out, mlp_in, mlp_out, cotangent):
    bounds = jnp.cumsum(image_groups)
    group_ids = jnp.arange(NGROUPS, dtype=jnp.int32)
    group_image = lax.optimization_barrier(jnp.sum((bounds[None, :] <= group_ids[:, None]).astype(jnp.int32), axis=1))
    token_image = jnp.repeat(group_image, GROUP, total_repeat_length=TOKENS)
    latent_image = jnp.repeat(group_image, LPG, total_repeat_length=NLAT)
    forward = partial(layer, token_image=token_image, latent_image=latent_image)
    result, pullback = jax.vjp(forward, tokens.astype(jnp.float32), latents.astype(jnp.float32), read_query.astype(jnp.float32), read_key.astype(jnp.float32), read_value.astype(jnp.float32), read_out.astype(jnp.float32), write_query.astype(jnp.float32), write_key.astype(jnp.float32), write_value.astype(jnp.float32), write_out.astype(jnp.float32), mlp_in.astype(jnp.float32), mlp_out.astype(jnp.float32))
    grads = pullback(cotangent.astype(jnp.float32))
    return (result.astype(jnp.bfloat16), grads[0], grads[1], grads[2], grads[3], grads[4], grads[5], grads[6], grads[7], grads[8], grads[9], grads[10], grads[11])
```

```python
from functools import partial

import jax
import jax.numpy as jnp
from jax import lax
from jax.experimental import pallas as pl
from jax.experimental.pallas import tpu as pltpu
from jax.sharding import PartitionSpec as P

MESH = pl.DeviceIdType.MESH

HD = 64
GROUP = 256
LPG = 8


epsilon = 1e-05
triple = lax.Precision.HIGH


def norm_rows(values):
    center = values - jnp.mean(values, axis=-1, keepdims=True)
    return center * lax.rsqrt(jnp.mean(center * center, axis=-1, keepdims=True) + epsilon)


def matmul(left, right):
    return jnp.dot(left, right, preferred_element_type=jnp.float32)


def left_trans(left, right):
    return lax.dot_general(
        left, right, (((0,), (0,)), ((), ())), preferred_element_type=jnp.float32
    )


def right_trans(left, right):
    return lax.dot_general(
        left, right, (((1,), (1,)), ((), ())), preferred_element_type=jnp.float32
    )


def grad_kernel(outer, parts_ref, out_ref, got_one, sums, got_two, send_one, recv_one, send_two, recv_two):
    tok = lax.axis_index("tok")
    head = lax.axis_index("head")
    mine = tok // 2
    side = lax.rem(tok, 2)
    partner = mine * 2 + (1 - side)
    barrier = pltpu.get_barrier_semaphore()
    pl.semaphore_signal(barrier, inc=1, device_id=(partner, head), device_id_type=MESH)

    def greet(step, carry):
        peer = lax.rem(mine + step, outer) * 2 + side
        pl.semaphore_signal(barrier, inc=1, device_id=(peer, head), device_id_type=MESH)
        return carry

    lax.fori_loop(1, outer, greet, 0)
    pl.semaphore_wait(barrier, outer)

    def first(block):
        return pltpu.make_async_remote_copy(
            src_ref=parts_ref.at[block, 1 - side],
            dst_ref=got_one.at[block],
            send_sem=send_one.at[block],
            recv_sem=recv_one.at[block],
            device_id=(partner, head),
            device_id_type=MESH,
        )

    def second(block, source):
        return pltpu.make_async_remote_copy(
            src_ref=sums.at[block],
            dst_ref=got_two.at[source],
            send_sem=send_two.at[block],
            recv_sem=recv_two.at[source],
            device_id=(block * 2 + side, head),
            device_id_type=MESH,
        )

    def start_first(step, carry):
        first(lax.rem(mine + step, outer)).start()
        return carry

    lax.fori_loop(1, outer + 1, start_first, 0)

    def start_second(step, carry):
        block = lax.rem(mine + step, outer)
        first(block).wait()
        total = parts_ref[block, side].astype(jnp.float32) + got_one[block].astype(jnp.float32)
        sums[block] = total.astype(jnp.bfloat16)
        second(block, mine).start()
        return carry

    lax.fori_loop(1, outer, start_second, 0)
    first(mine).wait()
    out_ref[...] = parts_ref[mine, side].astype(jnp.float32) + got_one[mine].astype(jnp.float32)

    def finish(step, carry):
        source = lax.rem(mine + step, outer)
        second(lax.rem(mine + outer - step, outer), source).wait_recv()
        out_ref[...] += got_two[source].astype(jnp.float32)
        return carry

    lax.fori_loop(1, outer, finish, 0)

    def drain(step, carry):
        second(lax.rem(mine + step, outer), mine).wait_send()
        return carry

    lax.fori_loop(1, outer, drain, 0)


def scatter_grads(parts, tok_count):
    outer = tok_count // 2
    rows, width = parts.shape[0] // tok_count, parts.shape[1]
    slots = pltpu.VMEM((outer, rows, width), jnp.bfloat16)
    sems = pltpu.SemaphoreType.DMA((outer,))
    return pl.pallas_call(
        partial(grad_kernel, outer),
        out_shape=jax.ShapeDtypeStruct((rows, width), jnp.float32),
        in_specs=[pl.BlockSpec(memory_space=pltpu.VMEM)],
        out_specs=pl.BlockSpec(memory_space=pltpu.VMEM),
        scratch_shapes=[slots, slots, slots, sems, sems, sems, sems],
        compiler_params=pltpu.CompilerParams(
            collective_id=0, has_side_effects=True, vmem_limit_bytes=56 << 20
        ),
        name="grad_scatter",
    )(parts.reshape(outer, 2, rows, width))


def heads_view(values):
    return values.reshape(values.shape[0], values.shape[1] // HD, HD)


def shards(
    tokens,
    latents,
    image_groups,
    read_query,
    read_key,
    read_value,
    read_out,
    write_query,
    write_key,
    write_value,
    write_out,
    mlp_in,
    mlp_out,
    cotangent,
):
    rows = tokens.shape[0]
    owned = latents.shape[0]
    column = read_query.shape[1]
    heads_here = column // HD
    tok_count = lax.axis_size("tok")
    head_count = lax.axis_size("head")
    tok_index = lax.axis_index("tok")
    head_index = lax.axis_index("head")
    groups_here = rows // GROUP
    total_groups = groups_here * tok_count
    all_latents = total_groups * LPG
    bounds = jnp.cumsum(image_groups)
    group_ids = jnp.arange(total_groups, dtype=jnp.int32)
    group_image = jnp.sum((bounds[None, :] <= group_ids[:, None]).astype(jnp.int32), axis=1)
    latent_image = jnp.repeat(group_image, LPG, total_repeat_length=all_latents)
    local_groups = lax.dynamic_slice_in_dim(group_image, tok_index * groups_here, groups_here)
    token_image = jnp.repeat(local_groups, GROUP, total_repeat_length=rows)
    own_image = lax.dynamic_slice_in_dim(latent_image, tok_index * owned, owned)
    key_image = jnp.concatenate([token_image, own_image], axis=0)
    key_count = rows + owned
    tokens_full = tokens.astype(jnp.float32)
    latents_full = latents.astype(jnp.float32)
    normed_x = norm_rows(tokens_full).astype(jnp.bfloat16)
    normed_lat = norm_rows(latents_full).astype(jnp.bfloat16)
    query_own = matmul(normed_lat, read_query).astype(jnp.bfloat16)
    query_all = lax.all_gather(query_own, "tok", axis=0, tiled=True)
    keys_here = jnp.concatenate(
        [matmul(normed_x, read_key), matmul(normed_lat, read_key)], axis=0
    ).astype(jnp.bfloat16)
    values_here = jnp.concatenate(
        [matmul(normed_x, read_value), matmul(normed_lat, read_value)], axis=0
    ).astype(jnp.bfloat16)
    keys_split = heads_view(keys_here)
    values_split = heads_view(values_here)
    latent_block = min(512, all_latents)
    latent_blocks = all_latents // latent_block

    def read_scores(query_block, image_block):
        scores = (
            jnp.einsum(
                "qhd,khd->qhk",
                heads_view(query_block),
                keys_split,
                preferred_element_type=jnp.float32,
            )
            * 0.125
        )
        mask = (image_block[:, None] == key_image[None, :])[:, None, :]
        return (scores, mask)

    def read_block(operands):
        query_block, image_block = operands
        scores, mask = read_scores(query_block, image_block)
        weights = jnp.where(mask, jnp.exp(scores), 0.0)
        totals = jnp.sum(weights, axis=-1)
        summed = jnp.einsum(
            "qhk,khd->qhd",
            weights,
            values_split,
            precision=triple,
            preferred_element_type=jnp.float32,
        )
        return (totals, summed.reshape(query_block.shape[0], column))

    query_blocks = query_all.reshape(latent_blocks, latent_block, column)
    image_blocks = latent_image.reshape(latent_blocks, latent_block)
    totals, sums = lax.map(read_block, (query_blocks, image_blocks))
    totals = totals.reshape(all_latents, heads_here)
    sums = sums.reshape(all_latents, column)
    totals_all, sums_all = lax.psum((totals, sums), "tok")
    total_own = lax.dynamic_slice_in_dim(totals_all, tok_index * owned, owned)
    sum_own = lax.dynamic_slice_in_dim(sums_all, tok_index * owned, owned)
    mixed_wide = (heads_view(sum_own) / total_own[:, :, None]).reshape(owned, column)
    read_mixed = mixed_wide.astype(jnp.bfloat16)
    latents_one = latents_full + lax.psum(matmul(read_mixed, read_out), "head")
    normed_one, norm_one_back = jax.vjp(norm_rows, latents_one)
    normed_one = normed_one.astype(jnp.bfloat16)
    wkey_own = matmul(normed_one, write_key).astype(jnp.bfloat16)
    wvalue_own = matmul(normed_one, write_value).astype(jnp.bfloat16)
    wkey_all, wvalue_all = (
        lax.all_gather(wkey_own, "tok", axis=0, tiled=True),
        lax.all_gather(wvalue_own, "tok", axis=0, tiled=True),
    )
    wkey_split = heads_view(wkey_all)
    wvalue_split = heads_view(wvalue_all)
    query_write = matmul(normed_x, write_query).astype(jnp.bfloat16)
    row_block = min(512, rows)
    row_blocks = rows // row_block

    def write_scores(query_block, image_block):
        scores = (
            jnp.einsum(
                "qhd,khd->qhk",
                heads_view(query_block),
                wkey_split,
                preferred_element_type=jnp.float32,
            )
            * 0.125
        )
        mask = (image_block[:, None] == latent_image[None, :])[:, None, :]
        return (scores, mask)

    def write_block(operands):
        query_block, image_block = operands
        scores, mask = write_scores(query_block, image_block)
        weights = jnp.where(mask, jnp.exp(scores), 0.0)
        totals_block = jnp.sum(weights, axis=-1, keepdims=True)
        probs = (weights / totals_block).astype(jnp.bfloat16)
        mixed = jnp.einsum("qhk,khd->qhd", probs, wvalue_split, preferred_element_type=jnp.float32)
        return (
            mixed.reshape(query_block.shape[0], column).astype(jnp.bfloat16),
            jnp.log(totals_block[:, :, 0]),
        )

    wquery_blocks = query_write.reshape(row_blocks, row_block, column)
    token_blocks = token_image.reshape(row_blocks, row_block)
    write_mixed, write_logs = lax.map(write_block, (wquery_blocks, token_blocks))
    write_mixed = write_mixed.reshape(rows, column)
    tokens_one = tokens_full + lax.psum(matmul(write_mixed, write_out), "head")
    normed_two, norm_two_back = jax.vjp(norm_rows, tokens_one)
    normed_two = normed_two.astype(jnp.bfloat16)
    inner = matmul(normed_two, mlp_in)
    activated, gelu_back = jax.vjp(jax.nn.gelu, inner)
    activated = activated.astype(jnp.bfloat16)
    quarter = rows // head_count
    row_start = head_index * quarter
    branch = lax.psum_scatter(matmul(activated, mlp_out), "head", scatter_dimension=0, tiled=True)
    layer_out = (lax.dynamic_slice_in_dim(tokens_one, row_start, quarter) + branch).astype(
        jnp.bfloat16
    )
    grad_mlp_out = left_trans(cotangent, activated)
    grad_act = right_trans(cotangent, mlp_out)
    grad_inner = gelu_back(grad_act)[0].astype(jnp.bfloat16)
    grad_mlp_in = left_trans(normed_two, grad_inner)
    grad_normed_two = lax.psum(right_trans(grad_inner, mlp_in), "head")
    grad_tokens_one = cotangent.astype(jnp.float32) + norm_two_back(grad_normed_two)[0]
    grad_branch = grad_tokens_one.astype(jnp.bfloat16)
    grad_write_out = left_trans(grad_branch, write_mixed)
    grad_wmixed = right_trans(grad_branch, write_out).astype(jnp.bfloat16)

    def write_back(carry, operands):
        key_total, value_total = carry
        query_block, image_block, grad_block, log_block = operands
        scores, mask = write_scores(query_block, image_block)
        probs = jnp.where(mask, jnp.exp(scores - log_block[:, :, None]), 0.0)
        grad_probs = jnp.einsum(
            "qhd,khd->qhk", heads_view(grad_block), wvalue_split, preferred_element_type=jnp.float32
        )
        delta = jnp.sum(probs * grad_probs, axis=-1, keepdims=True)
        grad_scores = (probs * (grad_probs - delta)).astype(jnp.bfloat16)
        grad_query = (
            jnp.einsum("qhk,khd->qhd", grad_scores, wkey_split, preferred_element_type=jnp.float32)
            * 0.125
        )
        key_total = (
            key_total
            + jnp.einsum(
                "qhk,qhd->khd",
                grad_scores,
                heads_view(query_block),
                preferred_element_type=jnp.float32,
            ).reshape(all_latents, column)
            * 0.125
        )
        value_total = value_total + jnp.einsum(
            "qhk,qhd->khd",
            probs.astype(jnp.bfloat16),
            heads_view(grad_block),
            preferred_element_type=jnp.float32,
        ).reshape(all_latents, column)
        return (
            (key_total, value_total),
            grad_query.reshape(query_block.shape[0], column).astype(jnp.bfloat16),
        )

    latent_zeros = jnp.zeros((all_latents, column), jnp.float32)
    (grad_wkey_all, grad_wvalue_all), grad_wquery = lax.scan(
        write_back,
        (latent_zeros, latent_zeros),
        (
            wquery_blocks,
            token_blocks,
            grad_wmixed.reshape(row_blocks, row_block, column),
            write_logs,
        ),
    )
    grad_wquery = grad_wquery.reshape(rows, column)
    grad_wkey, grad_wvalue = (
        lax.psum_scatter(grad_wkey_all, "tok", scatter_dimension=0, tiled=True),
        lax.psum_scatter(grad_wvalue_all, "tok", scatter_dimension=0, tiled=True),
    )
    grad_wkey = grad_wkey.astype(jnp.bfloat16)
    grad_wvalue = grad_wvalue.astype(jnp.bfloat16)
    grad_write_key = left_trans(normed_one, grad_wkey)
    grad_write_value = left_trans(normed_one, grad_wvalue)
    grad_write_query = left_trans(normed_x, grad_wquery)
    grad_normed_one = lax.psum(
        right_trans(grad_wkey, write_key) + right_trans(grad_wvalue, write_value), "head"
    )
    grad_latents_one = norm_one_back(grad_normed_one)[0]
    grad_latent_branch = grad_latents_one.astype(jnp.bfloat16)
    grad_read_out = left_trans(grad_latent_branch, read_mixed)
    grad_rmixed = right_trans(grad_latent_branch, read_out).astype(jnp.bfloat16)
    grad_rmixed_wide = grad_rmixed.astype(jnp.float32)
    delta_own = jnp.sum(heads_view(grad_rmixed_wide * mixed_wide), axis=-1)
    log_own = jnp.log(total_own)
    grad_mixed_all, delta_all, log_all = (
        lax.all_gather(grad_rmixed_wide, "tok", axis=0, tiled=True),
        lax.all_gather(delta_own, "tok", axis=0, tiled=True),
        lax.all_gather(log_own, "tok", axis=0, tiled=True),
    )
    grad_mixed_all = grad_mixed_all.astype(jnp.bfloat16)

    def read_back(carry, operands):
        key_total, value_total = carry
        query_block, image_block, grad_block, delta_block, log_block = operands
        scores, mask = read_scores(query_block, image_block)
        probs = jnp.where(mask, jnp.exp(scores - log_block[:, :, None]), 0.0)
        grad_probs = jnp.einsum(
            "qhd,khd->qhk", heads_view(grad_block), values_split, preferred_element_type=jnp.float32
        )
        grad_scores = (probs * (grad_probs - delta_block[:, :, None])).astype(jnp.bfloat16)
        grad_query = (
            jnp.einsum("qhk,khd->qhd", grad_scores, keys_split, preferred_element_type=jnp.float32)
            * 0.125
        )
        key_total = (
            key_total
            + jnp.einsum(
                "qhk,qhd->khd",
                grad_scores,
                heads_view(query_block),
                preferred_element_type=jnp.float32,
            ).reshape(key_count, column)
            * 0.125
        )
        value_total = value_total + jnp.einsum(
            "qhk,qhd->khd",
            probs,
            heads_view(grad_block),
            precision=triple,
            preferred_element_type=jnp.float32,
        ).reshape(key_count, column)
        return ((key_total, value_total), grad_query.reshape(query_block.shape[0], column))

    key_zeros = jnp.zeros((key_count, column), jnp.float32)
    (grad_keys, grad_values), grad_query_all = lax.scan(
        read_back,
        (key_zeros, key_zeros),
        (
            query_blocks,
            image_blocks,
            grad_mixed_all.reshape(latent_blocks, latent_block, column),
            delta_all.reshape(latent_blocks, latent_block, heads_here),
            log_all.reshape(latent_blocks, latent_block, heads_here),
        ),
    )
    grad_query_all = grad_query_all.reshape(all_latents, column)
    grad_query_own = lax.psum_scatter(
        grad_query_all, "tok", scatter_dimension=0, tiled=True
    ).astype(jnp.bfloat16)
    grad_keys = grad_keys.astype(jnp.bfloat16)
    grad_values = grad_values.astype(jnp.bfloat16)
    grad_key_tok = grad_keys[:rows]
    grad_key_lat = grad_keys[rows:]
    grad_value_tok = grad_values[:rows]
    grad_value_lat = grad_values[rows:]
    grad_read_query = left_trans(normed_lat, grad_query_own)
    grad_read_key = left_trans(normed_x, grad_key_tok) + left_trans(normed_lat, grad_key_lat)
    grad_read_value = left_trans(normed_x, grad_value_tok) + left_trans(normed_lat, grad_value_lat)
    grad_normed_x = (
        right_trans(grad_key_tok, read_key)
        + right_trans(grad_value_tok, read_value)
        + right_trans(grad_wquery, write_query)
    )
    grad_normed_lat = (
        right_trans(grad_query_own, read_query)
        + right_trans(grad_key_lat, read_key)
        + right_trans(grad_value_lat, read_value)
    )
    grad_x_rows, grad_lat_rows = (
        lax.psum_scatter(grad_normed_x, "head", scatter_dimension=0, tiled=True),
        lax.psum_scatter(grad_normed_lat, "head", scatter_dimension=0, tiled=True),
    )
    latent_quarter = owned // head_count
    latent_start = head_index * latent_quarter
    token_rows = lax.dynamic_slice_in_dim(tokens_full, row_start, quarter)
    unused_x, norm_x_back = jax.vjp(norm_rows, token_rows)
    input_grad = (
        lax.dynamic_slice_in_dim(grad_tokens_one, row_start, quarter) + norm_x_back(grad_x_rows)[0]
    )
    latent_rows = lax.dynamic_slice_in_dim(latents_full, latent_start, latent_quarter)
    unused_lat, norm_lat_back = jax.vjp(norm_rows, latent_rows)
    latent_grad = (
        lax.dynamic_slice_in_dim(grad_latents_one, latent_start, latent_quarter)
        + norm_lat_back(grad_lat_rows)[0]
    )
    partials = jnp.concatenate(
        [
            grad_read_query,
            grad_read_key,
            grad_read_value,
            grad_read_out,
            grad_write_query,
            grad_write_key,
            grad_write_value,
            grad_write_out,
            grad_mlp_in,
            grad_mlp_out,
        ],
        axis=1,
    ).astype(jnp.bfloat16)
    grads = scatter_grads(partials, tok_count)
    summed = [grads[:, k * column : (k + 1) * column] for k in range(8)]
    hidden = mlp_in.shape[1]
    summed.append(grads[:, 8 * column : 8 * column + hidden])
    summed.append(grads[:, 8 * column + hidden :].T)
    summed[3] = summed[3].T
    summed[7] = summed[7].T
    return (
        layer_out,
        input_grad,
        latent_grad,
        summed[0],
        summed[1],
        summed[2],
        summed[3],
        summed[4],
        summed[5],
        summed[6],
        summed[7],
        summed[8],
        summed[9],
    )


def solution(mesh):
    return jax.shard_map(
        shards,
        mesh=mesh,
        in_specs=(
            P("tok", None),
            P("tok", None),
            P(),
            P(None, "head"),
            P(None, "head"),
            P(None, "head"),
            P("head", None),
            P(None, "head"),
            P(None, "head"),
            P(None, "head"),
            P("head", None),
            P(None, "head"),
            P("head", None),
            P("tok", None),
        ),
        out_specs=(
            P(("tok", "head"), None),
            P(("tok", "head"), None),
            P(("tok", "head"), None),
            P("tok", "head"),
            P("tok", "head"),
            P("tok", "head"),
            P("head", "tok"),
            P("tok", "head"),
            P("tok", "head"),
            P("tok", "head"),
            P("head", "tok"),
            P("tok", "head"),
            P("head", "tok"),
        ),
        check_vma=False,
    )
```

```python
from functools import partial

import jax
import jax.numpy as jnp
from jax import lax
from jax.experimental import pallas as pl
from jax.experimental.pallas import tpu as pltpu
from jax.sharding import PartitionSpec as P

MESH = pl.DeviceIdType.MESH

HD = 64
GROUP = 256
LPG = 8


epsilon = 1e-05
triple = lax.Precision.HIGH


def norm_rows(values):
    center = values - jnp.mean(values, axis=-1, keepdims=True)
    return center * lax.rsqrt(jnp.mean(center * center, axis=-1, keepdims=True) + epsilon)


def matmul(left, right):
    return jnp.dot(left, right, preferred_element_type=jnp.float32)


def left_trans(left, right):
    return lax.dot_general(
        left, right, (((0,), (0,)), ((), ())), preferred_element_type=jnp.float32
    )


def right_trans(left, right):
    return lax.dot_general(
        left, right, (((1,), (1,)), ((), ())), preferred_element_type=jnp.float32
    )


def grad_kernel(outer, parts_ref, out_ref, got_one, sums, got_two, send_one, recv_one, send_two, recv_two):
    tok = lax.axis_index("tok")
    head = lax.axis_index("head")
    mine = tok // 2
    side = lax.rem(tok, 2)
    partner = mine * 2 + (1 - side)
    barrier = pltpu.get_barrier_semaphore()
    pl.semaphore_signal(barrier, inc=1, device_id=(partner, head), device_id_type=MESH)

    def greet(step, carry):
        peer = lax.rem(mine + step, outer) * 2 + side
        pl.semaphore_signal(barrier, inc=1, device_id=(peer, head), device_id_type=MESH)
        return carry

    lax.fori_loop(1, outer, greet, 0)
    pl.semaphore_wait(barrier, outer)

    def first(block):
        return pltpu.make_async_remote_copy(
            src_ref=parts_ref.at[block, 1 - side],
            dst_ref=got_one.at[block],
            send_sem=send_one.at[block],
            recv_sem=recv_one.at[block],
            device_id=(partner, head),
            device_id_type=MESH,
        )

    def second(block, source):
        return pltpu.make_async_remote_copy(
            src_ref=sums.at[block],
            dst_ref=got_two.at[source],
            send_sem=send_two.at[block],
            recv_sem=recv_two.at[source],
            device_id=(block * 2 + side, head),
            device_id_type=MESH,
        )

    def start_first(step, carry):
        first(lax.rem(mine + step, outer)).start()
        return carry

    lax.fori_loop(1, outer + 1, start_first, 0)

    def start_second(step, carry):
        block = lax.rem(mine + step, outer)
        first(block).wait()
        total = parts_ref[block, side].astype(jnp.float32) + got_one[block].astype(jnp.float32)
        sums[block] = total.astype(jnp.bfloat16)
        second(block, mine).start()
        return carry

    lax.fori_loop(1, outer, start_second, 0)
    first(mine).wait()
    out_ref[...] = parts_ref[mine, side].astype(jnp.float32) + got_one[mine].astype(jnp.float32)

    def finish(step, carry):
        source = lax.rem(mine + step, outer)
        second(lax.rem(mine + outer - step, outer), source).wait_recv()
        out_ref[...] += got_two[source].astype(jnp.float32)
        return carry

    lax.fori_loop(1, outer, finish, 0)

    def drain(step, carry):
        second(lax.rem(mine + step, outer), mine).wait_send()
        return carry

    lax.fori_loop(1, outer, drain, 0)


def scatter_grads(parts, tok_count):
    outer = tok_count // 2
    rows, width = parts.shape[0] // tok_count, parts.shape[1]
    slots = pltpu.VMEM((outer, rows, width), jnp.bfloat16)
    sems = pltpu.SemaphoreType.DMA((outer,))
    return pl.pallas_call(
        partial(grad_kernel, outer),
        out_shape=jax.ShapeDtypeStruct((rows, width), jnp.float32),
        in_specs=[pl.BlockSpec(memory_space=pltpu.VMEM)],
        out_specs=pl.BlockSpec(memory_space=pltpu.VMEM),
        scratch_shapes=[slots, slots, slots, sems, sems, sems, sems],
        compiler_params=pltpu.CompilerParams(
            collective_id=0, has_side_effects=True, vmem_limit_bytes=56 << 20
        ),
        name="grad_scatter",
    )(parts.reshape(outer, 2, rows, width))


SUB = 64
SCALE = 0.125
LOG2E = 1.4426950408889634
MASKED = -1e30
GELU_A = 0.7978845608028654
GELU_B = 0.044715


def nn(left, right):
    return lax.dot_general(left, right, (((1,), (0,)), ((), ())), preferred_element_type=jnp.float32)


def nt(left, right):
    return lax.dot_general(left, right, (((1,), (1,)), ((), ())), preferred_element_type=jnp.float32)


def tn(left, right):
    return lax.dot_general(left, right, (((0,), (0,)), ((), ())), preferred_element_type=jnp.float32)


def norm_parts(values):
    center = values - jnp.mean(values, axis=-1, keepdims=True)
    scale = lax.rsqrt(jnp.mean(center * center, axis=-1, keepdims=True) + epsilon)
    return center * scale, scale


def norm_vjp(normed, scale, grad):
    return scale * (
        grad
        - jnp.mean(grad, axis=-1, keepdims=True)
        - normed * jnp.mean(grad * normed, axis=-1, keepdims=True)
    )


def middle_kernel(
    tokens,
    cotangent,
    query_t,
    key,
    value,
    key_t,
    value_t,
    latent_image,
    token_image,
    write_out,
    mlp_in,
    mlp_out,
    layer_out,
    grad_one,
    grad_query_t,
    grad_key,
    grad_value,
    grad_mlp_in,
    grad_mlp_out,
    grad_write_out,
    update,
    mixed_t,
    log_total,
    own_a,
    send_a,
    got_a,
    half_a,
    cross_a,
    own_d,
    send_d,
    got_d,
    half_d,
    cross_d,
    summed_d,
    own_f,
    send_f,
    got_f,
    half_f,
    cross_f,
    acc_in,
    acc_out,
    acc_write,
    normed_s,
    act_s,
    inner_s,
    wide_s,
    send_sems,
    recv_sems,
):
    chunks = query_t.shape[0]
    heads = key.shape[0]
    latents = key.shape[1]
    width = tokens.shape[2]
    block = min(512, latents)
    blocks = latents // block
    tok = lax.axis_index("tok")
    head = lax.axis_index("head")
    core = lax.rem(head, 2)
    side = head // 2
    other = 1 - core
    core_peer = (tok, side * 2 + other)
    side_peer = (tok, (1 - side) * 2 + core)
    barrier = pltpu.get_barrier_semaphore()
    for peer in (core_peer, side_peer):
        pl.semaphore_signal(barrier, inc=1, device_id=peer, device_id_type=MESH)
    pl.semaphore_wait(barrier, 2)

    def copy(kind, chunk, source, target, peer):
        slot = lax.rem(chunk, 2)
        return pltpu.make_async_remote_copy(
            src_ref=source,
            dst_ref=target,
            send_sem=send_sems.at[kind, slot],
            recv_sem=recv_sems.at[kind, slot],
            device_id=peer,
            device_id_type=MESH,
        )

    def core_a(c):
        return copy(0, c, send_a, got_a.at[lax.rem(c, 2)], core_peer)

    def cross_copy_a(c):
        return copy(1, c, half_a, cross_a.at[lax.rem(c, 2)], side_peer)

    def core_u(c):
        return copy(2, c, update.at[c, core], update.at[c, core], core_peer)

    def core_d(c):
        return copy(3, c, send_d, got_d.at[lax.rem(c, 2)], core_peer)

    def cross_copy_d(c):
        return copy(4, c, half_d, cross_d.at[lax.rem(c, 2)], side_peer)

    def core_s(c):
        half = summed_d.at[lax.rem(c, 2), core]
        return copy(5, c, half, half, core_peer)

    def core_f(c):
        return copy(6, c, send_f, got_f.at[lax.rem(c, 2)], core_peer)

    def cross_copy_f(c):
        return copy(7, c, half_f.at[1 - side], cross_f.at[lax.rem(c, 2)], side_peer)

    def rows_of(ref, c):
        part = pl.ds(pl.multiple_of(c * SUB, SUB), SUB)
        return jnp.concatenate([ref[q, part, :] for q in (0, 2, 1, 3)], axis=0)

    def mask_of(c, start):
        image = latent_image[pl.ds(start, block), :]
        image = jnp.concatenate([image, image], axis=1)
        return jnp.where(image == token_image[c], 0.0, MASKED)

    def each_block(body, carry):
        if blocks == 1:
            return body(0, carry)
        return lax.fori_loop(0, blocks, lambda b, kept: body(b * block, kept), carry)

    def halve(wide, own, send):
        wide_s[...] = wide.reshape(wide_s.shape)
        own[...] = wide_s[core]
        send[...] = wide_s[other].astype(jnp.bfloat16)

    acc_in[...] = jnp.zeros_like(acc_in)
    acc_out[...] = jnp.zeros_like(acc_out)
    acc_write[...] = jnp.zeros_like(acc_write)
    grad_key[...] = jnp.zeros_like(grad_key)
    grad_value[...] = jnp.zeros_like(grad_value)

    def head_rows(h):
        return slice(h * HD, (h + 1) * HD)

    def write_forward(c):
        query = query_t[c]

        def body(start, carry):
            here = pl.ds(start, block)
            bias = mask_of(c, start)
            kept = []
            for h in range(heads):
                scores = nn(key[h, here, :], query[head_rows(h)])
                weights = jnp.exp2(scores * (SCALE * LOG2E) + bias)
                total = jnp.sum(weights, axis=0, keepdims=True)
                mixed = nn(value_t[head_rows(h), here], weights.astype(jnp.bfloat16))
                kept.append((carry[h][0] + total, carry[h][1] + mixed))
            return tuple(kept)

        zero = (jnp.zeros((1, query.shape[1]), jnp.float32), jnp.zeros((HD, query.shape[1]), jnp.float32))
        totals = each_block(body, (zero,) * heads)
        mixed = jnp.concatenate([part / total for total, part in totals], axis=0)
        mixed = mixed.astype(jnp.bfloat16)
        mixed_t[c] = mixed
        for h in range(heads):
            log_total[c, h : h + 1] = -jnp.log2(totals[h][0])
        halve(tn(mixed, write_out[...]), own_a, send_a)
        core_a(c).start()

    def finish_update(c):
        cross_copy_a(c).wait()
        mine = half_a[...].astype(jnp.float32) + cross_a[lax.rem(c, 2)].astype(jnp.float32)
        update[c, core] = mine.astype(jnp.bfloat16)
        core_u(c).start()

    def cross_update(c):
        core_a(c).wait()
        half_a[...] = (own_a[...] + got_a[lax.rem(c, 2)].astype(jnp.float32)).astype(jnp.bfloat16)
        cross_copy_a(c).start()

    def one_rows(c):
        moved = update[c].reshape(4 * SUB, width).astype(jnp.float32)
        return rows_of(tokens, c).astype(jnp.float32) + moved

    def feed_forward(c):
        core_u(c).wait()
        normed, unused = norm_parts(one_rows(c))
        normed = normed.astype(jnp.bfloat16)
        normed_s[...] = normed
        inner = nn(normed, mlp_in[...])
        square = inner * inner
        tanh = jnp.tanh(GELU_A * inner * (1.0 + GELU_B * square))
        half = 0.5 + 0.5 * tanh
        active = (inner * half).astype(jnp.bfloat16)
        act_s[...] = active
        slope = half + 0.5 * GELU_A * inner * (1.0 - tanh * tanh) * (1.0 + 3.0 * GELU_B * square)
        grad_inner = (nt(rows_of(cotangent, c), mlp_out[...]) * slope).astype(jnp.bfloat16)
        inner_s[...] = grad_inner
        halve(nt(grad_inner, mlp_in[...]), own_d, send_d)
        core_d(c).start()
        halve(nn(active, mlp_out[...]), own_f, send_f)
        core_f(c).start()

    def finish_grad(c):
        slot = lax.rem(c, 2)
        cross_copy_d(c).wait()
        mine = half_d[...].astype(jnp.float32) + cross_d[slot].astype(jnp.float32)
        summed_d[slot, core] = mine.astype(jnp.bfloat16)
        core_s(c).start()
        cross_copy_f(c).wait()
        part = pl.ds(pl.multiple_of(c * SUB, SUB), SUB)
        moved = update[c].reshape(2, 2, SUB, width)
        mine = jnp.where(core == 0, moved[0], moved[1])
        mine = jnp.where(side == 0, mine[0], mine[1]).astype(jnp.float32)
        total = tokens[head, part, :].astype(jnp.float32) + mine + half_f[side].astype(jnp.float32)
        layer_out[part, :] = (total + cross_f[slot].astype(jnp.float32)).astype(jnp.bfloat16)

    def cross_grad(c):
        slot = lax.rem(c, 2)
        core_d(c).wait()
        half_d[...] = (own_d[...] + got_d[slot].astype(jnp.float32)).astype(jnp.bfloat16)
        cross_copy_d(c).start()
        core_f(c).wait()
        total = own_f[...] + got_f[slot].astype(jnp.float32)
        half_f[...] = total.astype(jnp.bfloat16).reshape(half_f.shape)
        cross_copy_f(c).start()

    def weight_grads(c):
        acc_in[...] += tn(normed_s[...], inner_s[...])
        acc_out[...] += tn(rows_of(cotangent, c), act_s[...])

    def write_backward(c):
        core_s(c).wait()
        normed, scale = norm_parts(one_rows(c))
        grad = summed_d[lax.rem(c, 2)].reshape(4 * SUB, width).astype(jnp.float32)
        wide = rows_of(cotangent, c).astype(jnp.float32) + norm_vjp(normed, scale, grad)
        wide_s[...] = wide.reshape(wide_s.shape)
        part = pl.ds(pl.multiple_of(c * SUB, SUB), SUB)
        mine = pl.ds(pl.multiple_of(side * SUB, SUB), SUB)
        grad_one[part, :] = wide_s[core, mine, :]
        narrow = wide.astype(jnp.bfloat16)
        mixed = mixed_t[c]
        acc_write[...] += nn(mixed, narrow)
        grad_mixed = nt(write_out[...], narrow).astype(jnp.bfloat16)
        query = query_t[c]
        product = grad_mixed.astype(jnp.float32) * mixed.astype(jnp.float32)

        def body(start, carry):
            here = pl.ds(start, block)
            bias = mask_of(c, start)
            kept = []
            for h in range(heads):
                rows = head_rows(h)
                scores = nn(key[h, here, :], query[rows])
                weights = jnp.exp2(scores * (SCALE * LOG2E) + (bias + log_total[c, h : h + 1]))
                grad_weights = nn(value[h, here, :], grad_mixed[rows])
                delta = jnp.sum(product[rows], axis=0, keepdims=True)
                grad_scores = (weights * (grad_weights - delta)).astype(jnp.bfloat16)
                grad_key[h, here, :] += nt(grad_scores, query[rows])
                grad_value[h, here, :] += nt(weights.astype(jnp.bfloat16), grad_mixed[rows])
                kept.append(carry[h] + nn(key_t[rows, here], grad_scores))
            return tuple(kept)

        zero = jnp.zeros((HD, query.shape[1]), jnp.float32)
        grads = each_block(body, (zero,) * heads)
        grad_query_t[c] = (jnp.concatenate(grads, axis=0) * SCALE).astype(jnp.bfloat16)

    def step(i, carry):
        @pl.when(i < chunks)
        def _():
            write_forward(i)

        @pl.when(jnp.logical_and(i >= 1, i <= chunks))
        def _():
            finish_update(i - 1)

        @pl.when(i < chunks)
        def _():
            cross_update(i)

        @pl.when(jnp.logical_and(i >= 1, i <= chunks))
        def _():
            feed_forward(i - 1)

        @pl.when(i >= 2)
        def _():
            finish_grad(i - 2)

        @pl.when(jnp.logical_and(i >= 1, i <= chunks))
        def _():
            cross_grad(i - 1)
            weight_grads(i - 1)

        @pl.when(i >= 2)
        def _():
            write_backward(i - 2)

        return carry

    lax.fori_loop(0, chunks + 2, step, 0)
    grad_key[...] = grad_key[...] * SCALE
    grad_mlp_in[...] = acc_in[...].astype(jnp.bfloat16)
    grad_mlp_out[...] = acc_out[...].astype(jnp.bfloat16)
    grad_write_out[...] = acc_write[...].T.astype(jnp.bfloat16)


def middle(tokens, cotangent, query_write, keys, values, latent_image, token_image, write_out, mlp_in, mlp_out):
    rows, width = tokens.shape
    column = write_out.shape[0]
    hidden = mlp_in.shape[1]
    heads = column // HD
    latents = keys.shape[0]
    quarter = rows // 4
    chunks = quarter // SUB
    size = 4 * SUB
    by_chunk = query_write.reshape(2, 2, chunks, SUB, column).transpose(2, 4, 1, 0, 3)
    query_t = by_chunk.reshape(chunks, column, size)
    images = token_image.reshape(2, 2, chunks, SUB).transpose(2, 1, 0, 3).reshape(chunks, 1, size)
    latent_wide = jnp.broadcast_to(latent_image[:, None], (latents, 128))
    key_heads = keys.reshape(latents, heads, HD).transpose(1, 0, 2)
    value_heads = values.reshape(latents, heads, HD).transpose(1, 0, 2)
    half = (2 * SUB, width)
    low, wide = jnp.bfloat16, jnp.float32
    vmem = pl.BlockSpec(memory_space=pltpu.VMEM)
    exchange = [
        pltpu.VMEM(half, wide),
        pltpu.VMEM(half, low),
        pltpu.VMEM((2, *half), low),
        pltpu.VMEM(half, low),
        pltpu.VMEM((2, *half), low),
    ]
    outs = pl.pallas_call(
        middle_kernel,
        out_shape=[
            jax.ShapeDtypeStruct((quarter, width), low),
            jax.ShapeDtypeStruct((quarter, width), wide),
            jax.ShapeDtypeStruct((chunks, column, size), low),
            jax.ShapeDtypeStruct((heads, latents, HD), wide),
            jax.ShapeDtypeStruct((heads, latents, HD), wide),
            jax.ShapeDtypeStruct((width, hidden), low),
            jax.ShapeDtypeStruct((width, hidden), low),
            jax.ShapeDtypeStruct((width, column), low),
        ],
        in_specs=[vmem] * 12,
        out_specs=[vmem] * 8,
        scratch_shapes=[
            pltpu.VMEM((chunks, 2, *half), low),
            pltpu.VMEM((chunks, column, size), low),
            pltpu.VMEM((chunks, 8, size), wide),
            *exchange,
            *exchange,
            pltpu.VMEM((2, 2, *half), low),
            pltpu.VMEM(half, wide),
            pltpu.VMEM(half, low),
            pltpu.VMEM((2, *half), low),
            pltpu.VMEM((2, SUB, width), low),
            pltpu.VMEM((2, SUB, width), low),
            pltpu.VMEM((width, hidden), wide),
            pltpu.VMEM((width, hidden), wide),
            pltpu.VMEM((column, width), wide),
            pltpu.VMEM((size, width), low),
            pltpu.VMEM((size, hidden), low),
            pltpu.VMEM((size, hidden), low),
            pltpu.VMEM((2, *half), wide),
            pltpu.SemaphoreType.DMA((8, 2)),
            pltpu.SemaphoreType.DMA((8, 2)),
        ],
        compiler_params=pltpu.CompilerParams(
            collective_id=1, has_side_effects=True, vmem_limit_bytes=62 << 20
        ),
        name="middle",
    )(
        tokens.reshape(4, quarter, width),
        cotangent.reshape(4, quarter, width),
        query_t,
        key_heads,
        value_heads,
        keys.T,
        values.T,
        latent_wide,
        images,
        write_out,
        mlp_in,
        mlp_out,
    )
    out, grad_one, grad_query_t, grad_key, grad_value, grad_in, grad_out, grad_write = outs
    grad_query = grad_query_t.reshape(chunks, column, 2, 2, SUB).transpose(3, 2, 0, 4, 1)
    return (
        out,
        grad_one,
        grad_query.reshape(rows, column),
        grad_key.transpose(1, 0, 2).reshape(latents, column),
        grad_value.transpose(1, 0, 2).reshape(latents, column),
        grad_in,
        grad_out,
        grad_write,
    )


def heads_view(values):
    return values.reshape(values.shape[0], values.shape[1] // HD, HD)


def shards(
    tokens,
    latents,
    image_groups,
    read_query,
    read_key,
    read_value,
    read_out,
    write_query,
    write_key,
    write_value,
    write_out,
    mlp_in,
    mlp_out,
    cotangent,
):
    rows = tokens.shape[0]
    owned = latents.shape[0]
    column = read_query.shape[1]
    heads_here = column // HD
    tok_count = lax.axis_size("tok")
    head_count = lax.axis_size("head")
    tok_index = lax.axis_index("tok")
    head_index = lax.axis_index("head")
    groups_here = rows // GROUP
    total_groups = groups_here * tok_count
    all_latents = total_groups * LPG
    bounds = jnp.cumsum(image_groups)
    group_ids = jnp.arange(total_groups, dtype=jnp.int32)
    group_image = jnp.sum((bounds[None, :] <= group_ids[:, None]).astype(jnp.int32), axis=1)
    latent_image = jnp.repeat(group_image, LPG, total_repeat_length=all_latents)
    local_groups = lax.dynamic_slice_in_dim(group_image, tok_index * groups_here, groups_here)
    token_image = jnp.repeat(local_groups, GROUP, total_repeat_length=rows)
    own_image = lax.dynamic_slice_in_dim(latent_image, tok_index * owned, owned)
    key_image = jnp.concatenate([token_image, own_image], axis=0)
    key_count = rows + owned
    tokens_full = tokens.astype(jnp.float32)
    latents_full = latents.astype(jnp.float32)
    normed_x = norm_rows(tokens_full).astype(jnp.bfloat16)
    normed_lat = norm_rows(latents_full).astype(jnp.bfloat16)
    query_own = matmul(normed_lat, read_query).astype(jnp.bfloat16)
    query_all = lax.all_gather(query_own, "tok", axis=0, tiled=True)
    keys_here = jnp.concatenate(
        [matmul(normed_x, read_key), matmul(normed_lat, read_key)], axis=0
    ).astype(jnp.bfloat16)
    values_here = jnp.concatenate(
        [matmul(normed_x, read_value), matmul(normed_lat, read_value)], axis=0
    ).astype(jnp.bfloat16)
    keys_split = heads_view(keys_here)
    values_split = heads_view(values_here)
    latent_block = min(512, all_latents)
    latent_blocks = all_latents // latent_block

    def read_scores(query_block, image_block):
        scores = (
            jnp.einsum(
                "qhd,khd->qhk",
                heads_view(query_block),
                keys_split,
                preferred_element_type=jnp.float32,
            )
            * 0.125
        )
        mask = (image_block[:, None] == key_image[None, :])[:, None, :]
        return (scores, mask)

    def read_block(operands):
        query_block, image_block = operands
        scores, mask = read_scores(query_block, image_block)
        weights = jnp.where(mask, jnp.exp(scores), 0.0)
        totals = jnp.sum(weights, axis=-1)
        summed = jnp.einsum(
            "qhk,khd->qhd",
            weights,
            values_split,
            precision=triple,
            preferred_element_type=jnp.float32,
        )
        return (totals, summed.reshape(query_block.shape[0], column))

    query_blocks = query_all.reshape(latent_blocks, latent_block, column)
    image_blocks = latent_image.reshape(latent_blocks, latent_block)
    totals, sums = lax.map(read_block, (query_blocks, image_blocks))
    totals = totals.reshape(all_latents, heads_here)
    sums = sums.reshape(all_latents, column)
    totals_all, sums_all = lax.psum((totals, sums), "tok")
    total_own = lax.dynamic_slice_in_dim(totals_all, tok_index * owned, owned)
    sum_own = lax.dynamic_slice_in_dim(sums_all, tok_index * owned, owned)
    mixed_wide = (heads_view(sum_own) / total_own[:, :, None]).reshape(owned, column)
    read_mixed = mixed_wide.astype(jnp.bfloat16)
    latents_one = latents_full + lax.psum(matmul(read_mixed, read_out), "head")
    normed_one, norm_one_back = jax.vjp(norm_rows, latents_one)
    normed_one = normed_one.astype(jnp.bfloat16)
    wkey_own = matmul(normed_one, write_key).astype(jnp.bfloat16)
    wvalue_own = matmul(normed_one, write_value).astype(jnp.bfloat16)
    wkey_all, wvalue_all = (
        lax.all_gather(wkey_own, "tok", axis=0, tiled=True),
        lax.all_gather(wvalue_own, "tok", axis=0, tiled=True),
    )
    query_write = matmul(normed_x, write_query).astype(jnp.bfloat16)
    layer_out, grad_one_own, grad_wquery, grad_wkey_all, grad_wvalue_all, grad_mlp_in, grad_mlp_out, grad_write_out = middle(
        tokens, cotangent, query_write, wkey_all, wvalue_all, latent_image, token_image, write_out, mlp_in, mlp_out
    )
    quarter = rows // head_count
    row_start = head_index * quarter
    grad_wkey, grad_wvalue = (
        lax.psum_scatter(grad_wkey_all, "tok", scatter_dimension=0, tiled=True),
        lax.psum_scatter(grad_wvalue_all, "tok", scatter_dimension=0, tiled=True),
    )
    grad_wkey = grad_wkey.astype(jnp.bfloat16)
    grad_wvalue = grad_wvalue.astype(jnp.bfloat16)
    grad_write_key = left_trans(normed_one, grad_wkey)
    grad_write_value = left_trans(normed_one, grad_wvalue)
    grad_write_query = left_trans(normed_x, grad_wquery)
    grad_normed_one = lax.psum(
        right_trans(grad_wkey, write_key) + right_trans(grad_wvalue, write_value), "head"
    )
    grad_latents_one = norm_one_back(grad_normed_one)[0]
    grad_latent_branch = grad_latents_one.astype(jnp.bfloat16)
    grad_read_out = left_trans(grad_latent_branch, read_mixed)
    grad_rmixed = right_trans(grad_latent_branch, read_out).astype(jnp.bfloat16)
    grad_rmixed_wide = grad_rmixed.astype(jnp.float32)
    delta_own = jnp.sum(heads_view(grad_rmixed_wide * mixed_wide), axis=-1)
    log_own = jnp.log(total_own)
    grad_mixed_all, delta_all, log_all = (
        lax.all_gather(grad_rmixed_wide, "tok", axis=0, tiled=True),
        lax.all_gather(delta_own, "tok", axis=0, tiled=True),
        lax.all_gather(log_own, "tok", axis=0, tiled=True),
    )
    grad_mixed_all = grad_mixed_all.astype(jnp.bfloat16)

    def read_back(carry, operands):
        key_total, value_total = carry
        query_block, image_block, grad_block, delta_block, log_block = operands
        scores, mask = read_scores(query_block, image_block)
        probs = jnp.where(mask, jnp.exp(scores - log_block[:, :, None]), 0.0)
        grad_probs = jnp.einsum(
            "qhd,khd->qhk", heads_view(grad_block), values_split, preferred_element_type=jnp.float32
        )
        grad_scores = (probs * (grad_probs - delta_block[:, :, None])).astype(jnp.bfloat16)
        grad_query = (
            jnp.einsum("qhk,khd->qhd", grad_scores, keys_split, preferred_element_type=jnp.float32)
            * 0.125
        )
        key_total = (
            key_total
            + jnp.einsum(
                "qhk,qhd->khd",
                grad_scores,
                heads_view(query_block),
                preferred_element_type=jnp.float32,
            ).reshape(key_count, column)
            * 0.125
        )
        value_total = value_total + jnp.einsum(
            "qhk,qhd->khd",
            probs,
            heads_view(grad_block),
            precision=triple,
            preferred_element_type=jnp.float32,
        ).reshape(key_count, column)
        return ((key_total, value_total), grad_query.reshape(query_block.shape[0], column))

    key_zeros = jnp.zeros((key_count, column), jnp.float32)
    (grad_keys, grad_values), grad_query_all = lax.scan(
        read_back,
        (key_zeros, key_zeros),
        (
            query_blocks,
            image_blocks,
            grad_mixed_all.reshape(latent_blocks, latent_block, column),
            delta_all.reshape(latent_blocks, latent_block, heads_here),
            log_all.reshape(latent_blocks, latent_block, heads_here),
        ),
    )
    grad_query_all = grad_query_all.reshape(all_latents, column)
    grad_query_own = lax.psum_scatter(
        grad_query_all, "tok", scatter_dimension=0, tiled=True
    ).astype(jnp.bfloat16)
    grad_keys = grad_keys.astype(jnp.bfloat16)
    grad_values = grad_values.astype(jnp.bfloat16)
    grad_key_tok = grad_keys[:rows]
    grad_key_lat = grad_keys[rows:]
    grad_value_tok = grad_values[:rows]
    grad_value_lat = grad_values[rows:]
    grad_read_query = left_trans(normed_lat, grad_query_own)
    grad_read_key = left_trans(normed_x, grad_key_tok) + left_trans(normed_lat, grad_key_lat)
    grad_read_value = left_trans(normed_x, grad_value_tok) + left_trans(normed_lat, grad_value_lat)
    grad_normed_x = (
        right_trans(grad_key_tok, read_key)
        + right_trans(grad_value_tok, read_value)
        + right_trans(grad_wquery, write_query)
    )
    grad_normed_lat = (
        right_trans(grad_query_own, read_query)
        + right_trans(grad_key_lat, read_key)
        + right_trans(grad_value_lat, read_value)
    )
    grad_x_rows, grad_lat_rows = (
        lax.psum_scatter(grad_normed_x, "head", scatter_dimension=0, tiled=True),
        lax.psum_scatter(grad_normed_lat, "head", scatter_dimension=0, tiled=True),
    )
    latent_quarter = owned // head_count
    latent_start = head_index * latent_quarter
    token_rows = lax.dynamic_slice_in_dim(tokens_full, row_start, quarter)
    unused_x, norm_x_back = jax.vjp(norm_rows, token_rows)
    input_grad = (
        grad_one_own + norm_x_back(grad_x_rows)[0]
    )
    latent_rows = lax.dynamic_slice_in_dim(latents_full, latent_start, latent_quarter)
    unused_lat, norm_lat_back = jax.vjp(norm_rows, latent_rows)
    latent_grad = (
        lax.dynamic_slice_in_dim(grad_latents_one, latent_start, latent_quarter)
        + norm_lat_back(grad_lat_rows)[0]
    )
    partials = jnp.concatenate(
        [
            grad_read_query.astype(jnp.bfloat16),
            grad_read_key.astype(jnp.bfloat16),
            grad_read_value.astype(jnp.bfloat16),
            grad_read_out.astype(jnp.bfloat16),
            grad_write_query.astype(jnp.bfloat16),
            grad_write_key.astype(jnp.bfloat16),
            grad_write_value.astype(jnp.bfloat16),
            grad_write_out,
            grad_mlp_in,
            grad_mlp_out,
        ],
        axis=1,
    )
    grads = scatter_grads(partials, tok_count)
    summed = [grads[:, k * column : (k + 1) * column] for k in range(8)]
    hidden = mlp_in.shape[1]
    summed.append(grads[:, 8 * column : 8 * column + hidden])
    summed.append(grads[:, 8 * column + hidden :].T)
    summed[3] = summed[3].T
    summed[7] = summed[7].T
    return (
        layer_out,
        input_grad,
        latent_grad,
        summed[0],
        summed[1],
        summed[2],
        summed[3],
        summed[4],
        summed[5],
        summed[6],
        summed[7],
        summed[8],
        summed[9],
    )


def solution(mesh):
    return jax.shard_map(
        shards,
        mesh=mesh,
        in_specs=(
            P("tok", None),
            P("tok", None),
            P(),
            P(None, "head"),
            P(None, "head"),
            P(None, "head"),
            P("head", None),
            P(None, "head"),
            P(None, "head"),
            P(None, "head"),
            P("head", None),
            P(None, "head"),
            P("head", None),
            P("tok", None),
        ),
        out_specs=(
            P(("tok", "head"), None),
            P(("tok", "head"), None),
            P(("tok", "head"), None),
            P("tok", "head"),
            P("tok", "head"),
            P("tok", "head"),
            P("head", "tok"),
            P("tok", "head"),
            P("tok", "head"),
            P("tok", "head"),
            P("head", "tok"),
            P("tok", "head"),
            P("head", "tok"),
        ),
        check_vma=False,
    )
```

```python
from functools import partial

import jax
import jax.numpy as jnp
from jax import lax
from jax.experimental import pallas as pl
from jax.experimental.pallas import tpu as pltpu
from jax.sharding import PartitionSpec as P

MESH = pl.DeviceIdType.MESH
HD = 64
GROUP = 256
LPG = 8
epsilon = 1e-05
SUB = 64
SCALE = 0.125
LOG2E = 1.4426950408889634
MASKED = -1e30
GELU_A = 0.7978845608028654
GELU_B = 0.044715


def nn(left, right):
    return lax.dot_general(left, right, (((1,), (0,)), ((), ())), preferred_element_type=jnp.float32)


def nt(left, right):
    return lax.dot_general(left, right, (((1,), (1,)), ((), ())), preferred_element_type=jnp.float32)


def tn(left, right):
    return lax.dot_general(left, right, (((0,), (0,)), ((), ())), preferred_element_type=jnp.float32)


def norm_parts(values):
    center = values - jnp.mean(values, axis=-1, keepdims=True)
    scale = lax.rsqrt(jnp.mean(center * center, axis=-1, keepdims=True) + epsilon)
    return center * scale, scale


def norm_vjp(normed, scale, grad):
    return scale * (
        grad
        - jnp.mean(grad, axis=-1, keepdims=True)
        - normed * jnp.mean(grad * normed, axis=-1, keepdims=True)
    )


def image_of(counts, group):
    bound = jnp.int32(0)
    image = jnp.zeros_like(group)
    for m in range(counts.shape[0]):
        bound = bound + counts[m]
        image = image + jnp.where(bound <= group, 1, 0)
    return image


def latent_row_image(counts, start, count):
    group = lax.shift_right_logical(lax.broadcasted_iota(jnp.int32, (1, count), 1) + start, 3)
    return image_of(counts, group)


def head_rows(h):
    return slice(h * HD, (h + 1) * HD)


def chunk_rows(ref, c):
    part = pl.ds(pl.multiple_of(c * SUB, SUB), SUB)
    return jnp.concatenate([ref[q, part, :] for q in (0, 2, 1, 3)], axis=0)


def greet_all(tok, head, tok_count, head_count):
    barrier = pltpu.get_barrier_semaphore()

    def greet(step, carry):
        peer = lax.rem(tok + step, tok_count)
        pl.semaphore_signal(barrier, inc=1, device_id=(peer, head), device_id_type=MESH)
        return carry

    lax.fori_loop(1, tok_count, greet, 0)
    for step in range(1, head_count):
        peer = lax.rem(head + step, head_count)
        pl.semaphore_signal(barrier, inc=1, device_id=(tok, peer), device_id_type=MESH)
    pl.semaphore_wait(barrier, tok_count + head_count - 2)


class Spread:
    def __init__(self, axis, tok, head, count, source, got, sems):
        self.axis, self.tok, self.head, self.count = axis, tok, head, count
        self.me = tok if axis == "tok" else head
        self.source, self.got, self.sems = source, got, sems

    def copy(self, peer, slot):
        return pltpu.make_async_remote_copy(
            src_ref=self.source(peer),
            dst_ref=self.got.at[slot],
            send_sem=self.sems.at[0, peer],
            recv_sem=self.sems.at[1, slot],
            device_id=(peer, self.head) if self.axis == "tok" else (self.tok, peer),
            device_id_type=MESH,
        )

    def start(self):
        def go(step, carry):
            self.copy(lax.rem(self.me + step, self.count), self.me).start()
            return carry

        lax.fori_loop(1, self.count, go, 0)

    def wait(self):
        def go(step, carry):
            peer = lax.rem(self.me + step, self.count)
            self.copy(peer, peer).wait()
            return carry

        lax.fori_loop(1, self.count, go, 0)


class Scatter:
    def __init__(self, tok, head, parts, got_one, sums, got_two, sems):
        self.head, self.mine, self.side = head, tok // 2, lax.rem(tok, 2)
        self.parts, self.got_one, self.sums, self.got_two, self.sems = parts, got_one, sums, got_two, sems
        self.outer = parts.shape[0]

    def first(self, block):
        return pltpu.make_async_remote_copy(
            src_ref=self.parts.at[block, 1 - self.side],
            dst_ref=self.got_one.at[block],
            send_sem=self.sems.at[0, block],
            recv_sem=self.sems.at[1, block],
            device_id=(self.mine * 2 + (1 - self.side), self.head),
            device_id_type=MESH,
        )

    def second(self, block, source):
        return pltpu.make_async_remote_copy(
            src_ref=self.sums.at[block],
            dst_ref=self.got_two.at[source],
            send_sem=self.sems.at[2, block],
            recv_sem=self.sems.at[3, source],
            device_id=(block * 2 + self.side, self.head),
            device_id_type=MESH,
        )

    def start(self):
        def go(step, carry):
            self.first(lax.rem(self.mine + step, self.outer)).start()
            return carry

        lax.fori_loop(1, self.outer + 1, go, 0)

    def forward(self, step):
        block = lax.rem(self.mine + step, self.outer)
        self.first(block).wait()
        total = self.parts[block, self.side].astype(jnp.float32) + self.got_one[block].astype(jnp.float32)
        self.sums[block] = total.astype(jnp.bfloat16)
        self.second(block, self.mine).start()

    def forward_all(self):
        def go(step, carry):
            self.forward(step)
            return carry

        lax.fori_loop(1, self.outer, go, 0)

    def finish(self):
        self.first(self.mine).wait()
        total = self.parts[self.mine, self.side].astype(jnp.float32) + self.got_one[self.mine].astype(jnp.float32)

        def go(step, total):
            peer = lax.rem(self.mine + step, self.outer)
            self.second(peer, peer).wait()
            return total + self.got_two[peer].astype(jnp.float32)

        return lax.fori_loop(1, self.outer, go, total)


def scatter_scratch(outer, rows, width):
    slots = pltpu.VMEM((outer, rows, width), jnp.bfloat16)
    return [slots, slots, slots, pltpu.SemaphoreType.DMA((4, outer))]


def split_three(value):
    high = value.astype(jnp.bfloat16).astype(jnp.float32)
    rest = value - high
    middle_part = rest.astype(jnp.bfloat16).astype(jnp.float32)
    return high, middle_part, rest - middle_part


def pick_lanes(shape, columns):
    lane = lax.broadcasted_iota(jnp.int32, shape, 1)
    value = jnp.zeros(shape, jnp.float32)
    for at, column in columns:
        value = jnp.where(lane == at, column, value)
    return value


def by_head(shape, columns):
    lane = lax.broadcasted_iota(jnp.int32, shape, 1)
    value = jnp.broadcast_to(columns[-1], shape)
    for h in range(len(columns) - 2, -1, -1):
        value = jnp.where(lane < (h + 1) * HD, columns[h], value)
    return value


def chunk_bias(counts, tok, groups_here, c, quarter, row_image, rows):
    kept = []
    for q in (0, 2, 1, 3):
        group = tok * groups_here + (q * quarter + c * SUB) // GROUP
        image = image_of(counts, group)
        kept.append([jnp.where(row_image == image, row, MASKED) for row in rows])
    return kept


def add_rows(values, rows):
    count = values.shape[0] // len(rows)
    return jnp.concatenate([values[k * count : (k + 1) * count] + row for k, row in enumerate(rows)], axis=0)


def front_kernel(
    counts, tokens, latents, rquery, rkey, rvalue, rout, wquery, wkey, wvalue,
    query_t, key, value, key_t, value_t, read_key, read_value, read_key_t, own_key, own_value, own_key_t,
    read_query_t, lat_one, mixed_out,
    normed_s, query_all, value_t_s, own_value_t, sums, sums_send, sums_got, head_parts, pair_all,
    query_sems, sums_sems, head_sems, pair_sems,
):
    tok_count, owned = query_all.shape[0], query_all.shape[1]
    head_count = head_parts.shape[0]
    chunks, column = query_t.shape[0], query_t.shape[1]
    heads = column // HD
    quarter = tokens.shape[1]
    groups_here = 4 * quarter // GROUP
    latent_count = tok_count * owned
    block = min(512, latent_count)
    blocks, per = latent_count // block, block // owned
    tok, head = lax.axis_index("tok"), lax.axis_index("head")
    low = jnp.bfloat16
    latents_wide = latents[...].astype(jnp.float32)
    normed_lat = norm_parts(latents_wide)[0].astype(low)
    query_all[tok] = nn(normed_lat, rquery[...]).astype(low)
    greet_all(tok, head, tok_count, head_count)
    queries = Spread("tok", tok, head, tok_count, lambda peer: query_all.at[tok], query_all, query_sems)
    queries.start()

    def keep_heads(ref, wide):
        for h in range(heads):
            ref[h] = wide[:, head_rows(h)]

    keys = nn(normed_lat, rkey[...]).astype(low)
    values = nn(normed_lat, rvalue[...]).astype(low)
    keep_heads(own_key, keys)
    keep_heads(own_value, values)
    own_key_t[...] = keys.T
    own_value_t[...] = values.T

    def project(c, carry):
        normed = norm_parts(chunk_rows(tokens, c).astype(jnp.float32))[0].astype(low)
        normed_s[c] = normed
        keys = nn(normed, rkey[...]).astype(low)
        values = nn(normed, rvalue[...]).astype(low)
        keep_heads(read_key.at[c], keys)
        keep_heads(read_value.at[c], values)
        read_key_t[c] = keys.T
        value_t_s[c] = values.T
        return carry

    lax.fori_loop(0, chunks, project, 0)
    sums[...] = jnp.zeros_like(sums)
    queries.wait()

    def attend(scores, rows, values_t, here, h):
        weights = jnp.exp2(add_rows(scores * (SCALE * LOG2E), rows))
        sums[column + h : column + h + 1, here] += jnp.sum(weights, axis=0, keepdims=True)
        sums[head_rows(h), here] += nn(values_t, weights.astype(low))

    def read_block(b, carry):
        start = pl.multiple_of(b * block, block)
        here = pl.ds(start, block)
        query = query_all[pl.ds(b * per, per)].reshape(block, column).T
        read_query_t[:, here] = query
        row_image = latent_row_image(counts, start, block)
        zero = jnp.zeros((1, block), jnp.float32)

        def read_chunk(c, carry):
            rows = chunk_bias(counts, tok, groups_here, c, quarter, row_image, [zero])
            rows = [row[0] for row in rows]
            for h in range(heads):
                scores = nn(read_key[c, h], query[head_rows(h)])
                attend(scores, rows, value_t_s[c, head_rows(h)], here, h)
            return carry

        lax.fori_loop(0, chunks, read_chunk, 0)
        rows = [
            jnp.where(row_image == image_of(counts, tok * groups_here + g), zero, MASKED)
            for g in range(owned // LPG)
        ]
        for h in range(heads):
            scores = nn(own_key[h], query[head_rows(h)])
            attend(scores, rows, own_value_t[head_rows(h), :], here, h)
        total = sums[column : column + heads, here]
        high = total.astype(low).astype(jnp.float32)
        sums[column : column + heads, here] = high
        sums[column + heads : column + 2 * heads, here] = total - high
        sums_send[pl.ds(b * per, per)] = sums[:, here].T.astype(low).reshape(per, owned, sums.shape[0])
        return carry

    lax.fori_loop(0, blocks, read_block, 0)
    totals = Spread("tok", tok, head, tok_count, lambda peer: sums_send.at[peer], sums_got, sums_sems)
    totals.start()

    def project_query(c, carry):
        query_t[c] = nn(normed_s[c], wquery[...]).astype(low).T
        return carry

    lax.fori_loop(0, chunks, project_query, 0)
    totals.wait()
    sums_got[tok] = sums_send[tok]
    summed = lax.fori_loop(
        1, tok_count, lambda s, kept: kept + sums_got[s].astype(jnp.float32), sums_got[0].astype(jnp.float32)
    )
    whole = [
        summed[:, column + h : column + h + 1] + summed[:, column + heads + h : column + heads + h + 1]
        for h in range(heads)
    ]
    mixed = summed[:, :column] / by_head((owned, column), whole)
    mixed_out[:, :column] = mixed
    mixed_out[:, column:] = pick_lanes(
        (owned, mixed_out.shape[1] - column), [(h, -jnp.log2(whole[h])) for h in range(heads)]
    )
    head_parts[head] = nn(mixed.astype(low), rout[...]).astype(low)
    moved = Spread("head", tok, head, head_count, lambda peer: head_parts.at[head], head_parts, head_sems)
    moved.start()
    moved.wait()
    latents_one = latents_wide
    for s in range(head_count):
        latents_one = latents_one + head_parts[s].astype(jnp.float32)
    lat_one[...] = latents_one
    normed_one = norm_parts(latents_one)[0].astype(low)
    pair_all[tok, 0] = nn(normed_one, wkey[...]).astype(low)
    pair_all[tok, 1] = nn(normed_one, wvalue[...]).astype(low)
    pairs = Spread("tok", tok, head, tok_count, lambda peer: pair_all.at[tok], pair_all, pair_sems)
    pairs.start()
    pairs.wait()

    def unpack(b, carry):
        start = pl.multiple_of(b * block, block)
        here = pl.ds(start, block)
        for k, (straight, turned) in enumerate(((key, key_t), (value, value_t))):
            wide = pair_all[pl.ds(b * per, per), k].reshape(block, column)
            for h in range(heads):
                straight[h, here, :] = wide[:, head_rows(h)]
            turned[:, here] = wide.T
        return carry

    lax.fori_loop(0, blocks, unpack, 0)


def front(counts, tokens, latents, rquery, rkey, rvalue, rout, wquery, wkey, wvalue, tok_count, head_count):
    rows, width = tokens.shape
    owned, column = latents.shape[0], rquery.shape[1]
    heads = column // HD
    quarter = rows // 4
    chunks, size = quarter // SUB, 4 * SUB
    latent_count = owned * tok_count
    low, wide = jnp.bfloat16, jnp.float32
    vmem = pl.BlockSpec(memory_space=pltpu.VMEM)
    packed = 256
    return pl.pallas_call(
        front_kernel,
        out_shape=[
            jax.ShapeDtypeStruct((chunks, column, size), low),
            jax.ShapeDtypeStruct((heads, latent_count, HD), low),
            jax.ShapeDtypeStruct((heads, latent_count, HD), low),
            jax.ShapeDtypeStruct((column, latent_count), low),
            jax.ShapeDtypeStruct((column, latent_count), low),
            jax.ShapeDtypeStruct((chunks, heads, size, HD), low),
            jax.ShapeDtypeStruct((chunks, heads, size, HD), low),
            jax.ShapeDtypeStruct((chunks, column, size), low),
            jax.ShapeDtypeStruct((heads, owned, HD), low),
            jax.ShapeDtypeStruct((heads, owned, HD), low),
            jax.ShapeDtypeStruct((column, owned), low),
            jax.ShapeDtypeStruct((column, latent_count), low),
            jax.ShapeDtypeStruct((owned, width), wide),
            jax.ShapeDtypeStruct((owned, packed), wide),
        ],
        in_specs=[pl.BlockSpec(memory_space=pltpu.SMEM)] + [vmem] * 9,
        out_specs=[vmem] * 14,
        scratch_shapes=[
            pltpu.VMEM((chunks, size, width), low),
            pltpu.VMEM((tok_count, owned, column), low),
            pltpu.VMEM((chunks, column, size), low),
            pltpu.VMEM((column, owned), low),
            pltpu.VMEM((packed, latent_count), wide),
            pltpu.VMEM((tok_count, owned, packed), low),
            pltpu.VMEM((tok_count, owned, packed), low),
            pltpu.VMEM((head_count, owned, width), low),
            pltpu.VMEM((tok_count, 2, owned, column), low),
            pltpu.SemaphoreType.DMA((2, tok_count)),
            pltpu.SemaphoreType.DMA((2, tok_count)),
            pltpu.SemaphoreType.DMA((2, head_count)),
            pltpu.SemaphoreType.DMA((2, tok_count)),
        ],
        compiler_params=pltpu.CompilerParams(collective_id=2, has_side_effects=True, vmem_limit_bytes=62 << 20),
        name="front",
    )(counts, tokens.reshape(4, quarter, width), latents, rquery, rkey, rvalue, rout, wquery, wkey, wvalue)


def middle_kernel(
    counts,
    tokens,
    cotangent,
    query_t,
    key,
    value,
    key_t,
    value_t,
    write_out,
    mlp_in,
    mlp_out,
    layer_out,
    grad_one,
    grad_query_t,
    grad_pairs,
    grad_mlp_in,
    grad_mlp_out,
    grad_write_out,
    update,
    mixed_t,
    log_total,
    own_a,
    send_a,
    got_a,
    half_a,
    cross_a,
    own_d,
    send_d,
    got_d,
    half_d,
    cross_d,
    summed_d,
    own_f,
    send_f,
    got_f,
    half_f,
    cross_f,
    acc_in,
    acc_out,
    acc_write,
    normed_s,
    act_s,
    inner_s,
    wide_s,
    latent_image,
    grad_key,
    grad_value,
    send_sems,
    recv_sems,
):
    chunks = query_t.shape[0]
    heads = key.shape[0]
    latents = key.shape[1]
    width = tokens.shape[2]
    block = min(512, latents)
    blocks = latents // block
    tok = lax.axis_index("tok")
    head = lax.axis_index("head")
    core = lax.rem(head, 2)
    side = head // 2
    other = 1 - core
    core_peer = (tok, side * 2 + other)
    side_peer = (tok, (1 - side) * 2 + core)
    barrier = pltpu.get_barrier_semaphore()
    for peer in (core_peer, side_peer):
        pl.semaphore_signal(barrier, inc=1, device_id=peer, device_id_type=MESH)
    pl.semaphore_wait(barrier, 2)

    def copy(kind, chunk, source, target, peer):
        slot = lax.rem(chunk, 2)
        return pltpu.make_async_remote_copy(
            src_ref=source,
            dst_ref=target,
            send_sem=send_sems.at[kind, slot],
            recv_sem=recv_sems.at[kind, slot],
            device_id=peer,
            device_id_type=MESH,
        )

    def core_a(c):
        return copy(0, c, send_a, got_a.at[lax.rem(c, 2)], core_peer)

    def cross_copy_a(c):
        return copy(1, c, half_a, cross_a.at[lax.rem(c, 2)], side_peer)

    def core_u(c):
        return copy(2, c, update.at[c, core], update.at[c, core], core_peer)

    def core_d(c):
        return copy(3, c, send_d, got_d.at[lax.rem(c, 2)], core_peer)

    def cross_copy_d(c):
        return copy(4, c, half_d, cross_d.at[lax.rem(c, 2)], side_peer)

    def core_s(c):
        half = summed_d.at[lax.rem(c, 2), core]
        return copy(5, c, half, half, core_peer)

    def core_f(c):
        return copy(6, c, send_f, got_f.at[lax.rem(c, 2)], core_peer)

    def cross_copy_f(c):
        return copy(7, c, half_f.at[1 - side], cross_f.at[lax.rem(c, 2)], side_peer)

    group = lax.shift_right_logical(lax.broadcasted_iota(jnp.int32, latent_image.shape, 0), 3)
    latent_image[...] = image_of(counts, group)
    quarter = tokens.shape[1]

    def mask_of(c, start):
        image = latent_image[pl.ds(start, block), :]
        image = jnp.concatenate([image, image], axis=1)
        lane = lax.broadcasted_iota(jnp.int32, (1, 4 * SUB), 1)
        part = lax.shift_right_logical(lane, 6)
        part = 2 * lax.rem(part, 2) + part // 2
        row = part * quarter + c * SUB
        group = tok * (4 * quarter // GROUP) + lax.shift_right_logical(row, 8)
        return jnp.where(image == image_of(counts, group), 0.0, MASKED)

    def each_block(body, carry):
        if blocks == 1:
            return body(0, carry)
        return lax.fori_loop(0, blocks, lambda b, kept: body(b * block, kept), carry)

    def halve(wide, own, send):
        wide_s[...] = wide.reshape(wide_s.shape)
        own[...] = wide_s[core]
        send[...] = wide_s[other].astype(jnp.bfloat16)

    acc_in[...] = jnp.zeros_like(acc_in)
    acc_out[...] = jnp.zeros_like(acc_out)
    acc_write[...] = jnp.zeros_like(acc_write)
    grad_key[...] = jnp.zeros_like(grad_key)
    grad_value[...] = jnp.zeros_like(grad_value)

    def write_forward(c):
        query = query_t[c]

        def body(start, carry):
            here = pl.ds(start, block)
            bias = mask_of(c, start)
            kept = []
            for h in range(heads):
                scores = nn(key[h, here, :], query[head_rows(h)])
                weights = jnp.exp2(scores * (SCALE * LOG2E) + bias)
                total = jnp.sum(weights, axis=0, keepdims=True)
                mixed = nn(value_t[head_rows(h), here], weights.astype(jnp.bfloat16))
                kept.append((carry[h][0] + total, carry[h][1] + mixed))
            return tuple(kept)

        zero = (jnp.zeros((1, query.shape[1]), jnp.float32), jnp.zeros((HD, query.shape[1]), jnp.float32))
        totals = each_block(body, (zero,) * heads)
        mixed = jnp.concatenate([part / total for total, part in totals], axis=0)
        mixed = mixed.astype(jnp.bfloat16)
        mixed_t[c] = mixed
        for h in range(heads):
            log_total[c, h : h + 1] = -jnp.log2(totals[h][0])
        halve(tn(mixed, write_out[...]), own_a, send_a)
        core_a(c).start()

    def finish_update(c):
        cross_copy_a(c).wait()
        mine = half_a[...].astype(jnp.float32) + cross_a[lax.rem(c, 2)].astype(jnp.float32)
        update[c, core] = mine.astype(jnp.bfloat16)
        core_u(c).start()

    def cross_update(c):
        core_a(c).wait()
        half_a[...] = (own_a[...] + got_a[lax.rem(c, 2)].astype(jnp.float32)).astype(jnp.bfloat16)
        cross_copy_a(c).start()

    def one_rows(c):
        moved = update[c].reshape(4 * SUB, width).astype(jnp.float32)
        return chunk_rows(tokens, c).astype(jnp.float32) + moved

    def feed_forward(c):
        core_u(c).wait()
        normed, unused = norm_parts(one_rows(c))
        normed = normed.astype(jnp.bfloat16)
        normed_s[...] = normed
        inner = nn(normed, mlp_in[...])
        square = inner * inner
        tanh = jnp.tanh(GELU_A * inner * (1.0 + GELU_B * square))
        half = 0.5 + 0.5 * tanh
        active = (inner * half).astype(jnp.bfloat16)
        act_s[...] = active
        slope = half + 0.5 * GELU_A * inner * (1.0 - tanh * tanh) * (1.0 + 3.0 * GELU_B * square)
        grad_inner = (nt(chunk_rows(cotangent, c), mlp_out[...]) * slope).astype(jnp.bfloat16)
        inner_s[...] = grad_inner
        halve(nt(grad_inner, mlp_in[...]), own_d, send_d)
        core_d(c).start()
        halve(nn(active, mlp_out[...]), own_f, send_f)
        core_f(c).start()

    def finish_grad(c):
        slot = lax.rem(c, 2)
        cross_copy_d(c).wait()
        mine = half_d[...].astype(jnp.float32) + cross_d[slot].astype(jnp.float32)
        summed_d[slot, core] = mine.astype(jnp.bfloat16)
        core_s(c).start()
        cross_copy_f(c).wait()
        part = pl.ds(pl.multiple_of(c * SUB, SUB), SUB)
        moved = update[c].reshape(2, 2, SUB, width)
        mine = jnp.where(core == 0, moved[0], moved[1])
        mine = jnp.where(side == 0, mine[0], mine[1]).astype(jnp.float32)
        total = tokens[head, part, :].astype(jnp.float32) + mine + half_f[side].astype(jnp.float32)
        layer_out[part, :] = (total + cross_f[slot].astype(jnp.float32)).astype(jnp.bfloat16)

    def cross_grad(c):
        slot = lax.rem(c, 2)
        core_d(c).wait()
        half_d[...] = (own_d[...] + got_d[slot].astype(jnp.float32)).astype(jnp.bfloat16)
        cross_copy_d(c).start()
        core_f(c).wait()
        total = own_f[...] + got_f[slot].astype(jnp.float32)
        half_f[...] = total.astype(jnp.bfloat16).reshape(half_f.shape)
        cross_copy_f(c).start()

    def weight_grads(c):
        acc_in[...] += tn(normed_s[...], inner_s[...])
        acc_out[...] += tn(chunk_rows(cotangent, c), act_s[...])

    def write_backward(c):
        core_s(c).wait()
        normed, scale = norm_parts(one_rows(c))
        grad = summed_d[lax.rem(c, 2)].reshape(4 * SUB, width).astype(jnp.float32)
        wide = chunk_rows(cotangent, c).astype(jnp.float32) + norm_vjp(normed, scale, grad)
        wide_s[...] = wide.reshape(wide_s.shape)
        part = pl.ds(pl.multiple_of(c * SUB, SUB), SUB)
        mine = pl.ds(pl.multiple_of(side * SUB, SUB), SUB)
        grad_one[part, :] = wide_s[core, mine, :]
        narrow = wide.astype(jnp.bfloat16)
        mixed = mixed_t[c]
        acc_write[...] += nn(mixed, narrow)
        grad_mixed = nt(write_out[...], narrow).astype(jnp.bfloat16)
        query = query_t[c]
        product = grad_mixed.astype(jnp.float32) * mixed.astype(jnp.float32)

        def body(start, carry):
            here = pl.ds(start, block)
            bias = mask_of(c, start)
            kept = []
            for h in range(heads):
                rows = head_rows(h)
                scores = nn(key[h, here, :], query[rows])
                weights = jnp.exp2(scores * (SCALE * LOG2E) + (bias + log_total[c, h : h + 1]))
                grad_weights = nn(value[h, here, :], grad_mixed[rows])
                delta = jnp.sum(product[rows], axis=0, keepdims=True)
                grad_scores = (weights * (grad_weights - delta)).astype(jnp.bfloat16)
                grad_key[h, here, :] += nt(grad_scores, query[rows])
                grad_value[h, here, :] += nt(weights.astype(jnp.bfloat16), grad_mixed[rows])
                kept.append(carry[h] + nn(key_t[rows, here], grad_scores))
            return tuple(kept)

        zero = jnp.zeros((HD, query.shape[1]), jnp.float32)
        grads = each_block(body, (zero,) * heads)
        grad_query_t[c] = (jnp.concatenate(grads, axis=0) * SCALE).astype(jnp.bfloat16)

    def step(i, carry):
        @pl.when(i < chunks)
        def _():
            write_forward(i)

        @pl.when(jnp.logical_and(i >= 1, i <= chunks))
        def _():
            finish_update(i - 1)

        @pl.when(i < chunks)
        def _():
            cross_update(i)

        @pl.when(jnp.logical_and(i >= 1, i <= chunks))
        def _():
            feed_forward(i - 1)

        @pl.when(i >= 2)
        def _():
            finish_grad(i - 2)

        @pl.when(jnp.logical_and(i >= 1, i <= chunks))
        def _():
            cross_grad(i - 1)
            weight_grads(i - 1)

        @pl.when(i >= 2)
        def _():
            write_backward(i - 2)

        return carry

    lax.fori_loop(0, chunks + 2, step, 0)
    owned = grad_pairs.shape[2]

    def pack(b, carry):
        here = pl.ds(pl.multiple_of(b * block, block), block)
        there = pl.ds(b * (block // owned), block // owned)
        shape = (block // owned, owned, heads * HD)
        keys = jnp.concatenate([grad_key[h, here, :] for h in range(heads)], axis=1)
        values = jnp.concatenate([grad_value[h, here, :] for h in range(heads)], axis=1)
        grad_pairs[there, 0] = (keys * SCALE).astype(jnp.bfloat16).reshape(shape)
        grad_pairs[there, 1] = values.astype(jnp.bfloat16).reshape(shape)
        return carry

    lax.fori_loop(0, blocks, pack, 0)
    grad_mlp_in[...] = acc_in[...].astype(jnp.bfloat16)
    grad_mlp_out[...] = acc_out[...].astype(jnp.bfloat16)
    grad_write_out[...] = acc_write[...].T.astype(jnp.bfloat16)


def middle(counts, tokens, cotangent, query_t, key, value, key_t, value_t, write_out, mlp_in, mlp_out, tok_count):
    rows, width = tokens.shape
    column = write_out.shape[0]
    hidden = mlp_in.shape[1]
    heads = column // HD
    latents = key.shape[1]
    owned = latents // tok_count
    quarter = rows // 4
    chunks = quarter // SUB
    size = 4 * SUB
    half = (2 * SUB, width)
    low, wide = jnp.bfloat16, jnp.float32
    vmem = pl.BlockSpec(memory_space=pltpu.VMEM)
    exchange = [
        pltpu.VMEM(half, wide),
        pltpu.VMEM(half, low),
        pltpu.VMEM((2, *half), low),
        pltpu.VMEM(half, low),
        pltpu.VMEM((2, *half), low),
    ]
    return pl.pallas_call(
        middle_kernel,
        out_shape=[
            jax.ShapeDtypeStruct((quarter, width), low),
            jax.ShapeDtypeStruct((quarter, width), wide),
            jax.ShapeDtypeStruct((chunks, column, size), low),
            jax.ShapeDtypeStruct((tok_count, 2, owned, column), low),
            jax.ShapeDtypeStruct((width, hidden), low),
            jax.ShapeDtypeStruct((width, hidden), low),
            jax.ShapeDtypeStruct((width, column), low),
        ],
        in_specs=[pl.BlockSpec(memory_space=pltpu.SMEM)] + [vmem] * 10,
        out_specs=[vmem] * 7,
        scratch_shapes=[
            pltpu.VMEM((chunks, 2, *half), low),
            pltpu.VMEM((chunks, column, size), low),
            pltpu.VMEM((chunks, 8, size), wide),
            *exchange,
            *exchange,
            pltpu.VMEM((2, 2, *half), low),
            pltpu.VMEM(half, wide),
            pltpu.VMEM(half, low),
            pltpu.VMEM((2, *half), low),
            pltpu.VMEM((2, SUB, width), low),
            pltpu.VMEM((2, SUB, width), low),
            pltpu.VMEM((width, hidden), wide),
            pltpu.VMEM((width, hidden), wide),
            pltpu.VMEM((column, width), wide),
            pltpu.VMEM((size, width), low),
            pltpu.VMEM((size, hidden), low),
            pltpu.VMEM((size, hidden), low),
            pltpu.VMEM((2, *half), wide),
            pltpu.VMEM((latents, 128), jnp.int32),
            pltpu.VMEM((heads, latents, HD), wide),
            pltpu.VMEM((heads, latents, HD), wide),
            pltpu.SemaphoreType.DMA((8, 2)),
            pltpu.SemaphoreType.DMA((8, 2)),
        ],
        compiler_params=pltpu.CompilerParams(
            collective_id=1, has_side_effects=True, vmem_limit_bytes=62 << 20
        ),
        name="middle",
    )(
        counts,
        tokens.reshape(4, quarter, width),
        cotangent.reshape(4, quarter, width),
        query_t,
        key,
        value,
        key_t,
        value_t,
        write_out,
        mlp_in,
        mlp_out,
    )


def back_kernel(
    counts, tokens, latents, grad_one, lat_one, mixed_in, read_key, read_value, read_key_t, own_key, own_value,
    own_key_t, query_t, grad_query_t, grad_pairs, parts_in, parts_out, grad_write, rquery, rkey, rvalue, rout,
    wquery, wkey, wvalue,
    input_grad, latent_grad, out_in, out_out, out_early, out_late, out_query,
    got_pairs, head_parts, output_all, output_t, rows_s, acc_query, acc_read, grad_own, query_sum, query_send,
    query_got, own_f, send_f, got_f, half_f, cross_f, wide_s, lat_parts, lat_got,
    in_one, in_sums, in_two, in_sems, out_one, out_sums, out_two, out_sems,
    parts_early, early_one, early_sums, early_two, early_sems,
    parts_late, late_one, late_sums, late_two, late_sems,
    parts_query, q_one, q_sums, q_two, q_sems,
    pair_sems, head_sems, output_sems, query_sems, lat_sems, send_sems, recv_sems,
):
    tok_count, owned, column = query_got.shape
    head_count = head_parts.shape[0]
    chunks = read_key.shape[0]
    heads = column // HD
    quarter, width = tokens.shape[1], tokens.shape[2]
    groups_here = 4 * quarter // GROUP
    latent_count = tok_count * owned
    block = min(512, latent_count)
    blocks, per = latent_count // block, block // owned
    tok, head = lax.axis_index("tok"), lax.axis_index("head")
    core, side = lax.rem(head, 2), head // 2
    other = 1 - core
    low, wide = jnp.bfloat16, jnp.float32
    greet_all(tok, head, tok_count, head_count)
    pairs = Spread("tok", tok, head, tok_count, lambda peer: grad_pairs.at[peer], got_pairs, pair_sems)
    pairs.start()
    by_in = Scatter(tok, head, parts_in, in_one, in_sums, in_two, in_sems)
    by_out = Scatter(tok, head, parts_out, out_one, out_sums, out_two, out_sems)
    by_in.start()
    by_out.start()
    early = Scatter(tok, head, parts_early, early_one, early_sums, early_two, early_sems)
    late = Scatter(tok, head, parts_late, late_one, late_sums, late_two, late_sems)
    final = Scatter(tok, head, parts_query, q_one, q_sums, q_two, q_sems)

    def put_parts(ref, at, value):
        share = value.shape[0] // tok_count
        for b in range(tok_count):
            ref[b // 2, b % 2, :, at : at + value.shape[1]] = value[b * share : (b + 1) * share].astype(low)

    def normed_chunk(c):
        return norm_parts(chunk_rows(tokens, c).astype(wide))[0].astype(low)

    acc_query[...] = jnp.zeros_like(acc_query)

    def query_weights(c, carry):
        acc_query[...] += tn(normed_chunk(c), grad_query_t[c].T)
        return carry

    lax.fori_loop(0, chunks, query_weights, 0)
    put_parts(parts_early, 0, acc_query[...])
    put_parts(parts_early, column, grad_write[...])
    pairs.wait()
    got_pairs[tok] = grad_pairs[tok]
    summed = lax.fori_loop(
        1, tok_count, lambda s, kept: kept + got_pairs[s].astype(wide), got_pairs[0].astype(wide)
    )
    grad_key, grad_value = summed[0].astype(low), summed[1].astype(low)
    head_parts[head] = (nt(grad_key, wkey[...]) + nt(grad_value, wvalue[...])).astype(low)
    moved = Spread("head", tok, head, head_count, lambda peer: head_parts.at[head], head_parts, head_sems)
    moved.start()
    normed_one, scale_one = norm_parts(lat_one[...])
    narrow_one = normed_one.astype(low)
    put_parts(parts_early, 2 * column, tn(narrow_one, grad_key))
    put_parts(parts_early, 3 * column, tn(narrow_one, grad_value))
    moved.wait()
    grad = head_parts[0].astype(wide)
    for s in range(1, head_count):
        grad = grad + head_parts[s].astype(wide)
    grad_lat_one = norm_vjp(normed_one, scale_one, grad)
    grad_own[...] = grad_lat_one
    narrow = grad_lat_one.astype(low)
    grad_mixed = nt(narrow, rout[...]).astype(low)
    mixed = mixed_in[:, :column]
    product = grad_mixed.astype(wide) * mixed
    extra = []
    for h in range(heads):
        delta = jnp.sum(product[:, head_rows(h)], axis=1, keepdims=True)
        logs = mixed_in[:, column + h : column + h + 1]
        for k, (first, second) in enumerate(zip(split_three(delta), split_three(logs), strict=True)):
            extra.append((3 * h + k, first))
            extra.append((3 * (heads + h) + k, second))
    output_all[tok, :, :column] = grad_mixed
    output_all[tok, :, column:] = pick_lanes((owned, output_all.shape[2] - column), extra).astype(low)
    outputs = Spread("tok", tok, head, tok_count, lambda peer: output_all.at[tok], output_all, output_sems)
    outputs.start()
    put_parts(parts_early, 4 * column, tn(narrow, mixed.astype(low)))
    early.start()
    acc_read[...] = jnp.zeros_like(acc_read)
    query_sum[...] = jnp.zeros_like(query_sum)
    by_in.forward_all()
    outputs.wait()

    def turn(b, carry):
        here = pl.ds(pl.multiple_of(b * block, block), block)
        turned = output_all[pl.ds(b * per, per)].reshape(block, output_all.shape[2]).astype(wide).T
        output_t[:, here] = turned[:column].astype(low)
        for h in range(2 * heads):
            at = column + 3 * h
            rows_s[h : h + 1, here] = turned[at : at + 1] + turned[at + 1 : at + 2] + turned[at + 2 : at + 3]
        return carry

    lax.fori_loop(0, blocks, turn, 0)

    def read_back(keys, values, keys_t, rows_for, here, h):
        hr = head_rows(h)
        query, output = query_t[hr, here], output_t[hr, here]
        scores = nn(keys, query)
        weights = jnp.exp2(add_rows(scores * (SCALE * LOG2E), rows_for(h)))
        grad_weights = nn(values, output)
        grad_scores = (weights * (grad_weights - rows_s[h : h + 1, here])).astype(low)
        query_sum[hr, here] += nn(keys_t, grad_scores)
        return nt(grad_scores, query), nt(weights.astype(low), output)

    def each_block(body, carry):
        if blocks == 1:
            return body(0, carry)
        return lax.fori_loop(0, blocks, body, carry)

    def key_grads(count, key_of, value_of, key_t_of, images):
        def body(b, carry):
            start = b * block
            here = pl.ds(start, block)
            row_image = latent_row_image(counts, start, block)

            def rows_for(h):
                logs = rows_s[heads + h : heads + h + 1, here]
                return [jnp.where(row_image == image, logs, MASKED) for image in images]

            kept = []
            for h in range(heads):
                dk, dv = read_back(key_of(h), value_of(h), key_t_of(h), rows_for, here, h)
                kept.append((carry[h][0] + dk, carry[h][1] + dv))
            return tuple(kept)

        zero = jnp.zeros((count, HD), wide)
        grads = each_block(body, ((zero, zero),) * heads)
        keys = jnp.concatenate([grads[h][0] for h in range(heads)], axis=1) * SCALE
        values = jnp.concatenate([grads[h][1] for h in range(heads)], axis=1)
        return keys.astype(low), values.astype(low)

    own_images = [image_of(counts, tok * groups_here + g) for g in range(owned // LPG)]
    own_dk, own_dv = key_grads(
        owned, lambda h: own_key[h], lambda h: own_value[h], lambda h: own_key_t[head_rows(h), :], own_images
    )

    def copy(kind, chunk, source, target, peer):
        slot = lax.rem(chunk, 2)
        return pltpu.make_async_remote_copy(
            src_ref=source,
            dst_ref=target,
            send_sem=send_sems.at[kind, slot],
            recv_sem=recv_sems.at[kind, slot],
            device_id=(tok, peer),
            device_id_type=MESH,
        )

    def core_copy(c):
        return copy(0, c, send_f, got_f.at[lax.rem(c, 2)], side * 2 + other)

    def cross_copy(c):
        return copy(1, c, half_f.at[1 - side], cross_f.at[lax.rem(c, 2)], (1 - side) * 2 + core)

    def compute(c):
        images = [
            image_of(counts, tok * groups_here + (q * quarter + c * SUB) // GROUP) for q in (0, 2, 1, 3)
        ]
        dk, dv = key_grads(
            4 * SUB,
            lambda h: read_key[c, h],
            lambda h: read_value[c, h],
            lambda h: read_key_t[c, head_rows(h), :],
            images,
        )
        moved = nt(dk, rkey[...]) + nt(dv, rvalue[...]) + tn(grad_query_t[c], wquery_t_of(wquery))
        wide_s[...] = moved.reshape(wide_s.shape)
        own_f[...] = wide_s[core]
        send_f[...] = wide_s[other].astype(low)
        core_copy(c).start()
        normed = normed_chunk(c)
        acc_read[0] += tn(normed, dk)
        acc_read[1] += tn(normed, dv)

    def wquery_t_of(ref):
        return ref[...].T

    def cross(c):
        core_copy(c).wait()
        total = own_f[...] + got_f[lax.rem(c, 2)].astype(wide)
        half_f[...] = total.astype(low).reshape(half_f.shape)
        cross_copy(c).start()

    def finish(c):
        cross_copy(c).wait()
        part = pl.ds(pl.multiple_of(c * SUB, SUB), SUB)
        total = half_f[side].astype(wide) + cross_f[lax.rem(c, 2)].astype(wide)
        normed, scale = norm_parts(tokens[head, part, :].astype(wide))
        input_grad[part, :] = grad_one[part, :] + norm_vjp(normed, scale, total)

    def step(c, carry):
        @pl.when(c >= 1)
        def _():
            @pl.when(c >= 2)
            def _():
                finish(c - 2)

            cross(c - 1)

        @pl.when(c < chunks)
        def _():
            compute(c)

        return carry

    half_way = chunks // 2
    lax.fori_loop(0, half_way, step, 0)
    by_out.forward_all()
    lax.fori_loop(half_way, chunks, step, 0)
    early.forward_all()

    def turn_query(b, carry):
        here = pl.ds(pl.multiple_of(b * block, block), block)
        turned = (query_sum[:, here] * SCALE).T.astype(low)
        query_send[pl.ds(b * per, per)] = turned.reshape(per, owned, column)
        return carry

    lax.fori_loop(0, blocks, turn_query, 0)
    queries = Spread("tok", tok, head, tok_count, lambda peer: query_send.at[peer], query_got, query_sems)
    queries.start()
    normed_lat, scale_lat = norm_parts(latents[...].astype(wide))
    narrow_lat = normed_lat.astype(low)
    put_parts(parts_late, 0, acc_read[0] + tn(narrow_lat, own_dk))
    put_parts(parts_late, column, acc_read[1] + tn(narrow_lat, own_dv))
    late.start()
    step(chunks, 0)
    queries.wait()
    query_got[tok] = query_send[tok]
    summed = lax.fori_loop(
        1, tok_count, lambda s, kept: kept + query_got[s].astype(wide), query_got[0].astype(wide)
    )
    grad_query = summed.astype(low)
    lat_total = nt(grad_query, rquery[...]) + nt(own_dk, rkey[...]) + nt(own_dv, rvalue[...])
    lat_parts[...] = lat_total.astype(low).reshape(lat_parts.shape)
    lats = Spread("head", tok, head, head_count, lambda peer: lat_parts.at[peer], lat_got, lat_sems)
    lats.start()
    put_parts(parts_query, 0, tn(narrow_lat, grad_query))
    final.start()
    late.forward_all()
    finish(chunks - 1)
    out_in[...] = by_in.finish()
    final.forward_all()
    lats.wait()
    lat_got[head] = lat_parts[head]
    total = lat_got[0].astype(wide)
    for s in range(1, head_count):
        total = total + lat_got[s].astype(wide)
    share = owned // head_count
    mine = pl.ds(pl.multiple_of(head * share, share), share)
    normed, scale = norm_parts(latents[mine, :].astype(wide))
    latent_grad[...] = grad_own[mine, :] + norm_vjp(normed, scale, total)
    out_out[...] = by_out.finish()
    out_early[...] = early.finish()
    out_late[...] = late.finish()
    out_query[...] = final.finish()


def back(
    counts, tokens, latents, grad_one, lat_one, mixed, read_key, read_value, read_key_t, own_key, own_value,
    own_key_t, query_t, grad_query_t, grad_pairs, grad_in, grad_out, grad_write, rquery, rkey, rvalue, rout,
    wquery, wkey, wvalue, tok_count, head_count,
):
    rows, width = tokens.shape
    owned, column = latents.shape[0], rquery.shape[1]
    hidden = grad_in.shape[1]
    quarter = rows // 4
    chunks, size = quarter // SUB, 4 * SUB
    latent_count = owned * tok_count
    outer, share = tok_count // 2, width // tok_count
    low, wide = jnp.bfloat16, jnp.float32
    vmem = pl.BlockSpec(memory_space=pltpu.VMEM)
    packed = 256
    half = (2 * SUB, width)

    def with_parts(columns):
        return [pltpu.VMEM((outer, 2, share, columns), low)] + scatter_scratch(outer, share, columns)

    return pl.pallas_call(
        back_kernel,
        out_shape=[
            jax.ShapeDtypeStruct((quarter, width), wide),
            jax.ShapeDtypeStruct((owned // head_count, width), wide),
            jax.ShapeDtypeStruct((share, hidden), wide),
            jax.ShapeDtypeStruct((share, hidden), wide),
            jax.ShapeDtypeStruct((share, 5 * column), wide),
            jax.ShapeDtypeStruct((share, 2 * column), wide),
            jax.ShapeDtypeStruct((share, column), wide),
        ],
        in_specs=[pl.BlockSpec(memory_space=pltpu.SMEM)] + [vmem] * 24,
        out_specs=[vmem] * 7,
        scratch_shapes=[
            pltpu.VMEM((tok_count, 2, owned, column), low),
            pltpu.VMEM((head_count, owned, width), low),
            pltpu.VMEM((tok_count, owned, packed), low),
            pltpu.VMEM((column, latent_count), low),
            pltpu.VMEM((8, latent_count), wide),
            pltpu.VMEM((width, column), wide),
            pltpu.VMEM((2, width, column), wide),
            pltpu.VMEM((owned, width), wide),
            pltpu.VMEM((column, latent_count), wide),
            pltpu.VMEM((tok_count, owned, column), low),
            pltpu.VMEM((tok_count, owned, column), low),
            pltpu.VMEM(half, wide),
            pltpu.VMEM(half, low),
            pltpu.VMEM((2, *half), low),
            pltpu.VMEM((2, SUB, width), low),
            pltpu.VMEM((2, SUB, width), low),
            pltpu.VMEM((2, *half), wide),
            pltpu.VMEM((head_count, owned // head_count, width), low),
            pltpu.VMEM((head_count, owned // head_count, width), low),
            *scatter_scratch(outer, share, hidden),
            *scatter_scratch(outer, share, hidden),
            *with_parts(5 * column),
            *with_parts(2 * column),
            *with_parts(column),
            pltpu.SemaphoreType.DMA((2, tok_count)),
            pltpu.SemaphoreType.DMA((2, head_count)),
            pltpu.SemaphoreType.DMA((2, tok_count)),
            pltpu.SemaphoreType.DMA((2, tok_count)),
            pltpu.SemaphoreType.DMA((2, head_count)),
            pltpu.SemaphoreType.DMA((2, 2)),
            pltpu.SemaphoreType.DMA((2, 2)),
        ],
        compiler_params=pltpu.CompilerParams(collective_id=3, has_side_effects=True, vmem_limit_bytes=62 << 20),
        name="back",
    )(
        counts, tokens.reshape(4, quarter, width), latents, grad_one, lat_one, mixed, read_key, read_value,
        read_key_t, own_key, own_value, own_key_t, query_t, grad_query_t, grad_pairs,
        grad_in.reshape(outer, 2, share, hidden), grad_out.reshape(outer, 2, share, hidden), grad_write,
        rquery, rkey, rvalue, rout, wquery, wkey, wvalue,
    )


def shards(
    tokens,
    latents,
    image_groups,
    read_query,
    read_key,
    read_value,
    read_out,
    write_query,
    write_key,
    write_value,
    write_out,
    mlp_in,
    mlp_out,
    cotangent,
):
    column = read_query.shape[1]
    tok_count = lax.axis_size("tok")
    head_count = lax.axis_size("head")
    (
        wquery_t, wkey, wvalue, wkey_t, wvalue_t, rkey, rvalue, rkey_t, own_key, own_value, own_key_t,
        rquery_t, lat_one, mixed,
    ) = front(
        image_groups, tokens, latents, read_query, read_key, read_value, read_out, write_query, write_key,
        write_value, tok_count, head_count,
    )
    layer_out, grad_one, grad_wquery_t, grad_pairs, grad_in, grad_out, grad_write = middle(
        image_groups, tokens, cotangent, wquery_t, wkey, wvalue, wkey_t, wvalue_t, write_out, mlp_in, mlp_out,
        tok_count,
    )
    input_grad, latent_grad, grad_mlp_in, grad_mlp_out, early, late, grad_read_query = back(
        image_groups, tokens, latents, grad_one, lat_one, mixed, rkey, rvalue, rkey_t, own_key, own_value,
        own_key_t, rquery_t, grad_wquery_t, grad_pairs, grad_in, grad_out, grad_write, read_query, read_key,
        read_value, read_out, write_query, write_key, write_value, tok_count, head_count,
    )

    def part(array, k):
        return array[:, k * column : (k + 1) * column]

    return (
        layer_out,
        input_grad,
        latent_grad,
        grad_read_query,
        part(late, 0),
        part(late, 1),
        part(early, 4).T,
        part(early, 0),
        part(early, 2),
        part(early, 3),
        part(early, 1).T,
        grad_mlp_in,
        grad_mlp_out.T,
    )
def solution(mesh):
    return jax.shard_map(
        shards,
        mesh=mesh,
        in_specs=(
            P("tok", None),
            P("tok", None),
            P(),
            P(None, "head"),
            P(None, "head"),
            P(None, "head"),
            P("head", None),
            P(None, "head"),
            P(None, "head"),
            P(None, "head"),
            P("head", None),
            P(None, "head"),
            P("head", None),
            P("tok", None),
        ),
        out_specs=(
            P(("tok", "head"), None),
            P(("tok", "head"), None),
            P(("tok", "head"), None),
            P("tok", "head"),
            P("tok", "head"),
            P("tok", "head"),
            P("head", "tok"),
            P("tok", "head"),
            P("tok", "head"),
            P("tok", "head"),
            P("head", "tok"),
            P("tok", "head"),
            P("head", "tok"),
        ),
        check_vma=False,
    )
```

```python
from functools import partial
from types import SimpleNamespace

import jax
import jax.numpy as jnp
from jax import lax
from jax.experimental import pallas as pl
from jax.experimental.pallas import tpu as pltpu
from jax.sharding import PartitionSpec as P

MESH = pl.DeviceIdType.MESH
HD = 64
GROUP = 256
LPG = 8
epsilon = 1e-05
SUB = 64
SCALE = 0.125
LOG2E = 1.4426950408889634
MASKED = -1e30
GELU_A = 0.7978845608028654
GELU_B = 0.044715


def nn(left, right):
    return lax.dot_general(left, right, (((1,), (0,)), ((), ())), preferred_element_type=jnp.float32)


def nt(left, right):
    return lax.dot_general(left, right, (((1,), (1,)), ((), ())), preferred_element_type=jnp.float32)


def tn(left, right):
    return lax.dot_general(left, right, (((0,), (0,)), ((), ())), preferred_element_type=jnp.float32)


def norm_parts(values):
    center = values - jnp.mean(values, axis=-1, keepdims=True)
    scale = lax.rsqrt(jnp.mean(center * center, axis=-1, keepdims=True) + epsilon)
    return center * scale, scale


def norm_vjp(normed, scale, grad):
    return scale * (
        grad
        - jnp.mean(grad, axis=-1, keepdims=True)
        - normed * jnp.mean(grad * normed, axis=-1, keepdims=True)
    )


def image_of(counts, group):
    bound = jnp.int32(0)
    image = jnp.zeros_like(group)
    for m in range(counts.shape[0]):
        bound = bound + counts[m]
        image = image + jnp.where(bound <= group, 1, 0)
    return image


def latent_row_image(counts, start, count):
    group = lax.shift_right_logical(lax.broadcasted_iota(jnp.int32, (1, count), 1) + start, 3)
    return image_of(counts, group)


def head_rows(h):
    return slice(h * HD, (h + 1) * HD)


def chunk_rows(ref, c):
    part = pl.ds(pl.multiple_of(c * SUB, SUB), SUB)
    return jnp.concatenate([ref[q, part, :] for q in (0, 2, 1, 3)], axis=0)


def greet_all(r, d):
    barrier = pltpu.get_barrier_semaphore()

    def greet(step, carry):
        peer = lax.rem(r.tok + step, d.tok_count)
        pl.semaphore_signal(barrier, inc=1, device_id=(peer, r.head), device_id_type=MESH)
        return carry

    lax.fori_loop(1, d.tok_count, greet, 0)
    for step in range(1, d.head_count):
        peer = lax.rem(r.head + step, d.head_count)
        pl.semaphore_signal(barrier, inc=1, device_id=(r.tok, peer), device_id_type=MESH)
    pl.semaphore_wait(barrier, d.tok_count + d.head_count - 2)


class Spread:
    def __init__(self, axis, tok, head, count, source, got, sems):
        self.axis, self.tok, self.head, self.count = axis, tok, head, count
        self.me = tok if axis == "tok" else head
        self.source, self.got, self.sems = source, got, sems

    def copy(self, peer, slot):
        return pltpu.make_async_remote_copy(
            src_ref=self.source(peer),
            dst_ref=self.got.at[slot],
            send_sem=self.sems.at[0, peer],
            recv_sem=self.sems.at[1, slot],
            device_id=(peer, self.head) if self.axis == "tok" else (self.tok, peer),
            device_id_type=MESH,
        )

    def start(self):
        def go(step, carry):
            self.copy(lax.rem(self.me + step, self.count), self.me).start()
            return carry

        lax.fori_loop(1, self.count, go, 0)

    def wait(self):
        def go(step, carry):
            peer = lax.rem(self.me + step, self.count)
            self.copy(peer, peer).wait()
            return carry

        lax.fori_loop(1, self.count, go, 0)


class Scatter:
    def __init__(self, r, parts, got_one, got_two, sems):
        self.head, self.mine, self.side = r.head, r.tok // 2, lax.rem(r.tok, 2)
        self.parts, self.got_one, self.got_two, self.sems = parts, got_one, got_two, sems
        self.outer = parts.shape[0]

    def first(self, block):
        return pltpu.make_async_remote_copy(
            src_ref=self.parts.at[block, 1 - self.side],
            dst_ref=self.got_one.at[block],
            send_sem=self.sems.at[0, block],
            recv_sem=self.sems.at[1, block],
            device_id=(self.mine * 2 + (1 - self.side), self.head),
            device_id_type=MESH,
        )

    def second(self, block, source):
        return pltpu.make_async_remote_copy(
            src_ref=self.got_one.at[block],
            dst_ref=self.got_two.at[source],
            send_sem=self.sems.at[2, block],
            recv_sem=self.sems.at[3, source],
            device_id=(block * 2 + self.side, self.head),
            device_id_type=MESH,
        )

    def start(self):
        def go(step, carry):
            self.first(lax.rem(self.mine + step, self.outer)).start()
            return carry

        lax.fori_loop(1, self.outer + 1, go, 0)

    def total(self, block):
        self.first(block).wait()
        both = self.parts[block, self.side].astype(jnp.float32) + self.got_one[block].astype(jnp.float32)
        return both.astype(jnp.bfloat16)

    def forward(self):
        def go(step, carry):
            block = lax.rem(self.mine + step, self.outer)
            self.got_one[block] = self.total(block)
            self.second(block, self.mine).start()
            return carry

        lax.fori_loop(1, self.outer, go, 0)

    def finish(self):
        self.got_two[self.mine] = self.total(self.mine)

        def go(step, carry):
            peer = lax.rem(self.mine + step, self.outer)
            self.second(peer, peer).wait()
            return carry

        lax.fori_loop(1, self.outer, go, 0)


def split_three(value):
    high = value.astype(jnp.bfloat16).astype(jnp.float32)
    rest = value - high
    middle_part = rest.astype(jnp.bfloat16).astype(jnp.float32)
    return high, middle_part, rest - middle_part


def pick_lanes(shape, columns):
    lane = lax.broadcasted_iota(jnp.int32, shape, 1)
    value = jnp.zeros(shape, jnp.float32)
    for at, column in columns:
        value = jnp.where(lane == at, column, value)
    return value


def by_head(shape, columns):
    lane = lax.broadcasted_iota(jnp.int32, shape, 1)
    value = jnp.broadcast_to(columns[-1], shape)
    for h in range(len(columns) - 2, -1, -1):
        value = jnp.where(lane < (h + 1) * HD, columns[h], value)
    return value


def chunk_bias(counts, tok, groups_here, c, quarter, row_image, rows):
    kept = []
    for q in (0, 2, 1, 3):
        group = tok * groups_here + (q * quarter + c * SUB) // GROUP
        image = image_of(counts, group)
        kept.append([jnp.where(row_image == image, row, MASKED) for row in rows])
    return kept


def add_rows(values, rows):
    count = values.shape[0] // len(rows)
    return jnp.concatenate([values[k * count : (k + 1) * count] + row for k, row in enumerate(rows)], axis=0)


def token_images(r, d, c):
    return [
        image_of(r.counts, r.tok * d.groups_here + (q * d.quarter + c * SUB) // GROUP) for q in (0, 2, 1, 3)
    ]


def spread_of(r, d, axis, source, got, sems):
    count = d.tok_count if axis == "tok" else d.head_count
    return Spread(axis, r.tok, r.head, count, source, got, sems)


def sum_slots(ref, count):
    first = ref[0].astype(jnp.float32)
    return lax.fori_loop(1, count, lambda s, kept: kept + ref[s].astype(jnp.float32), first)


def each_block(d, body, carry):
    if d.blocks == 1:
        return body(0, carry)
    return lax.fori_loop(0, d.blocks, lambda b, kept: body(b, kept), carry)


def block_at(d, b):
    start = b * d.block if d.blocks == 1 else pl.multiple_of(b * d.block, d.block)
    return start, pl.ds(start, d.block)


def keep_heads(ref, wide, heads):
    for h in range(heads):
        ref[h] = wide[:, head_rows(h)]


def chunk_core_side(r):
    return lax.rem(r.head, 2), r.head // 2


def loads(r):
    pairs = (
        (r.write_out_hbm, r.write_out),
        (r.mlp_in_hbm, r.mlp_in),
        (r.mlp_out_hbm, r.mlp_out),
        (r.cotangent_hbm, r.cotangent),
    )
    return [pltpu.make_async_copy(source, target, r.load_sems.at[k]) for k, (source, target) in enumerate(pairs)]


def front_phase(r, d):
    low = jnp.bfloat16
    heads, column, chunks, owned = d.heads, d.column, d.chunks, d.owned
    latents_wide = r.latents[...].astype(jnp.float32)
    normed_lat = norm_parts(latents_wide)[0].astype(low)
    r.query_all[r.tok] = nt(normed_lat, r.rquery[...]).astype(low)
    greet_all(r, d)
    queries = spread_of(r, d, "tok", lambda peer: r.query_all.at[r.tok], r.query_all, r.query_sems)
    queries.start()
    keys = nt(normed_lat, r.rkey[...]).astype(low)
    values = nt(normed_lat, r.rvalue[...]).astype(low)
    keep_heads(r.own_key, keys, heads)
    keep_heads(r.own_value, values, heads)
    r.own_key_t[...] = keys.T
    r.own_value_t[...] = values.T

    def project(c, carry):
        normed = norm_parts(chunk_rows(r.tokens, c).astype(jnp.float32))[0].astype(low)
        r.update[c] = normed.reshape(r.update.shape[1:])
        keys = nt(normed, r.rkey[...]).astype(low)
        values = nt(normed, r.rvalue[...]).astype(low)
        keep_heads(r.read_key.at[c], keys, heads)
        keep_heads(r.read_value.at[c], values, heads)
        r.read_key_t[c] = keys.T
        r.read_value_t[c] = values.T
        return carry

    lax.fori_loop(0, chunks, project, 0)
    r.sums[...] = jnp.zeros_like(r.sums)
    queries.wait()

    def attend(scores, rows, values_t, here, h):
        weights = jnp.exp2(add_rows(scores * (SCALE * LOG2E), rows))
        r.sums[column + h : column + h + 1, here] += jnp.sum(weights, axis=0, keepdims=True)
        r.sums[head_rows(h), here] += nn(values_t, weights.astype(low))

    def read_block(b, carry):
        start, here = block_at(d, b)
        query = r.query_all[pl.ds(b * d.per, d.per)].reshape(d.block, column).T
        r.read_query_t[:, here] = query
        row_image = latent_row_image(r.counts, start, d.block)

        def masks(images):
            return [jnp.where(row_image == image, 0.0, MASKED) for image in images]

        def read_chunk(c, carry):
            rows = masks(token_images(r, d, c))
            for h in range(heads):
                attend(nn(r.read_key[c, h], query[head_rows(h)]), rows, r.read_value_t[c, head_rows(h)], here, h)
            return carry

        lax.fori_loop(0, chunks, read_chunk, 0)
        rows = masks([image_of(r.counts, r.tok * d.groups_here + g) for g in range(d.groups_here)])
        for h in range(heads):
            attend(nn(r.own_key[h], query[head_rows(h)]), rows, r.own_value_t[head_rows(h), :], here, h)
        total = r.sums[column : column + heads, here]
        high = total.astype(low).astype(jnp.float32)
        r.sums[column : column + heads, here] = high
        r.sums[column + heads : column + 2 * heads, here] = total - high
        r.sums_send[pl.ds(b * d.per, d.per)] = r.sums[:, here].T.astype(low).reshape(d.per, owned, d.packed)
        return carry

    each_block(d, read_block, 0)
    totals = spread_of(r, d, "tok", lambda peer: r.sums_send.at[peer], r.sums_got, r.sums_sems)
    totals.start()

    def project_query(c, carry):
        r.query_t[c] = nt(r.wquery[...], r.update[c].reshape(4 * SUB, d.width)).astype(low)
        return carry

    lax.fori_loop(0, chunks, project_query, 0)
    totals.wait()
    r.sums_got[r.tok] = r.sums_send[r.tok]
    summed = sum_slots(r.sums_got, d.tok_count)
    whole = [
        summed[:, column + h : column + h + 1] + summed[:, column + heads + h : column + heads + h + 1]
        for h in range(heads)
    ]
    mixed = summed[:, :column] / by_head((owned, column), whole)
    r.mixed[:, :column] = mixed
    r.mixed[:, column:] = pick_lanes(
        (owned, d.packed - column), [(h, -jnp.log2(whole[h])) for h in range(heads)]
    )
    r.head_parts[r.head] = nn(mixed.astype(low), r.rout[...]).astype(low)
    moved = spread_of(r, d, "head", lambda peer: r.head_parts.at[r.head], r.head_parts, r.head_sems)
    moved.start()
    moved.wait()
    latents_one = latents_wide
    for s in range(d.head_count):
        latents_one = latents_one + r.head_parts[s].astype(jnp.float32)
    r.lat_one[...] = latents_one
    normed_one = norm_parts(latents_one)[0].astype(low)
    r.pair_all[r.tok, :, :column] = nt(normed_one, r.wkey[...]).astype(low)
    r.pair_all[r.tok, :, column:] = nt(normed_one, r.wvalue[...]).astype(low)
    pairs = spread_of(r, d, "tok", lambda peer: r.pair_all.at[r.tok], r.pair_all, r.pair_sems)
    pairs.start()
    pairs.wait()

    def unpack(b, carry):
        start, here = block_at(d, b)
        wide = r.pair_all[pl.ds(b * d.per, d.per)].reshape(d.block, 2 * column)
        for h in range(heads):
            r.key[h, here, :] = wide[:, head_rows(h)]
            r.value[h, here, :] = wide[:, head_rows(heads + h)]
        turned = wide.T
        r.key_t[:, here] = turned[:column]
        r.value_t[:, here] = turned[column:]
        return carry

    each_block(d, unpack, 0)


def mlp_scatters(r):
    return (
        Scatter(r, r.parts_in, r.in_one, r.in_two, r.in_sems),
        Scatter(r, r.parts_out, r.out_one, r.out_two, r.out_sems),
    )


def cross_f(r, c):
    core, side = chunk_core_side(r)
    return pltpu.make_async_remote_copy(
        src_ref=r.f_half.at[c, 1 - side],
        dst_ref=r.f_cross.at[c],
        send_sem=r.f_sems.at[0, c],
        recv_sem=r.f_sems.at[1, c],
        device_id=(r.tok, (1 - side) * 2 + core),
        device_id_type=MESH,
    )


def middle_phase(r, d, merged):
    chunks, heads, width = d.chunks, d.heads, d.width
    core, side = chunk_core_side(r)
    other = 1 - core
    core_peer = (r.tok, side * 2 + other)
    side_peer = (r.tok, (1 - side) * 2 + core)
    for load in loads(r):
        load.wait()

    def copy(kind, chunk, source, target, peer):
        slot = lax.rem(chunk, 2)
        return pltpu.make_async_remote_copy(
            src_ref=source,
            dst_ref=target,
            send_sem=r.send_sems.at[kind, slot],
            recv_sem=r.recv_sems.at[kind, slot],
            device_id=peer,
            device_id_type=MESH,
        )

    def core_a(c):
        return copy(0, c, r.send_a, r.got_a.at[lax.rem(c, 2)], core_peer)

    def cross_copy_a(c):
        return copy(1, c, r.half_a, r.cross_a.at[lax.rem(c, 2)], side_peer)

    def core_u(c):
        return copy(2, c, r.update.at[c, core], r.update.at[c, core], core_peer)

    def core_d(c):
        return copy(3, c, r.send_d, r.got_d.at[lax.rem(c, 2)], core_peer)

    def cross_copy_d(c):
        return copy(4, c, r.half_d, r.cross_d.at[lax.rem(c, 2)], side_peer)

    def core_s(c):
        half = r.summed_d.at[lax.rem(c, 2), core]
        return copy(5, c, half, half, core_peer)

    def core_f(c):
        return copy(6, c, r.send_f, r.got_f.at[lax.rem(c, 2)], core_peer)

    group = lax.shift_right_logical(lax.broadcasted_iota(jnp.int32, r.latent_image.shape, 0), 3)
    r.latent_image[...] = image_of(r.counts, group)

    def mask_of(c, here):
        image = r.latent_image[here, :]
        image = jnp.concatenate([image, image], axis=1)
        lane = lax.broadcasted_iota(jnp.int32, (1, 4 * SUB), 1)
        part = lax.shift_right_logical(lane, 6)
        part = 2 * lax.rem(part, 2) + part // 2
        row = part * d.quarter + c * SUB
        group = r.tok * d.groups_here + lax.shift_right_logical(row, 8)
        return jnp.where(image == image_of(r.counts, group), 0.0, MASKED)

    def halve(wide, own, send):
        r.wide_s[...] = wide.reshape(r.wide_s.shape)
        own[...] = r.wide_s[core]
        send[...] = r.wide_s[other].astype(jnp.bfloat16)

    r.acc_in[...] = jnp.zeros_like(r.acc_in)
    r.acc_out[...] = jnp.zeros_like(r.acc_out)
    r.acc_write[...] = jnp.zeros_like(r.acc_write)
    r.grad_key[...] = jnp.zeros_like(r.grad_key)
    r.grad_value[...] = jnp.zeros_like(r.grad_value)

    def write_forward(c):
        query = r.query_t[c]

        def body(b, carry):
            here = block_at(d, b)[1]
            bias = mask_of(c, here)
            kept = []
            for h in range(heads):
                scores = nn(r.key[h, here, :], query[head_rows(h)])
                weights = jnp.exp2(scores * (SCALE * LOG2E) + bias)
                total = jnp.sum(weights, axis=0, keepdims=True)
                mixed = nn(r.value_t[head_rows(h), here], weights.astype(jnp.bfloat16))
                kept.append((carry[h][0] + total, carry[h][1] + mixed))
            return tuple(kept)

        size = 4 * SUB
        zero = (jnp.zeros((1, size), jnp.float32), jnp.zeros((HD, size), jnp.float32))
        totals = each_block(d, body, (zero,) * heads)
        mixed = jnp.concatenate([part / total for total, part in totals], axis=0)
        mixed = mixed.astype(jnp.bfloat16)
        r.mixed_t[c] = mixed
        for h in range(heads):
            r.log_total[c, h : h + 1] = -jnp.log2(totals[h][0])
        halve(tn(mixed, r.write_out[...]), r.own_a, r.send_a)
        core_a(c).start()

    def finish_update(c):
        cross_copy_a(c).wait()
        mine = r.half_a[...].astype(jnp.float32) + r.cross_a[lax.rem(c, 2)].astype(jnp.float32)
        r.update[c, core] = mine.astype(jnp.bfloat16)
        core_u(c).start()

    def cross_update(c):
        core_a(c).wait()
        r.half_a[...] = (r.own_a[...] + r.got_a[lax.rem(c, 2)].astype(jnp.float32)).astype(jnp.bfloat16)
        cross_copy_a(c).start()

    def one_rows(c):
        moved = r.update[c].reshape(4 * SUB, width).astype(jnp.float32)
        return chunk_rows(r.tokens, c).astype(jnp.float32) + moved

    def feed_forward(c):
        core_u(c).wait()
        normed = norm_parts(one_rows(c))[0].astype(jnp.bfloat16)
        r.normed_s[...] = normed
        inner = nn(normed, r.mlp_in[...])
        square = inner * inner
        tanh = jnp.tanh(GELU_A * inner * (1.0 + GELU_B * square))
        half = 0.5 + 0.5 * tanh
        active = (inner * half).astype(jnp.bfloat16)
        r.act_s[...] = active
        slope = half + 0.5 * GELU_A * inner * (1.0 - tanh * tanh) * (1.0 + 3.0 * GELU_B * square)
        grad_inner = (nt(chunk_rows(r.cotangent, c), r.mlp_out[...]) * slope).astype(jnp.bfloat16)
        r.inner_s[...] = grad_inner
        halve(nt(grad_inner, r.mlp_in[...]), r.own_d, r.send_d)
        core_d(c).start()
        halve(nn(active, r.mlp_out[...]), r.own_f, r.send_f)
        core_f(c).start()

    def finish_grad(c):
        slot = lax.rem(c, 2)
        cross_copy_d(c).wait()
        mine = r.half_d[...].astype(jnp.float32) + r.cross_d[slot].astype(jnp.float32)
        r.summed_d[slot, core] = mine.astype(jnp.bfloat16)
        core_s(c).start()

    def cross_grad(c):
        slot = lax.rem(c, 2)
        core_d(c).wait()
        r.half_d[...] = (r.own_d[...] + r.got_d[slot].astype(jnp.float32)).astype(jnp.bfloat16)
        cross_copy_d(c).start()

    def keep_forward(c):
        slot = lax.rem(c, 2)
        core_f(c).wait()
        total = (r.own_f[...] + r.got_f[slot].astype(jnp.float32)).reshape(2, SUB, width)
        r.f_half[c] = total.astype(jnp.bfloat16)
        part = pl.ds(pl.multiple_of(c * SUB, SUB), SUB)
        rows = pl.ds(pl.multiple_of(side * SUB, SUB), SUB)
        mine = jnp.where(side == 0, total[0], total[1]) + r.update[c, core, rows, :].astype(jnp.float32)
        r.f_half[c, side] = (mine + r.tokens[r.head, part, :].astype(jnp.float32)).astype(jnp.bfloat16)

    def weight_grads(c):
        r.acc_in[...] += tn(r.normed_s[...], r.inner_s[...])
        r.acc_out[...] += tn(chunk_rows(r.cotangent, c), r.act_s[...])

    def write_backward(c):
        core_s(c).wait()
        normed, scale = norm_parts(one_rows(c))
        grad = r.summed_d[lax.rem(c, 2)].reshape(4 * SUB, width).astype(jnp.float32)
        wide = chunk_rows(r.cotangent, c).astype(jnp.float32) + norm_vjp(normed, scale, grad)
        r.wide_s[...] = wide.reshape(r.wide_s.shape)
        part = pl.ds(pl.multiple_of(c * SUB, SUB), SUB)
        mine = pl.ds(pl.multiple_of(side * SUB, SUB), SUB)
        r.grad_one[part, :] = r.wide_s[core, mine, :]
        narrow = wide.astype(jnp.bfloat16)
        mixed = r.mixed_t[c]
        r.acc_write[...] += nn(mixed, narrow)
        grad_mixed = nt(r.write_out[...], narrow).astype(jnp.bfloat16)
        query = r.query_t[c]
        product = grad_mixed.astype(jnp.float32) * mixed.astype(jnp.float32)

        def body(b, carry):
            here = block_at(d, b)[1]
            bias = mask_of(c, here)
            kept = []
            for h in range(heads):
                rows = head_rows(h)
                scores = nn(r.key[h, here, :], query[rows])
                weights = jnp.exp2(scores * (SCALE * LOG2E) + (bias + r.log_total[c, h : h + 1]))
                grad_weights = nn(r.value[h, here, :], grad_mixed[rows])
                delta = jnp.sum(product[rows], axis=0, keepdims=True)
                grad_scores = (weights * (grad_weights - delta)).astype(jnp.bfloat16)
                r.grad_key[h, here, :] += nt(grad_scores, query[rows])
                r.grad_value[h, here, :] += nt(weights.astype(jnp.bfloat16), grad_mixed[rows])
                kept.append(carry[h] + nn(r.key_t[rows, here], grad_scores))
            return tuple(kept)

        zero = jnp.zeros((HD, 4 * SUB), jnp.float32)
        grads = each_block(d, body, (zero,) * heads)
        r.grad_query_t[c] = (jnp.concatenate(grads, axis=0) * SCALE).astype(jnp.bfloat16)

    def step(i, carry):
        @pl.when(i < chunks)
        def _():
            write_forward(i)

        @pl.when(jnp.logical_and(i >= 1, i <= chunks))
        def _():
            finish_update(i - 1)

        @pl.when(i < chunks)
        def _():
            cross_update(i)

        @pl.when(jnp.logical_and(i >= 1, i <= chunks))
        def _():
            feed_forward(i - 1)

        @pl.when(i >= 2)
        def _():
            finish_grad(i - 2)

        @pl.when(jnp.logical_and(i >= 1, i <= chunks))
        def _():
            cross_grad(i - 1)
            weight_grads(i - 1)
            keep_forward(i - 1)

        @pl.when(i >= 2)
        def _():
            write_backward(i - 2)

        return carry

    lax.fori_loop(0, chunks + 1, step, 0)
    put_parts(d, r.parts_in, 0, r.acc_in)
    put_parts(d, r.parts_out, 0, r.acc_out)
    if merged:
        mlp_scatters(r)[0].start()
    finish_grad(chunks - 1)
    if merged:
        for c in range(chunks):
            cross_f(r, c).start()
    write_backward(chunks - 1)

    def pack(b, carry):
        here = block_at(d, b)[1]
        there = pl.ds(b * d.per, d.per)
        both = [r.grad_key[h, here, :] * SCALE for h in range(heads)]
        both += [r.grad_value[h, here, :] for h in range(heads)]
        wide = jnp.concatenate(both, axis=1).astype(jnp.bfloat16)
        r.grad_pairs[there] = wide.reshape(d.per, d.owned, 2 * d.column)
        return carry

    each_block(d, pack, 0)
    r.grad_write[...] = r.acc_write[...].T.astype(jnp.bfloat16)


def put_parts(d, ref, at, value):
    width = value.shape[1]
    for b in range(d.tok_count):
        rows = slice(b * d.share, (b + 1) * d.share)
        ref[b // 2, b % 2, :, at : at + width] = value[rows, :].astype(jnp.bfloat16)


def back_phase(r, d, merged):
    chunks, heads, width, column, owned = d.chunks, d.heads, d.width, d.column, d.owned
    low, wide = jnp.bfloat16, jnp.float32
    core, side = chunk_core_side(r)
    other = 1 - core
    pairs = spread_of(r, d, "tok", lambda peer: r.grad_pairs.at[peer], r.got_pairs, r.pairs_sems)
    pairs.start()
    by_in, by_out = mlp_scatters(r)
    early = Scatter(r, r.parts_early, r.early_one, r.early_two, r.early_sems)
    late = Scatter(r, r.parts_late, r.late_one, r.late_two, r.late_sems)
    final = Scatter(r, r.parts_final, r.final_one, r.final_two, r.final_sems)
    if not merged:
        by_in.start()
        for c in range(chunks):
            cross_f(r, c).start()
    r.acc_in[...] = jnp.zeros_like(r.acc_in)
    r.acc_out[...] = jnp.zeros_like(r.acc_out)
    at_key, at_value = slice(0, column), slice(256, 256 + column)

    def query_weights(c, carry):
        normed = norm_parts(chunk_rows(r.tokens, c).astype(wide))[0].astype(low)
        r.update[c] = normed.reshape(r.update.shape[1:])
        r.acc_in[:, :column] += tn(normed, r.grad_query_t[c].T)
        return carry

    lax.fori_loop(0, chunks, query_weights, 0)
    put_parts(d, r.parts_early, 0, r.acc_in[:, :column])
    put_parts(d, r.parts_early, column, r.grad_write)
    pairs.wait()
    by_out.start()
    by_in.forward()
    r.got_pairs[r.tok] = r.grad_pairs[r.tok]
    summed = sum_slots(r.got_pairs, d.tok_count).astype(low)
    grad_key, grad_value = summed[:, :column], summed[:, column:]
    r.head_parts[r.head] = (nn(grad_key, r.wkey[...]) + nn(grad_value, r.wvalue[...])).astype(low)
    moved = spread_of(r, d, "head", lambda peer: r.head_parts.at[r.head], r.head_parts, r.heads_sems)
    moved.start()
    normed_one, scale_one = norm_parts(r.lat_one[...])
    put_parts(d, r.parts_early, 2 * column, tn(normed_one.astype(low), summed))
    moved.wait()
    grad_lat_one = norm_vjp(normed_one, scale_one, sum_slots(r.head_parts, d.head_count))
    r.grad_own[...] = grad_lat_one
    narrow = grad_lat_one.astype(low)
    grad_mixed = nt(narrow, r.rout[...]).astype(low)
    mixed = r.mixed[:, :column]
    product = grad_mixed.astype(wide) * mixed
    extra = []
    for h in range(heads):
        delta = jnp.sum(product[:, head_rows(h)], axis=1, keepdims=True)
        logs = r.mixed[:, column + h : column + h + 1]
        for k, (first, second) in enumerate(zip(split_three(delta), split_three(logs), strict=True)):
            extra.append((3 * h + k, first))
            extra.append((3 * (heads + h) + k, second))
    r.output_all[r.tok, :, :column] = grad_mixed
    r.output_all[r.tok, :, column:] = pick_lanes((owned, d.packed - column), extra).astype(low)
    outputs = spread_of(r, d, "tok", lambda peer: r.output_all.at[r.tok], r.output_all, r.output_sems)
    outputs.start()
    put_parts(d, r.parts_early, 4 * column, tn(narrow, mixed.astype(low)))
    r.query_sum[...] = jnp.zeros_like(r.query_sum)
    outputs.wait()
    early.start()
    by_out.forward()

    def turn(b, carry):
        here = block_at(d, b)[1]
        turned = r.output_all[pl.ds(b * d.per, d.per)].reshape(d.block, d.packed).astype(wide).T
        r.output_t[:, here] = turned[:column].astype(low)
        for h in range(2 * heads):
            at = column + 3 * h
            r.rows[h : h + 1, here] = turned[at : at + 1] + turned[at + 1 : at + 2] + turned[at + 2 : at + 3]
        return carry

    each_block(d, turn, 0)

    def key_grads(count, key_of, value_of, key_t_of, images):
        def body(b, carry):
            start, here = block_at(d, b)
            row_image = latent_row_image(r.counts, start, d.block)
            kept = []
            for h in range(heads):
                hr = head_rows(h)
                logs = r.rows[heads + h : heads + h + 1, here]
                rows = [jnp.where(row_image == image, logs, MASKED) for image in images]
                query, output = r.read_query_t[hr, here], r.output_t[hr, here]
                weights = jnp.exp2(add_rows(nn(key_of(h), query) * (SCALE * LOG2E), rows))
                grad_weights = nn(value_of(h), output)
                grad_scores = (weights * (grad_weights - r.rows[h : h + 1, here])).astype(low)
                r.query_sum[hr, here] += nn(key_t_of(h), grad_scores)
                kept.append(
                    (carry[h][0] + nt(grad_scores, query), carry[h][1] + nt(weights.astype(low), output))
                )
            return tuple(kept)

        zero = jnp.zeros((count, HD), wide)
        grads = each_block(d, body, ((zero, zero),) * heads)
        keys = jnp.concatenate([grads[h][0] for h in range(heads)], axis=1) * SCALE
        values = jnp.concatenate([grads[h][1] for h in range(heads)], axis=1)
        return keys.astype(low), values.astype(low)

    def core_copy(c):
        slot = lax.rem(c, 2)
        return pltpu.make_async_remote_copy(
            src_ref=r.send_f,
            dst_ref=r.got_f.at[slot],
            send_sem=r.core_sems.at[0, slot],
            recv_sem=r.core_sems.at[1, slot],
            device_id=(r.tok, side * 2 + other),
            device_id_type=MESH,
        )

    def cross_copy(c):
        return pltpu.make_async_remote_copy(
            src_ref=r.x_half.at[c, 1 - side],
            dst_ref=r.x_cross.at[c],
            send_sem=r.x_sems.at[0, c],
            recv_sem=r.x_sems.at[1, c],
            device_id=(r.tok, (1 - side) * 2 + core),
            device_id_type=MESH,
        )

    def compute(c):
        dk, dv = key_grads(
            4 * SUB,
            lambda h: r.read_key[c, h],
            lambda h: r.read_value[c, h],
            lambda h: r.read_key_t[c, head_rows(h), :],
            token_images(r, d, c),
        )
        moved = nn(dk, r.rkey[...]) + nn(dv, r.rvalue[...]) + tn(r.grad_query_t[c], r.wquery[...])
        r.wide_s[...] = moved.reshape(r.wide_s.shape)
        r.own_f[...] = r.wide_s[core]
        r.send_f[...] = r.wide_s[other].astype(low)
        core_copy(c).start()
        normed = r.update[c].reshape(4 * SUB, width)
        r.acc_out[:, at_key] += tn(normed, dk)
        r.acc_out[:, at_value] += tn(normed, dv)

    def cross(c):
        core_copy(c).wait()
        total = r.own_f[...] + r.got_f[lax.rem(c, 2)].astype(wide)
        r.x_half[c] = total.astype(low).reshape(2, SUB, width)
        cross_copy(c).start()

    def step(c, carry):
        @pl.when(c >= 1)
        def _():
            cross(c - 1)

        compute(c)
        return carry

    lax.fori_loop(0, chunks // 2, step, 0)
    early.forward()
    lax.fori_loop(chunks // 2, chunks, step, 0)
    own_dk, own_dv = key_grads(
        owned,
        lambda h: r.own_key[h],
        lambda h: r.own_value[h],
        lambda h: r.own_key_t[head_rows(h), :],
        [image_of(r.counts, r.tok * d.groups_here + g) for g in range(d.groups_here)],
    )

    def turn_query(b, carry):
        here = block_at(d, b)[1]
        turned = (r.query_sum[:, here] * SCALE).T.astype(low)
        r.query_send[pl.ds(b * d.per, d.per)] = turned.reshape(d.per, owned, column)
        return carry

    each_block(d, turn_query, 0)
    queries = spread_of(r, d, "tok", lambda peer: r.query_send.at[peer], r.query_got, r.back_query_sems)
    queries.start()
    cross(chunks - 1)
    normed_lat, scale_lat = norm_parts(r.latents[...].astype(wide))
    narrow_lat = normed_lat.astype(low)
    put_parts(d, r.parts_late, 0, r.acc_out[:, at_key] + tn(narrow_lat, own_dk))
    put_parts(d, r.parts_late, column, r.acc_out[:, at_value] + tn(narrow_lat, own_dv))
    late.start()
    queries.wait()
    r.query_got[r.tok] = r.query_send[r.tok]
    grad_query = sum_slots(r.query_got, d.tok_count).astype(low)
    lat_total = nn(grad_query, r.rquery[...]) + nn(own_dk, r.rkey[...]) + nn(own_dv, r.rvalue[...])
    r.lat_parts[...] = lat_total.astype(low).reshape(r.lat_parts.shape)
    lats = spread_of(r, d, "head", lambda peer: r.lat_parts.at[peer], r.lat_got, r.lat_sems)
    lats.start()
    put_parts(d, r.parts_final, 0, tn(narrow_lat, grad_query))
    final.start()
    late.forward()
    by_in.finish()
    final.forward()
    lats.wait()
    r.lat_got[r.head] = r.lat_parts[r.head]
    total = sum_slots(r.lat_got, d.head_count)
    count = owned // d.head_count
    mine = pl.ds(pl.multiple_of(r.head * count, count), count)
    normed, scale = norm_parts(r.latents[mine, :].astype(wide))
    r.lat_grad[...] = r.grad_own[mine, :] + norm_vjp(normed, scale, total)
    by_out.finish()
    early.finish()

    def wait_cross(c, carry):
        cross_copy(c).wait()
        cross_f(r, c).wait()
        return carry

    lax.fori_loop(0, chunks, wait_cross, 0)
    late.finish()
    final.finish()


FRONT, MIDDLE, BACK = 1, 2, 4
OWN, CARRY, OUT = 0, 1, 2


def buffers(d):
    low, wide = jnp.bfloat16, jnp.float32
    size, half = 4 * SUB, (2 * SUB, d.width)
    n, h = d.tok_count, d.head_count
    front, middle, back = FRONT, MIDDLE, BACK
    every = front | middle | back
    by_chunk = (d.chunks, d.column, size)
    by_head, by_column = (d.heads, d.latent_count, HD), (d.column, d.latent_count)
    key_heads, own_heads = (d.chunks, d.heads, size, HD), (d.heads, d.owned, HD)
    pairs, queries, wide_rows = (n, d.owned, 2 * d.column), (n, d.owned, d.column), (n, d.owned, d.packed)
    halves, quarters = (d.chunks, 2, SUB, d.width), (d.chunks, SUB, d.width)
    tok_sems, head_sems, sum_sems = (2, n), (2, h), (4, d.outer)

    def slots(columns):
        return (d.outer, d.share, columns)

    def parts(columns):
        return (d.outer, 2, d.share, columns)

    return dict(
        query_t=(by_chunk, low, front | middle, CARRY),
        key=(by_head, low, front | middle, CARRY),
        value=(by_head, low, front | middle, CARRY),
        key_t=(by_column, low, front | middle, CARRY),
        value_t=(by_column, low, front | middle, CARRY),
        read_key=(key_heads, low, front | back, CARRY),
        read_value=(key_heads, low, front | back, CARRY),
        read_key_t=(by_chunk, low, front | back, CARRY),
        read_value_t=(by_chunk, low, front, OWN),
        own_key=(own_heads, low, front | back, CARRY),
        own_value=(own_heads, low, front | back, CARRY),
        own_key_t=((d.column, d.owned), low, front | back, CARRY),
        own_value_t=((d.column, d.owned), low, front, OWN),
        read_query_t=(by_column, low, front | back, CARRY),
        lat_one=((d.owned, d.width), wide, front | back, CARRY),
        mixed=((d.owned, d.packed), wide, front | back, CARRY),
        update=((d.chunks, 2, *half), low, every, OWN),
        query_all=(queries, low, front, OWN),
        sums=((d.packed, d.latent_count), wide, front, OWN),
        sums_send=(wide_rows, low, front, OWN),
        sums_got=(wide_rows, low, front, OWN),
        head_parts=((h, d.owned, d.width), low, front | back, OWN),
        pair_all=(pairs, low, front, OWN),
        query_sems=(tok_sems, None, front, OWN),
        sums_sems=(tok_sems, None, front, OWN),
        head_sems=(head_sems, None, front, OWN),
        pair_sems=(tok_sems, None, front, OWN),
        grad_one=((d.quarter, d.width), wide, middle, OUT),
        grad_query_t=(by_chunk, low, middle | back, CARRY),
        grad_pairs=(pairs, low, middle | back, CARRY),
        parts_in=(parts(d.hidden), low, middle | back, CARRY),
        parts_out=(parts(d.hidden), low, middle | back, CARRY),
        grad_write=((d.width, d.column), low, middle | back, CARRY),
        f_half=(halves, low, middle | back, OUT),
        write_out=((d.column, d.width), low, middle, OWN),
        mlp_in=((d.width, d.hidden), low, middle, OWN),
        mlp_out=((d.hidden, d.width), low, middle, OWN),
        cotangent=((4, d.quarter, d.width), low, middle, OWN),
        mixed_t=(by_chunk, low, middle, OWN),
        log_total=((d.chunks, 8, size), wide, middle, OWN),
        own_a=(half, wide, middle, OWN),
        send_a=(half, low, middle, OWN),
        got_a=((2, *half), low, middle, OWN),
        half_a=(half, low, middle, OWN),
        cross_a=((2, *half), low, middle, OWN),
        own_d=(half, wide, middle, OWN),
        send_d=(half, low, middle, OWN),
        got_d=((2, *half), low, middle, OWN),
        half_d=(half, low, middle, OWN),
        cross_d=((2, *half), low, middle, OWN),
        summed_d=((2, 2, *half), low, middle, OWN),
        own_f=(half, wide, middle | back, OWN),
        send_f=(half, low, middle | back, OWN),
        got_f=((2, *half), low, middle | back, OWN),
        acc_in=((d.width, d.hidden), wide, middle | back, OWN),
        acc_out=((d.width, d.hidden), wide, middle | back, OWN),
        acc_write=((d.column, d.width), wide, middle, OWN),
        normed_s=((size, d.width), low, middle, OWN),
        act_s=((size, d.hidden), low, middle, OWN),
        inner_s=((size, d.hidden), low, middle, OWN),
        wide_s=((2, *half), wide, middle | back, OWN),
        latent_image=((d.latent_count, 128), jnp.int32, middle, OWN),
        grad_key=(by_head, wide, middle, OWN),
        grad_value=(by_head, wide, middle, OWN),
        send_sems=((7, 2), None, middle, OWN),
        recv_sems=((7, 2), None, middle, OWN),
        load_sems=((4,), None, middle, OWN),
        f_cross=(quarters, low, back, OUT),
        x_half=(halves, low, back, OUT),
        x_cross=(quarters, low, back, OUT),
        in_two=(slots(d.hidden), low, back, OUT),
        out_two=(slots(d.hidden), low, back, OUT),
        early_two=(slots(5 * d.column), low, back, OUT),
        late_two=(slots(2 * d.column), low, back, OUT),
        final_two=(slots(d.column), low, back, OUT),
        lat_grad=((d.owned // h, d.width), wide, back, OUT),
        in_one=(slots(d.hidden), low, back, OWN),
        out_one=(slots(d.hidden), low, back, OWN),
        early_one=(slots(5 * d.column), low, back, OWN),
        late_one=(slots(2 * d.column), low, back, OWN),
        final_one=(slots(d.column), low, back, OWN),
        parts_early=(parts(5 * d.column), low, back, OWN),
        parts_late=(parts(2 * d.column), low, back, OWN),
        parts_final=(parts(d.column), low, back, OWN),
        got_pairs=(pairs, low, back, OWN),
        output_all=(wide_rows, low, back, OWN),
        output_t=(by_column, low, back, OWN),
        rows=((8, d.latent_count), wide, back, OWN),
        grad_own=((d.owned, d.width), wide, back, OWN),
        query_sum=(by_column, wide, back, OWN),
        query_send=(queries, low, back, OWN),
        query_got=(queries, low, back, OWN),
        lat_parts=((h, d.owned // h, d.width), low, back, OWN),
        lat_got=((h, d.owned // h, d.width), low, back, OWN),
        in_sems=(sum_sems, None, back, OWN),
        out_sems=(sum_sems, None, back, OWN),
        early_sems=(sum_sems, None, back, OWN),
        late_sems=(sum_sems, None, back, OWN),
        final_sems=(sum_sems, None, back, OWN),
        pairs_sems=(tok_sems, None, back, OWN),
        heads_sems=(head_sems, None, back, OWN),
        output_sems=(tok_sems, None, back, OWN),
        back_query_sems=(tok_sems, None, back, OWN),
        lat_sems=(head_sems, None, back, OWN),
        core_sems=((2, 2), None, back, OWN),
        x_sems=((2, d.chunks), None, back, OWN),
        f_sems=((2, d.chunks), None, back, OWN),
    )


def run(d, number, phases, inputs, made):
    table = buffers(d)
    later = (FRONT | MIDDLE | BACK) & ~(2 * phases - 1) if phases != FRONT | MIDDLE | BACK else 0
    given = {x: (array, memory) for x, (array, uses, memory) in inputs.items() if uses & phases}
    given |= {x: (made[x], pltpu.VMEM) for x in made if table[x][2] & phases}
    wanted, inside = [], []
    for x, (shape, kind, uses, keep) in table.items():
        if x in given or not uses & phases:
            continue
        (wanted if keep == OUT or (keep == CARRY and uses & later) else inside).append(x)
    names = [*given, *wanted, *inside]
    merged = phases == FRONT | MIDDLE | BACK

    def kernel(*refs):
        r = SimpleNamespace(**dict(zip(names, refs, strict=True)))
        r.tok, r.head = lax.axis_index("tok"), lax.axis_index("head")
        if phases & MIDDLE:
            for load in loads(r):
                load.start()
        if not phases & FRONT:
            greet_all(r, d)
        if phases & FRONT:
            front_phase(r, d)
        if phases & MIDDLE:
            middle_phase(r, d, merged)
        if phases & BACK:
            back_phase(r, d, merged)

    def scratch(x):
        shape, kind = table[x][:2]
        return pltpu.SemaphoreType.DMA(shape) if kind is None else pltpu.VMEM(shape, kind)

    out = pl.pallas_call(
        kernel,
        out_shape=[jax.ShapeDtypeStruct(*table[x][:2]) for x in wanted],
        in_specs=[pl.BlockSpec(memory_space=memory) for array, memory in given.values()],
        out_specs=[pl.BlockSpec(memory_space=pltpu.VMEM) for x in wanted],
        scratch_shapes=[scratch(x) for x in inside],
        compiler_params=pltpu.CompilerParams(
            collective_id=number, has_side_effects=True, vmem_limit_bytes=63 << 20
        ),
        name="phases%d" % phases,
    )(*[array for array, memory in given.values()])
    return dict(zip(wanted, out, strict=True))


def finish_kernel(
    index, tokens, grad_one, f_own, f_cross, x_own, x_cross, in_two, out_two, early_two, early_all, late_two, final_two, lat,
    layer_out, input_grad, latent_grad, g_rquery, g_rkey, g_rvalue, g_rout, g_wquery, g_wkey, g_wvalue, g_wout,
    g_in, g_out,
):
    wide = jnp.float32
    column = final_two.shape[2]
    rows, width = grad_one.shape

    def both(own, cross):
        return (own[...].astype(wide).reshape(rows, width)) + cross[...].astype(wide).reshape(rows, width)

    layer_out[...] = both(f_own, f_cross).astype(jnp.bfloat16)
    normed, scale = norm_parts(tokens[0].astype(wide))
    input_grad[...] = grad_one[...] + norm_vjp(normed, scale, both(x_own, x_cross))
    latent_grad[...] = lat[...]

    def total(ref):
        kept = ref[0].astype(wide)
        for s in range(1, ref.shape[0]):
            kept = kept + ref[s].astype(wide)
        return kept

    g_in[...] = total(in_two)
    g_out[...] = total(out_two)
    g_rquery[...] = total(final_two)
    late = total(late_two)
    g_rkey[...] = late[:, :column]
    g_rvalue[...] = late[:, column:]
    early = total(early_two)
    g_wquery[...] = early[:, :column]
    g_wkey[...] = early[:, 2 * column : 3 * column]
    g_wvalue[...] = early[:, 3 * column : 4 * column]

    @pl.when(pl.program_id(0) == 0)
    def _():
        early = total(early_all)
        g_wout[...] = early[:, column : 2 * column].T
        g_rout[...] = early[:, 4 * column :].T


def finish(d, tokens, m):
    steps = 2 if d.share % 32 == 0 else 1
    rows, share, parts = d.quarter // steps, d.share // steps, d.chunks // steps
    head = lax.axis_index("head")
    index = jnp.stack([head, head // 2]).astype(jnp.int32)
    half = pl.BlockSpec((parts, None, SUB, d.width), lambda i, at: (i, at[1], 0, 0))
    cross = pl.BlockSpec((parts, SUB, d.width), lambda i, at: (i, 0, 0))
    strip = pl.BlockSpec((rows, d.width), lambda i, at: (i, 0))
    whole = pl.BlockSpec((d.owned // d.head_count, d.width), lambda i, at: (0, 0))

    def slots(columns):
        return pl.BlockSpec((d.outer, share, columns), lambda i, at: (0, i, 0))

    def part(columns):
        return pl.BlockSpec((share, columns), lambda i, at: (i, 0))

    wide, column = jnp.float32, d.column
    grads = [column] * 8 + [d.hidden] * 2
    turned = (column, d.share)
    return pl.pallas_call(
        finish_kernel,
        out_shape=[
            jax.ShapeDtypeStruct((d.quarter, d.width), jnp.bfloat16),
            jax.ShapeDtypeStruct((d.quarter, d.width), wide),
            jax.ShapeDtypeStruct((d.owned // d.head_count, d.width), wide),
            *[jax.ShapeDtypeStruct(turned if k in (3, 7) else (d.share, columns), wide) for k, columns in enumerate(grads)],
        ],
        grid_spec=pltpu.PrefetchScalarGridSpec(
            num_scalar_prefetch=1,
            grid=(steps,),
            in_specs=[
                pl.BlockSpec((1, rows, d.width), lambda i, at: (at[0], i, 0)),
                strip,
                half,
                cross,
                half,
                cross,
                slots(d.hidden),
                slots(d.hidden),
                slots(5 * column),
                pl.BlockSpec((d.outer, d.share, 5 * column), lambda i, at: (0, 0, 0)),
                slots(2 * column),
                slots(column),
                whole,
            ],
            out_specs=[
                strip,
                strip,
                whole,
                *[
                    pl.BlockSpec(turned, lambda i, at: (0, 0)) if k in (3, 7) else part(columns)
                    for k, columns in enumerate(grads)
                ],
            ],
        ),
        compiler_params=pltpu.CompilerParams(vmem_limit_bytes=62 << 20),
        name="finish",
    )(
        index, tokens, m.grad_one, m.f_half, m.f_cross, m.x_half, m.x_cross, m.in_two, m.out_two, m.early_two,
        m.early_two, m.late_two, m.final_two, m.lat_grad,
    )


def shards(
    tokens,
    latents,
    image_groups,
    read_query,
    read_key,
    read_value,
    read_out,
    write_query,
    write_key,
    write_value,
    write_out,
    mlp_in,
    mlp_out,
    cotangent,
):
    d = SimpleNamespace(tok_count=lax.axis_size("tok"), head_count=lax.axis_size("head"))
    rows, d.width = tokens.shape
    d.owned, d.column, d.hidden, d.packed = latents.shape[0], read_query.shape[1], mlp_in.shape[1], 256
    d.heads, d.quarter, d.groups_here = d.column // HD, rows // 4, rows // GROUP
    d.chunks, d.latent_count = d.quarter // SUB, d.owned * d.tok_count
    d.block = min(512, d.latent_count)
    d.blocks, d.per = d.latent_count // d.block, d.block // d.owned
    d.outer, d.share = d.tok_count // 2, d.width // d.tok_count
    tokens = tokens.reshape(4, d.quarter, d.width)
    every, vmem = FRONT | MIDDLE | BACK, pltpu.VMEM
    inputs = dict(
        counts=(image_groups, every, pltpu.SMEM),
        tokens=(tokens, every, vmem),
        latents=(latents, FRONT | BACK, vmem),
        rquery=(read_query.T, FRONT | BACK, vmem),
        rkey=(read_key.T, FRONT | BACK, vmem),
        rvalue=(read_value.T, FRONT | BACK, vmem),
        rout=(read_out, FRONT | BACK, vmem),
        wquery=(write_query.T, FRONT | BACK, vmem),
        wkey=(write_key.T, FRONT | BACK, vmem),
        wvalue=(write_value.T, FRONT | BACK, vmem),
        write_out_hbm=(write_out, MIDDLE, pl.ANY),
        mlp_in_hbm=(mlp_in, MIDDLE, pl.ANY),
        mlp_out_hbm=(mlp_out, MIDDLE, pl.ANY),
        cotangent_hbm=(cotangent.reshape(4, d.quarter, d.width), MIDDLE, pl.ANY),
    )
    made = {}
    for number, phases in enumerate([every] if d.latent_count <= 512 else [FRONT, MIDDLE, BACK]):
        made |= run(d, number, phases, inputs, made)
    (
        layer_out, input_grad, latent_grad, g_rquery, g_rkey, g_rvalue, g_rout, g_wquery, g_wkey, g_wvalue, g_wout,
        g_in, g_out,
    ) = finish(d, tokens, SimpleNamespace(**made))
    return (
        layer_out,
        input_grad,
        latent_grad,
        g_rquery,
        g_rkey,
        g_rvalue,
        g_rout,
        g_wquery,
        g_wkey,
        g_wvalue,
        g_wout,
        g_in,
        g_out.T,
    )


def solution(mesh):
    return jax.shard_map(
        shards,
        mesh=mesh,
        in_specs=(
            P("tok", None),
            P("tok", None),
            P(),
            P(None, "head"),
            P(None, "head"),
            P(None, "head"),
            P("head", None),
            P(None, "head"),
            P(None, "head"),
            P(None, "head"),
            P("head", None),
            P(None, "head"),
            P("head", None),
            P("tok", None),
        ),
        out_specs=(
            P(("tok", "head"), None),
            P(("tok", "head"), None),
            P(("tok", "head"), None),
            P("tok", "head"),
            P("tok", "head"),
            P("tok", "head"),
            P("head", "tok"),
            P("tok", "head"),
            P("tok", "head"),
            P("tok", "head"),
            P("head", "tok"),
            P("tok", "head"),
            P("head", "tok"),
        ),
        check_vma=False,
    )
```

```python
from functools import partial
from types import SimpleNamespace

import jax
import jax.numpy as jnp
from jax import lax
from jax.experimental import pallas as pl
from jax.experimental.pallas import tpu as pltpu
from jax.sharding import PartitionSpec as P

MESH = pl.DeviceIdType.MESH
HD = 64
GROUP = 256
LPG = 8
epsilon = 1e-05
SUB = 64
SCALE = 0.125
LOG2E = 1.4426950408889634
MASKED = -1e30
GELU_A = 0.7978845608028654
GELU_B = 0.044715
LAG = 2
DEPTH = 3


def nn(left, right):
    return lax.dot_general(left, right, (((1,), (0,)), ((), ())), preferred_element_type=jnp.float32)


def nt(left, right):
    return lax.dot_general(left, right, (((1,), (1,)), ((), ())), preferred_element_type=jnp.float32)


def tn(left, right):
    return lax.dot_general(left, right, (((0,), (0,)), ((), ())), preferred_element_type=jnp.float32)


def norm_parts(values):
    center = values - jnp.mean(values, axis=-1, keepdims=True)
    scale = lax.rsqrt(jnp.mean(center * center, axis=-1, keepdims=True) + epsilon)
    return center * scale, scale


def norm_vjp(normed, scale, grad):
    return scale * (
        grad
        - jnp.mean(grad, axis=-1, keepdims=True)
        - normed * jnp.mean(grad * normed, axis=-1, keepdims=True)
    )


def image_of(counts, group):
    bound = jnp.int32(0)
    image = jnp.zeros_like(group)
    for m in range(counts.shape[0]):
        bound = bound + counts[m]
        image = image + jnp.where(bound <= group, 1, 0)
    return image


def latent_row_image(counts, start, count):
    group = lax.shift_right_logical(lax.broadcasted_iota(jnp.int32, (1, count), 1) + start, 3)
    return image_of(counts, group)


def head_rows(h):
    return slice(h * HD, (h + 1) * HD)


def chunk_rows(ref, c):
    part = pl.ds(pl.multiple_of(c * SUB, SUB), SUB)
    return jnp.concatenate([ref[q, part, :] for q in (0, 2, 1, 3)], axis=0)


def greet_all(r, d):
    barrier = pltpu.get_barrier_semaphore()

    def greet(step, carry):
        peer = lax.rem(r.tok + step, d.tok_count)
        pl.semaphore_signal(barrier, inc=1, device_id=(peer, r.head), device_id_type=MESH)
        return carry

    lax.fori_loop(1, d.tok_count, greet, 0)
    for step in range(1, d.head_count):
        peer = lax.rem(r.head + step, d.head_count)
        pl.semaphore_signal(barrier, inc=1, device_id=(r.tok, peer), device_id_type=MESH)
    pl.semaphore_wait(barrier, d.tok_count + d.head_count - 2)


class Spread:
    def __init__(self, axis, tok, head, count, source, got, sems):
        self.axis, self.tok, self.head, self.count = axis, tok, head, count
        self.me = tok if axis == "tok" else head
        self.source, self.got, self.sems = source, got, sems

    def copy(self, peer, slot):
        return pltpu.make_async_remote_copy(
            src_ref=self.source(peer),
            dst_ref=self.got.at[slot],
            send_sem=self.sems.at[0, peer],
            recv_sem=self.sems.at[1, slot],
            device_id=(peer, self.head) if self.axis == "tok" else (self.tok, peer),
            device_id_type=MESH,
        )

    def start(self):
        def go(step, carry):
            self.copy(lax.rem(self.me + step, self.count), self.me).start()
            return carry

        lax.fori_loop(1, self.count, go, 0)

    def wait(self):
        def go(step, carry):
            peer = lax.rem(self.me + step, self.count)
            self.copy(peer, peer).wait()
            return carry

        lax.fori_loop(1, self.count, go, 0)


class Scatter:
    def __init__(self, r, parts, got_one, got_two, sems):
        self.head, self.mine, self.side = r.head, r.tok // 2, lax.rem(r.tok, 2)
        self.parts, self.got_one, self.got_two, self.sems = parts, got_one, got_two, sems
        self.outer = parts.shape[0]

    def first(self, block):
        return pltpu.make_async_remote_copy(
            src_ref=self.parts.at[block, 1 - self.side],
            dst_ref=self.got_one.at[block],
            send_sem=self.sems.at[0, block],
            recv_sem=self.sems.at[1, block],
            device_id=(self.mine * 2 + (1 - self.side), self.head),
            device_id_type=MESH,
        )

    def second(self, block, source):
        return pltpu.make_async_remote_copy(
            src_ref=self.got_one.at[block],
            dst_ref=self.got_two.at[source],
            send_sem=self.sems.at[2, block],
            recv_sem=self.sems.at[3, source],
            device_id=(block * 2 + self.side, self.head),
            device_id_type=MESH,
        )

    def start_block(self, k):
        self.first(lax.rem(self.mine + k + 1, self.outer)).start()

    def forward_block(self, k):
        block = lax.rem(self.mine + k + 1, self.outer)
        self.got_one[block] = self.total(block)
        self.second(block, self.mine).start()

    def start(self):
        def go(k, carry):
            self.start_block(k)
            return carry

        lax.fori_loop(0, self.outer, go, 0)

    def total(self, block):
        self.first(block).wait()
        both = self.parts[block, self.side].astype(jnp.float32) + self.got_one[block].astype(jnp.float32)
        return both.astype(jnp.bfloat16)

    def forward(self):
        def go(k, carry):
            self.forward_block(k)
            return carry

        lax.fori_loop(0, self.outer - 1, go, 0)

    def finish(self):
        self.got_two[self.mine] = self.total(self.mine)

        def go(step, carry):
            peer = lax.rem(self.mine + step, self.outer)
            self.second(peer, peer).wait()
            return carry

        lax.fori_loop(1, self.outer, go, 0)


def split_three(value):
    high = value.astype(jnp.bfloat16).astype(jnp.float32)
    rest = value - high
    middle_part = rest.astype(jnp.bfloat16).astype(jnp.float32)
    return high, middle_part, rest - middle_part


def pick_lanes(shape, columns):
    lane = lax.broadcasted_iota(jnp.int32, shape, 1)
    value = jnp.zeros(shape, jnp.float32)
    for at, column in columns:
        value = jnp.where(lane == at, column, value)
    return value


def by_head(shape, columns):
    lane = lax.broadcasted_iota(jnp.int32, shape, 1)
    value = jnp.broadcast_to(columns[-1], shape)
    for h in range(len(columns) - 2, -1, -1):
        value = jnp.where(lane < (h + 1) * HD, columns[h], value)
    return value


def chunk_bias(counts, tok, groups_here, c, quarter, row_image, rows):
    kept = []
    for q in (0, 2, 1, 3):
        group = tok * groups_here + (q * quarter + c * SUB) // GROUP
        image = image_of(counts, group)
        kept.append([jnp.where(row_image == image, row, MASKED) for row in rows])
    return kept


def add_rows(values, rows):
    count = values.shape[0] // len(rows)
    return jnp.concatenate([values[k * count : (k + 1) * count] + row for k, row in enumerate(rows)], axis=0)


def token_images(r, d, c):
    return [
        image_of(r.counts, r.tok * d.groups_here + (q * d.quarter + c * SUB) // GROUP) for q in (0, 2, 1, 3)
    ]


def spread_of(r, d, axis, source, got, sems):
    count = d.tok_count if axis == "tok" else d.head_count
    return Spread(axis, r.tok, r.head, count, source, got, sems)


def sum_slots(ref, count):
    first = ref[0].astype(jnp.float32)
    return lax.fori_loop(1, count, lambda s, kept: kept + ref[s].astype(jnp.float32), first)


def each_block(d, body, carry):
    if d.blocks == 1:
        return body(0, carry)
    return lax.fori_loop(0, d.blocks, lambda b, kept: body(b, kept), carry)


def block_at(d, b):
    start = b * d.block if d.blocks == 1 else pl.multiple_of(b * d.block, d.block)
    return start, pl.ds(start, d.block)


def keep_heads(ref, wide, heads):
    for h in range(heads):
        ref[h] = wide[:, head_rows(h)]


def chunk_core_side(r):
    return lax.rem(r.head, 2), r.head // 2


def loads(r):
    pairs = (
        (r.write_out_hbm, r.write_out),
        (r.mlp_in_hbm, r.mlp_in),
        (r.mlp_out_hbm, r.mlp_out),
        (r.cotangent_hbm, r.store.at[0:4]),
    )
    return [pltpu.make_async_copy(source, target, r.load_sems.at[k]) for k, (source, target) in enumerate(pairs)]


def front_phase(r, d):
    low = jnp.bfloat16
    heads, column, chunks, owned = d.heads, d.column, d.chunks, d.owned
    latents_wide = r.latents[...].astype(jnp.float32)
    normed_lat = norm_parts(latents_wide)[0].astype(low)
    r.query_all[r.tok] = nt(normed_lat, r.rquery[...]).astype(low)
    greet_all(r, d)
    queries = spread_of(r, d, "tok", lambda peer: r.query_all.at[r.tok], r.query_all, r.query_sems)
    queries.start()
    keys = nt(normed_lat, r.rkey[...]).astype(low)
    values = nt(normed_lat, r.rvalue[...]).astype(low)
    keep_heads(r.own_key, keys, heads)
    keep_heads(r.own_value, values, heads)
    r.own_key_t[...] = keys.T
    r.own_value_t[...] = values.T

    def project(c, carry):
        normed = norm_parts(chunk_rows(r.tokens, c).astype(jnp.float32))[0].astype(low)
        r.update[c] = normed.reshape(r.update.shape[1:])
        keys = nt(normed, r.rkey[...]).astype(low)
        values = nt(normed, r.rvalue[...]).astype(low)
        keep_heads(r.read_key.at[c], keys, heads)
        keep_heads(r.read_value.at[c], values, heads)
        r.read_key_t[c] = keys.T
        r.read_value_t[c] = values.T
        return carry

    lax.fori_loop(0, chunks, project, 0)
    r.sums[...] = jnp.zeros_like(r.sums)
    queries.wait()

    def attend(scores, rows, values_t, here, h):
        weights = jnp.exp2(add_rows(scores * (SCALE * LOG2E), rows))
        r.sums[column + h : column + h + 1, here] += jnp.sum(weights, axis=0, keepdims=True)
        r.sums[head_rows(h), here] += nn(values_t, weights.astype(low))

    def read_block(b, carry):
        start, here = block_at(d, b)
        query = r.query_all[pl.ds(b * d.per, d.per)].reshape(d.block, column).T
        r.read_query_t[:, here] = query
        row_image = latent_row_image(r.counts, start, d.block)

        def masks(images):
            return [jnp.where(row_image == image, 0.0, MASKED) for image in images]

        def read_chunk(c, carry):
            rows = masks(token_images(r, d, c))
            for h in range(heads):
                attend(nn(r.read_key[c, h], query[head_rows(h)]), rows, r.read_value_t[c, head_rows(h)], here, h)
            return carry

        lax.fori_loop(0, chunks, read_chunk, 0)
        rows = masks([image_of(r.counts, r.tok * d.groups_here + g) for g in range(d.groups_here)])
        for h in range(heads):
            attend(nn(r.own_key[h], query[head_rows(h)]), rows, r.own_value_t[head_rows(h), :], here, h)
        total = r.sums[column : column + heads, here]
        high = total.astype(low).astype(jnp.float32)
        r.sums[column : column + heads, here] = high
        r.sums[column + heads : column + 2 * heads, here] = total - high
        r.sums_send[pl.ds(b * d.per, d.per)] = r.sums[:, here].T.astype(low).reshape(d.per, owned, d.packed)
        return carry

    each_block(d, read_block, 0)
    totals = spread_of(r, d, "tok", lambda peer: r.sums_send.at[peer], r.sums_got, r.sums_sems)
    totals.start()

    def project_query(c, carry):
        r.query_t[c] = nt(r.wquery[...], r.update[c].reshape(4 * SUB, d.width)).astype(low)
        return carry

    lax.fori_loop(0, chunks, project_query, 0)
    totals.wait()
    r.sums_got[r.tok] = r.sums_send[r.tok]
    summed = sum_slots(r.sums_got, d.tok_count)
    whole = [
        summed[:, column + h : column + h + 1] + summed[:, column + heads + h : column + heads + h + 1]
        for h in range(heads)
    ]
    mixed = summed[:, :column] / by_head((owned, column), whole)
    r.mixed[:, :column] = mixed
    r.mixed[:, column:] = pick_lanes(
        (owned, d.packed - column), [(h, -jnp.log2(whole[h])) for h in range(heads)]
    )
    r.head_parts[r.head] = nn(mixed.astype(low), r.rout[...]).astype(low)
    moved = spread_of(r, d, "head", lambda peer: r.head_parts.at[r.head], r.head_parts, r.head_sems)
    moved.start()
    moved.wait()
    latents_one = latents_wide
    for s in range(d.head_count):
        latents_one = latents_one + r.head_parts[s].astype(jnp.float32)
    r.lat_one[...] = latents_one
    normed_one = norm_parts(latents_one)[0].astype(low)
    r.pair_all[r.tok, :, :column] = nt(normed_one, r.wkey[...]).astype(low)
    r.pair_all[r.tok, :, column:] = nt(normed_one, r.wvalue[...]).astype(low)
    pairs = spread_of(r, d, "tok", lambda peer: r.pair_all.at[r.tok], r.pair_all, r.pair_sems)
    pairs.start()
    pairs.wait()

    def unpack(b, carry):
        start, here = block_at(d, b)
        wide = r.pair_all[pl.ds(b * d.per, d.per)].reshape(d.block, 2 * column)
        for h in range(heads):
            r.key[h, here, :] = wide[:, head_rows(h)]
            r.value[h, here, :] = wide[:, head_rows(heads + h)]
        turned = wide.T
        r.key_t[:, here] = turned[:column]
        r.value_t[:, here] = turned[column:]
        return carry

    each_block(d, unpack, 0)


def mlp_scatters(r):
    return (
        Scatter(r, r.parts_in, r.in_one, r.in_two, r.in_sems),
        Scatter(r, r.parts_out, r.out_one, r.out_two, r.out_sems),
    )


def cross_f(r, c):
    core, side = chunk_core_side(r)
    return pltpu.make_async_remote_copy(
        src_ref=r.f_half.at[c, 1 - side],
        dst_ref=r.f_cross.at[c],
        send_sem=r.f_sems.at[0, c],
        recv_sem=r.f_sems.at[1, c],
        device_id=(r.tok, (1 - side) * 2 + core),
        device_id_type=MESH,
    )


def middle_phase(r, d, merged):
    chunks, heads, width = d.chunks, d.heads, d.width
    core, side = chunk_core_side(r)
    other = 1 - core
    core_peer = (r.tok, side * 2 + other)
    side_peer = (r.tok, (1 - side) * 2 + core)
    for load in loads(r):
        load.wait()

    def copy(kind, chunk, source, target, peer):
        return pltpu.make_async_remote_copy(
            src_ref=source,
            dst_ref=target,
            send_sem=r.send_sems.at[kind, chunk],
            recv_sem=r.recv_sems.at[kind, chunk],
            device_id=peer,
            device_id_type=MESH,
        )

    def core_a(c):
        return copy(0, c, r.send_a, r.got_a.at[lax.rem(c, 2)], core_peer)

    def cross_copy_a(c):
        return copy(1, c, r.half_a.at[lax.rem(c, 3)], r.cross_a.at[c], side_peer)

    def core_u(c):
        return copy(2, c, r.update.at[c, core], r.update.at[c, core], core_peer)

    def core_d(c):
        return copy(3, c, r.send_d, r.got_d.at[lax.rem(c, 2)], core_peer)

    def half_d(c):
        rows = pl.ds(pl.multiple_of(lax.rem(c, 4) * 2 * SUB, 2 * SUB), 2 * SUB)
        return r.store.at[4 + c // 4, rows, :]

    def cross_d(c):
        rows = pl.ds(pl.multiple_of(lax.rem(c, 4) * 2 * SUB, 2 * SUB), 2 * SUB)
        return r.store.at[6 + c // 4, rows, :]

    def cross_copy_d(c):
        return copy(4, c, half_d(c), cross_d(c), side_peer)

    def core_s(c):
        half = r.summed_d.at[lax.rem(c, 4), core]
        return copy(5, c, half, half, core_peer)

    def core_f(c):
        return copy(6, c, r.send_f, r.got_f.at[lax.rem(c, 2)], core_peer)

    def latent_images(start):
        row = lax.broadcasted_iota(jnp.int32, r.latent_image.shape, 0) + start
        return image_of(r.counts, lax.shift_right_logical(row, 3))

    if d.blocks == 1:
        r.latent_image[...] = latent_images(0)

    def mask_of(c, b):
        image = r.latent_image[...] if d.blocks == 1 else latent_images(b * d.block)
        image = jnp.concatenate([image, image], axis=1)
        lane = lax.broadcasted_iota(jnp.int32, (1, 4 * SUB), 1)
        part = lax.shift_right_logical(lane, 6)
        part = 2 * lax.rem(part, 2) + part // 2
        row = part * d.quarter + c * SUB
        group = r.tok * d.groups_here + lax.shift_right_logical(row, 8)
        return jnp.where(image == image_of(r.counts, group), 0.0, MASKED)

    def halve(wide, own, send):
        r.wide_s[...] = wide.reshape(r.wide_s.shape)
        own[...] = r.wide_s[core]
        send[...] = r.wide_s[other].astype(jnp.bfloat16)

    r.acc_in[...] = jnp.zeros_like(r.acc_in)
    r.acc_out[...] = jnp.zeros_like(r.acc_out)
    r.acc_write[...] = jnp.zeros_like(r.acc_write)
    r.grad_key[...] = jnp.zeros_like(r.grad_key)
    r.grad_value[...] = jnp.zeros_like(r.grad_value)

    def write_forward(c):
        query = r.query_t[c]

        def body(b, carry):
            here = block_at(d, b)[1]
            bias = mask_of(c, b)
            kept = []
            for h in range(heads):
                scores = nn(r.key[h, here, :], query[head_rows(h)])
                weights = jnp.exp2(scores * (SCALE * LOG2E) + bias)
                total = jnp.sum(weights, axis=0, keepdims=True)
                mixed = nn(r.value_t[head_rows(h), here], weights.astype(jnp.bfloat16))
                kept.append((carry[h][0] + total, carry[h][1] + mixed))
            return tuple(kept)

        size = 4 * SUB
        zero = (jnp.zeros((1, size), jnp.float32), jnp.zeros((HD, size), jnp.float32))
        totals = each_block(d, body, (zero,) * heads)
        mixed = jnp.concatenate([part / total for total, part in totals], axis=0)
        mixed = mixed.astype(jnp.bfloat16)
        r.mixed_t[c] = mixed
        for h in range(heads):
            r.log_total[c, h : h + 1] = -jnp.log2(totals[h][0])
        halve(tn(mixed, r.write_out[...]), r.own_a, r.send_a)
        core_a(c).start()

    def finish_update(c):
        cross_copy_a(c).wait()
        mine = r.half_a[lax.rem(c, 3)].astype(jnp.float32) + r.cross_a[c].astype(jnp.float32)
        r.update[c, core] = mine.astype(jnp.bfloat16)
        core_u(c).start()

    def cross_update(c):
        core_a(c).wait()
        half = r.own_a[...] + r.got_a[lax.rem(c, 2)].astype(jnp.float32)
        r.half_a[lax.rem(c, 3)] = half.astype(jnp.bfloat16)
        cross_copy_a(c).start()

    def one_rows(c):
        moved = r.update[c].reshape(4 * SUB, width).astype(jnp.float32)
        return chunk_rows(r.tokens, c).astype(jnp.float32) + moved

    def feed_forward(c):
        core_u(c).wait()
        normed = norm_parts(one_rows(c))[0].astype(jnp.bfloat16)
        r.normed_s[...] = normed
        inner = nn(normed, r.mlp_in[...])
        square = inner * inner
        tanh = jnp.tanh(GELU_A * inner * (1.0 + GELU_B * square))
        half = 0.5 + 0.5 * tanh
        active = (inner * half).astype(jnp.bfloat16)
        r.act_s[...] = active
        slope = half + 0.5 * GELU_A * inner * (1.0 - tanh * tanh) * (1.0 + 3.0 * GELU_B * square)
        grad_inner = (nt(chunk_rows(r.store, c), r.mlp_out[...]) * slope).astype(jnp.bfloat16)
        r.inner_s[...] = grad_inner
        halve(nt(grad_inner, r.mlp_in[...]), r.own_d, r.send_d)
        core_d(c).start()
        halve(nn(active, r.mlp_out[...]), r.own_f, r.send_f)
        core_f(c).start()

    def finish_grad(c):
        cross_copy_d(c).wait()
        mine = half_d(c)[...].astype(jnp.float32) + cross_d(c)[...].astype(jnp.float32)
        r.summed_d[lax.rem(c, 4), core] = mine.astype(jnp.bfloat16)
        core_s(c).start()

    def cross_grad(c):
        slot = lax.rem(c, 2)
        core_d(c).wait()
        half_d(c)[...] = (r.own_d[...] + r.got_d[slot].astype(jnp.float32)).astype(jnp.bfloat16)

    def keep_forward(c):
        slot = lax.rem(c, 2)
        core_f(c).wait()
        total = (r.own_f[...] + r.got_f[slot].astype(jnp.float32)).reshape(2, SUB, width)
        r.f_half[c] = total.astype(jnp.bfloat16)
        part = pl.ds(pl.multiple_of(c * SUB, SUB), SUB)
        rows = pl.ds(pl.multiple_of(side * SUB, SUB), SUB)
        mine = jnp.where(side == 0, total[0], total[1]) + r.update[c, core, rows, :].astype(jnp.float32)
        r.f_half[c, side] = (mine + r.tokens[r.head, part, :].astype(jnp.float32)).astype(jnp.bfloat16)

    def weight_grads(c):
        r.acc_in[...] += tn(r.normed_s[...], r.inner_s[...])
        r.acc_out[...] += tn(chunk_rows(r.store, c), r.act_s[...])

    def write_backward(c):
        core_s(c).wait()
        normed, scale = norm_parts(one_rows(c))
        grad = r.summed_d[lax.rem(c, 4)].reshape(4 * SUB, width).astype(jnp.float32)
        wide = chunk_rows(r.store, c).astype(jnp.float32) + norm_vjp(normed, scale, grad)
        r.wide_s[...] = wide.reshape(r.wide_s.shape)
        part = pl.ds(pl.multiple_of(c * SUB, SUB), SUB)
        mine = pl.ds(pl.multiple_of(side * SUB, SUB), SUB)
        r.grad_one[part, :] = r.wide_s[core, mine, :]
        narrow = wide.astype(jnp.bfloat16)
        mixed = r.mixed_t[c]
        r.acc_write[...] += nn(mixed, narrow)
        grad_mixed = nt(r.write_out[...], narrow).astype(jnp.bfloat16)
        query = r.query_t[c]
        product = grad_mixed.astype(jnp.float32) * mixed.astype(jnp.float32)

        def body(b, carry):
            here = block_at(d, b)[1]
            bias = mask_of(c, b)
            kept = []
            for h in range(heads):
                rows = head_rows(h)
                scores = nn(r.key[h, here, :], query[rows])
                weights = jnp.exp2(scores * (SCALE * LOG2E) + (bias + r.log_total[c, h : h + 1]))
                grad_weights = nn(r.value[h, here, :], grad_mixed[rows])
                delta = jnp.sum(product[rows], axis=0, keepdims=True)
                grad_scores = (weights * (grad_weights - delta)).astype(jnp.bfloat16)
                r.grad_key[h, here, :] += nt(grad_scores, query[rows])
                r.grad_value[h, here, :] += nt(weights.astype(jnp.bfloat16), grad_mixed[rows])
                kept.append(carry[h] + nn(r.key_t[rows, here], grad_scores))
            return tuple(kept)

        zero = jnp.zeros((HD, 4 * SUB), jnp.float32)
        grads = each_block(d, body, (zero,) * heads)
        r.grad_query_t[c] = (jnp.concatenate(grads, axis=0) * SCALE).astype(jnp.bfloat16)

    def step(i, carry):
        @pl.when(jnp.logical_and(i >= DEPTH, i < chunks + DEPTH))
        def _():
            finish_update(i - DEPTH)

        @pl.when(i < chunks)
        def _():
            write_forward(i)

        @pl.when(i > DEPTH)
        def _():
            weight_grads(i - DEPTH - 1)
            keep_forward(i - DEPTH - 1)
            cross_grad(i - DEPTH - 1)

        @pl.when(i < chunks)
        def _():
            cross_update(i)

        @pl.when(i >= chunks)
        def _():
            cross_copy_d(i - chunks).start()

        @pl.when(jnp.logical_and(i >= DEPTH, i < chunks + DEPTH))
        def _():
            feed_forward(i - DEPTH)

        return carry

    ahead = DEPTH + 1
    lax.fori_loop(0, chunks + ahead, step, 0)
    put_parts(d, r.parts_in, 0, r.acc_in)
    put_parts(d, r.parts_out, 0, r.acc_out)
    by_in, by_out = mlp_scatters(r) if merged else (None, None)

    def back_step(c, carry):
        @pl.when(c < chunks)
        def _():
            finish_grad(c)

        @pl.when(c + ahead < chunks)
        def _():
            cross_copy_d(c + ahead).start()

        if merged:
            trickle(by_in, c)
            trickle(by_out, c - d.outer)

        @pl.when(c >= 1)
        def _():
            write_backward(c - 1)

        return carry

    lax.fori_loop(0, chunks + 1, back_step, 0)
    def pack(b, carry):
        here = block_at(d, b)[1]
        there = pl.ds(b * d.per, d.per)
        both = [r.grad_key[h, here, :] * SCALE for h in range(heads)]
        both += [r.grad_value[h, here, :] for h in range(heads)]
        wide = jnp.concatenate(both, axis=1).astype(jnp.bfloat16)
        r.grad_pairs[there] = wide.reshape(d.per, d.owned, 2 * d.column)
        return carry

    each_block(d, pack, 0)
    r.grad_write[...] = r.acc_write[...].T.astype(jnp.bfloat16)


def trickle(scatter, k):
    pl.when(jnp.logical_and(k >= 0, k < scatter.outer))(partial(scatter.start_block, k))
    pl.when(jnp.logical_and(k >= LAG, k < LAG + scatter.outer - 1))(partial(scatter.forward_block, k - LAG))


def put_parts(d, ref, at, value):
    width = value.shape[1]
    for b in range(d.tok_count):
        rows = slice(b * d.share, (b + 1) * d.share)
        ref[b // 2, b % 2, :, at : at + width] = value[rows, :].astype(jnp.bfloat16)


def back_phase(r, d, merged):
    chunks, heads, width, column, owned = d.chunks, d.heads, d.width, d.column, d.owned
    low, wide = jnp.bfloat16, jnp.float32
    core, side = chunk_core_side(r)
    other = 1 - core
    pairs = spread_of(r, d, "tok", lambda peer: r.grad_pairs.at[peer], r.got_pairs, r.pairs_sems)
    pairs.start()
    by_in, by_out = mlp_scatters(r)
    early = Scatter(r, r.parts_early, r.early_one, r.early_two, r.early_sems)
    later = Scatter(r, r.parts_second, r.second_one, r.second_two, r.second_sems)
    late = Scatter(r, r.parts_late, r.late_one, r.late_two, r.late_sems)
    final = Scatter(r, r.parts_final, r.final_one, r.final_two, r.final_sems)
    if not merged:
        by_in.start()
        by_out.start()
    first_f = chunks // 2
    for c in range(first_f):
        cross_f(r, c).start()
    r.acc_in[...] = jnp.zeros_like(r.acc_in)
    r.acc_out[...] = jnp.zeros_like(r.acc_out)
    at_key, at_value = slice(0, column), slice(256, 256 + column)

    def plain_weights(key, h, here, masks):
        scores = nn(key, r.read_query_t[head_rows(h), here]) * (SCALE * LOG2E)
        return jnp.exp2(add_rows(scores, masks))

    def masks_of(b, images):
        start, here = block_at(d, b)
        row_image = latent_row_image(r.counts, start, d.block)
        return [jnp.where(row_image == image, 0.0, MASKED) for image in images]

    def keep_weights(first, last):
        def keep(c, carry):
            masks = masks_of(0, token_images(r, d, c))
            top, low_rows = slice(0, 4 * SUB), slice(4 * SUB, 8 * SUB)
            for h in range(heads):
                weights = plain_weights(r.read_key[c, h], h, slice(0, d.block), masks).astype(low)
                if h == 0:
                    r.store[c, top, 0:512] = weights
                elif h == 1:
                    r.store[c, top, 512:768] = weights[:, 0:256]
                    r.store[c, low_rows, 0:256] = weights[:, 256:512]
                else:
                    r.store[c, low_rows, 256:768] = weights
            return carry

        if keeps_weights(d):
            lax.fori_loop(first, last, keep, 0)

    def kept_weights(c, h):
        top, low_rows = slice(0, 4 * SUB), slice(4 * SUB, 8 * SUB)
        if h == 0:
            return r.store[c, top, 0:512]
        if h == 1:
            return jnp.concatenate([r.store[c, top, 512:768], r.store[c, low_rows, 0:256]], axis=1)
        return r.store[c, low_rows, 256:768]

    def query_weights(c, carry):
        normed = norm_parts(chunk_rows(r.tokens, c).astype(wide))[0].astype(low)
        r.update[c] = normed.reshape(r.update.shape[1:])
        r.acc_in[:, :column] += tn(normed, r.grad_query_t[c].T)
        return carry

    lax.fori_loop(0, chunks, query_weights, 0)
    put_parts(d, r.parts_early, 0, r.acc_in[:, :column])
    put_parts(d, r.parts_early, column, r.grad_write)
    keep_weights(0, chunks // 2)
    pairs.wait()
    early.start()
    if not merged:
        by_in.forward()
        by_out.forward()
    r.got_pairs[r.tok] = r.grad_pairs[r.tok]
    summed = sum_slots(r.got_pairs, d.tok_count).astype(low)
    grad_key, grad_value = summed[:, :column], summed[:, column:]
    r.head_parts[r.head] = (nn(grad_key, r.wkey[...]) + nn(grad_value, r.wvalue[...])).astype(low)
    moved = spread_of(r, d, "head", lambda peer: r.head_parts.at[r.head], r.head_parts, r.heads_sems)
    moved.start()
    keep_weights(chunks // 2, 3 * chunks // 4)
    normed_one, scale_one = norm_parts(r.lat_one[...])
    put_parts(d, r.parts_second, 0, tn(normed_one.astype(low), summed))
    moved.wait()
    grad_lat_one = norm_vjp(normed_one, scale_one, sum_slots(r.head_parts, d.head_count))
    r.grad_own[...] = grad_lat_one
    narrow = grad_lat_one.astype(low)
    grad_mixed = nt(narrow, r.rout[...]).astype(low)
    mixed = r.mixed[:, :column]
    product = grad_mixed.astype(wide) * mixed
    extra = []
    for h in range(heads):
        delta = jnp.sum(product[:, head_rows(h)], axis=1, keepdims=True)
        logs = r.mixed[:, column + h : column + h + 1]
        for k, (first, second) in enumerate(zip(split_three(delta), split_three(logs), strict=True)):
            extra.append((3 * h + k, first))
            extra.append((3 * (heads + h) + k, second))
    r.output_all[r.tok, :, :column] = grad_mixed
    r.output_all[r.tok, :, column:] = pick_lanes((owned, d.packed - column), extra).astype(low)
    outputs = spread_of(r, d, "tok", lambda peer: r.output_all.at[r.tok], r.output_all, r.output_sems)
    outputs.start()
    put_parts(d, r.parts_second, 2 * column, tn(narrow, mixed.astype(low)))
    r.query_sum[...] = jnp.zeros_like(r.query_sum)
    keep_weights(3 * chunks // 4, chunks)
    outputs.wait()
    early.forward()

    def turn(b, carry):
        here = block_at(d, b)[1]
        turned = r.output_all[pl.ds(b * d.per, d.per)].reshape(d.block, d.packed).astype(wide).T
        def joined(k):
            at = column + 3 * k
            return turned[at : at + 1] + turned[at + 1 : at + 2] + turned[at + 2 : at + 3]

        for h in range(heads):
            inverse = jnp.exp2(joined(heads + h))
            r.output_t[head_rows(h), here] = (turned[head_rows(h)] * inverse).astype(low)
            r.rows[h : h + 1, here] = joined(h) * inverse
        return carry

    each_block(d, turn, 0)

    def key_grads(count, weights_of, value_of, key_t_of, images):
        def body(b, carry):
            here = block_at(d, b)[1]
            masks = masks_of(b, images)
            kept = []
            for h in range(heads):
                hr = head_rows(h)
                query, output = r.read_query_t[hr, here], r.output_t[hr, here]
                weights = weights_of(h, here, masks)
                grad_weights = nn(value_of(h), output) - r.rows[h : h + 1, here]
                grad_scores = (weights.astype(wide) * grad_weights).astype(low)
                r.query_sum[hr, here] += nn(key_t_of(h), grad_scores)
                kept.append(
                    (carry[h][0] + nt(grad_scores, query), carry[h][1] + nt(weights.astype(low), output))
                )
            return tuple(kept)

        zero = jnp.zeros((count, HD), wide)
        grads = each_block(d, body, ((zero, zero),) * heads)
        keys = jnp.concatenate([grads[h][0] for h in range(heads)], axis=1) * SCALE
        values = jnp.concatenate([grads[h][1] for h in range(heads)], axis=1)
        return keys.astype(low), values.astype(low)

    def core_copy(c):
        slot = lax.rem(c, 2)
        return pltpu.make_async_remote_copy(
            src_ref=r.send_f,
            dst_ref=r.got_f.at[slot],
            send_sem=r.core_sems.at[0, slot],
            recv_sem=r.core_sems.at[1, slot],
            device_id=(r.tok, side * 2 + other),
            device_id_type=MESH,
        )

    def cross_copy(c):
        return pltpu.make_async_remote_copy(
            src_ref=r.x_half.at[c, 1 - side],
            dst_ref=r.x_cross.at[c],
            send_sem=r.x_sems.at[0, c],
            recv_sem=r.x_sems.at[1, c],
            device_id=(r.tok, (1 - side) * 2 + core),
            device_id_type=MESH,
        )

    def compute(c):
        def weights_of(h, here, masks):
            return kept_weights(c, h) if keeps_weights(d) else plain_weights(r.read_key[c, h], h, here, masks)

        dk, dv = key_grads(
            4 * SUB,
            weights_of,
            lambda h: r.read_value[c, h],
            lambda h: r.read_key_t[c, head_rows(h), :],
            token_images(r, d, c),
        )
        moved = nn(dk, r.rkey[...]) + nn(dv, r.rvalue[...]) + tn(r.grad_query_t[c], r.wquery[...])
        r.wide_s[...] = moved.reshape(r.wide_s.shape)
        r.own_f[...] = r.wide_s[core]
        r.send_f[...] = r.wide_s[other].astype(low)
        core_copy(c).start()
        normed = r.update[c].reshape(4 * SUB, width)
        r.acc_out[:, at_key] += tn(normed, dk)
        r.acc_out[:, at_value] += tn(normed, dv)

    def cross(c):
        core_copy(c).wait()
        total = r.own_f[...] + r.got_f[lax.rem(c, 2)].astype(wide)
        r.x_half[c] = total.astype(low).reshape(2, SUB, width)
        cross_copy(c).start()

    def step(c, carry):
        @pl.when(c >= 1)
        def _():
            cross(c - 1)

        @pl.when(c >= first_f)
        def _():
            cross_f(r, c).start()

        compute(c)
        trickle(later, c)
        return carry

    lax.fori_loop(0, chunks // 2, step, 0)
    lax.fori_loop(chunks // 2, chunks, step, 0)
    own_dk, own_dv = key_grads(
        owned,
        lambda h, here, masks: plain_weights(r.own_key[h], h, here, masks),
        lambda h: r.own_value[h],
        lambda h: r.own_key_t[head_rows(h), :],
        [image_of(r.counts, r.tok * d.groups_here + g) for g in range(d.groups_here)],
    )

    def turn_query(b, carry):
        here = block_at(d, b)[1]
        turned = (r.query_sum[:, here] * SCALE).T.astype(low)
        r.query_send[pl.ds(b * d.per, d.per)] = turned.reshape(d.per, owned, column)
        return carry

    each_block(d, turn_query, 0)
    queries = spread_of(r, d, "tok", lambda peer: r.query_send.at[peer], r.query_got, r.back_query_sems)
    queries.start()
    cross(chunks - 1)
    normed_lat, scale_lat = norm_parts(r.latents[...].astype(wide))
    narrow_lat = normed_lat.astype(low)
    put_parts(d, r.parts_late, 0, r.acc_out[:, at_key] + tn(narrow_lat, own_dk))
    put_parts(d, r.parts_late, column, r.acc_out[:, at_value] + tn(narrow_lat, own_dv))
    late.start()
    queries.wait()
    r.query_got[r.tok] = r.query_send[r.tok]
    grad_query = sum_slots(r.query_got, d.tok_count).astype(low)
    lat_total = nn(grad_query, r.rquery[...]) + nn(own_dk, r.rkey[...]) + nn(own_dv, r.rvalue[...])
    r.lat_parts[...] = lat_total.astype(low).reshape(r.lat_parts.shape)
    lats = spread_of(r, d, "head", lambda peer: r.lat_parts.at[peer], r.lat_got, r.lat_sems)
    lats.start()
    put_parts(d, r.parts_final, 0, tn(narrow_lat, grad_query))
    final.start()
    late.forward()
    by_in.finish()
    final.forward()
    lats.wait()
    r.lat_got[r.head] = r.lat_parts[r.head]
    total = sum_slots(r.lat_got, d.head_count)
    count = owned // d.head_count
    mine = pl.ds(pl.multiple_of(r.head * count, count), count)
    normed, scale = norm_parts(r.latents[mine, :].astype(wide))
    r.lat_grad[...] = r.grad_own[mine, :] + norm_vjp(normed, scale, total)
    by_out.finish()
    early.finish()
    later.finish()

    def wait_cross(c, carry):
        cross_copy(c).wait()
        cross_f(r, c).wait()
        return carry

    lax.fori_loop(0, chunks, wait_cross, 0)
    late.finish()
    final.finish()


FRONT, MIDDLE, BACK = 1, 2, 4
OWN, CARRY, OUT = 0, 1, 2


def keeps_weights(d):
    return d.blocks == 1 and d.heads * d.block == 2 * d.width and d.chunks == 8 and d.quarter == 8 * SUB


def buffers(d):
    low, wide = jnp.bfloat16, jnp.float32
    size, half = 4 * SUB, (2 * SUB, d.width)
    n, h = d.tok_count, d.head_count
    front, middle, back = FRONT, MIDDLE, BACK
    every = front | middle | back
    by_chunk = (d.chunks, d.column, size)
    by_head, by_column = (d.heads, d.latent_count, HD), (d.column, d.latent_count)
    key_heads, own_heads = (d.chunks, d.heads, size, HD), (d.heads, d.owned, HD)
    pairs, queries, wide_rows = (n, d.owned, 2 * d.column), (n, d.owned, d.column), (n, d.owned, d.packed)
    halves, quarters = (d.chunks, 2, SUB, d.width), (d.chunks, SUB, d.width)
    tok_sems, head_sems, sum_sems = (2, n), (2, h), (4, d.outer)

    def slots(columns):
        return (d.outer, d.share, columns)

    def parts(columns):
        return (d.outer, 2, d.share, columns)

    return dict(
        query_t=(by_chunk, low, front | middle, CARRY),
        key=(by_head, low, front | middle, CARRY),
        value=(by_head, low, front | middle, CARRY),
        key_t=(by_column, low, front | middle, CARRY),
        value_t=(by_column, low, front | middle, CARRY),
        read_key=(key_heads, low, front | back, CARRY),
        read_value=(key_heads, low, front | back, CARRY),
        read_key_t=(by_chunk, low, front | back, CARRY),
        read_value_t=(by_chunk, low, front, OWN),
        own_key=(own_heads, low, front | back, CARRY),
        own_value=(own_heads, low, front | back, CARRY),
        own_key_t=((d.column, d.owned), low, front | back, CARRY),
        own_value_t=((d.column, d.owned), low, front, OWN),
        read_query_t=(by_column, low, front | back, CARRY),
        lat_one=((d.owned, d.width), wide, front | back, CARRY),
        mixed=((d.owned, d.packed), wide, front | back, CARRY),
        update=((d.chunks, 2, *half), low, every, OWN),
        query_all=(queries, low, front, OWN),
        sums=((d.packed, d.latent_count), wide, front, OWN),
        sums_send=(wide_rows, low, front, OWN),
        sums_got=(wide_rows, low, front, OWN),
        head_parts=((h, d.owned, d.width), low, front | back, OWN),
        pair_all=(pairs, low, front, OWN),
        query_sems=(tok_sems, None, front, OWN),
        sums_sems=(tok_sems, None, front, OWN),
        head_sems=(head_sems, None, front, OWN),
        pair_sems=(tok_sems, None, front, OWN),
        grad_one=((d.quarter, d.width), wide, middle, OUT),
        grad_query_t=(by_chunk, low, middle | back, CARRY),
        grad_pairs=(pairs, low, middle | back, CARRY),
        parts_in=(parts(d.hidden), low, middle | back, CARRY),
        parts_out=(parts(d.hidden), low, middle | back, CARRY),
        grad_write=((d.width, d.column), low, middle | back, CARRY),
        f_half=(halves, low, middle | back, OUT),
        write_out=((d.column, d.width), low, middle, OWN),
        mlp_in=((d.width, d.hidden), low, middle, OWN),
        mlp_out=((d.hidden, d.width), low, middle, OWN),
        store=((8, d.quarter, d.width), low, middle | back if keeps_weights(d) else middle, OWN),
        mixed_t=(by_chunk, low, middle, OWN),
        log_total=((d.chunks, 8, size), wide, middle, OWN),
        own_a=(half, wide, middle, OWN),
        send_a=(half, low, middle, OWN),
        got_a=((2, *half), low, middle, OWN),
        half_a=((3, *half), low, middle, OWN),
        cross_a=((d.chunks, *half), low, middle, OWN),
        own_d=(half, wide, middle, OWN),
        send_d=(half, low, middle, OWN),
        got_d=((2, *half), low, middle, OWN),
        summed_d=((4, 2, *half), low, middle, OWN),
        own_f=(half, wide, middle | back, OWN),
        send_f=(half, low, middle | back, OWN),
        got_f=((2, *half), low, middle | back, OWN),
        acc_in=((d.width, d.hidden), wide, middle | back, OWN),
        acc_out=((d.width, d.hidden), wide, middle | back, OWN),
        acc_write=((d.column, d.width), wide, middle, OWN),
        normed_s=((size, d.width), low, middle, OWN),
        act_s=((size, d.hidden), low, middle, OWN),
        inner_s=((size, d.hidden), low, middle, OWN),
        wide_s=((2, *half), wide, middle | back, OWN),
        latent_image=((d.block, 128), jnp.int32, middle, OWN),
        grad_key=(by_head, wide, middle, OWN),
        grad_value=(by_head, wide, middle, OWN),
        send_sems=((7, d.chunks), None, middle, OWN),
        recv_sems=((7, d.chunks), None, middle, OWN),
        load_sems=((4,), None, middle, OWN),
        f_cross=(quarters, low, back, OUT),
        x_half=(halves, low, back, OUT),
        x_cross=(quarters, low, back, OUT),
        in_two=(slots(d.hidden), low, back, OUT),
        out_two=(slots(d.hidden), low, back, OUT),
        early_two=(slots(2 * d.column), low, back, OUT),
        second_two=(slots(3 * d.column), low, back, OUT),
        late_two=(slots(2 * d.column), low, back, OUT),
        final_two=(slots(d.column), low, back, OUT),
        lat_grad=((d.owned // h, d.width), wide, back, OUT),
        in_one=(slots(d.hidden), low, back, OWN),
        out_one=(slots(d.hidden), low, back, OWN),
        early_one=(slots(2 * d.column), low, back, OWN),
        second_one=(slots(3 * d.column), low, back, OWN),
        late_one=(slots(2 * d.column), low, back, OWN),
        final_one=(slots(d.column), low, back, OWN),
        parts_early=(parts(2 * d.column), low, back, OWN),
        parts_second=(parts(3 * d.column), low, back, OWN),
        parts_late=(parts(2 * d.column), low, back, OWN),
        parts_final=(parts(d.column), low, back, OWN),
        got_pairs=(pairs, low, back, OWN),
        output_all=(wide_rows, low, back, OWN),
        output_t=(by_column, low, back, OWN),
        rows=((8, d.latent_count), wide, back, OWN),
        grad_own=((d.owned, d.width), wide, back, OWN),
        query_sum=(by_column, wide, back, OWN),
        query_send=(queries, low, back, OWN),
        query_got=(queries, low, back, OWN),
        lat_parts=((h, d.owned // h, d.width), low, back, OWN),
        lat_got=((h, d.owned // h, d.width), low, back, OWN),
        in_sems=(sum_sems, None, back, OWN),
        out_sems=(sum_sems, None, back, OWN),
        early_sems=(sum_sems, None, back, OWN),
        second_sems=(sum_sems, None, back, OWN),
        late_sems=(sum_sems, None, back, OWN),
        final_sems=(sum_sems, None, back, OWN),
        pairs_sems=(tok_sems, None, back, OWN),
        heads_sems=(head_sems, None, back, OWN),
        output_sems=(tok_sems, None, back, OWN),
        back_query_sems=(tok_sems, None, back, OWN),
        lat_sems=(head_sems, None, back, OWN),
        core_sems=((2, 2), None, back, OWN),
        x_sems=((2, d.chunks), None, back, OWN),
        f_sems=((2, d.chunks), None, back, OWN),
    )


def run(d, number, phases, inputs, made):
    table = buffers(d)
    later = (FRONT | MIDDLE | BACK) & ~(2 * phases - 1) if phases != FRONT | MIDDLE | BACK else 0
    given = {x: (array, memory) for x, (array, uses, memory) in inputs.items() if uses & phases}
    given |= {x: (made[x], pltpu.VMEM) for x in made if table[x][2] & phases}
    wanted, inside = [], []
    for x, (shape, kind, uses, keep) in table.items():
        if x in given or not uses & phases:
            continue
        (wanted if keep == OUT or (keep == CARRY and uses & later) else inside).append(x)
    names = [*given, *wanted, *inside]
    merged = phases == FRONT | MIDDLE | BACK

    def kernel(*refs):
        r = SimpleNamespace(**dict(zip(names, refs, strict=True)))
        r.tok, r.head = lax.axis_index("tok"), lax.axis_index("head")
        if phases & MIDDLE:
            for load in loads(r):
                load.start()
        if not phases & FRONT:
            greet_all(r, d)
        if phases & FRONT:
            front_phase(r, d)
        if phases & MIDDLE:
            middle_phase(r, d, merged)
        if phases & BACK:
            back_phase(r, d, merged)

    def scratch(x):
        shape, kind = table[x][:2]
        return pltpu.SemaphoreType.DMA(shape) if kind is None else pltpu.VMEM(shape, kind)

    out = pl.pallas_call(
        kernel,
        out_shape=[jax.ShapeDtypeStruct(*table[x][:2]) for x in wanted],
        in_specs=[pl.BlockSpec(memory_space=memory) for array, memory in given.values()],
        out_specs=[pl.BlockSpec(memory_space=pltpu.VMEM) for x in wanted],
        scratch_shapes=[scratch(x) for x in inside],
        compiler_params=pltpu.CompilerParams(
            collective_id=number, has_side_effects=True, vmem_limit_bytes=127 << 19
        ),
        name="phases%d" % phases,
    )(*[array for array, memory in given.values()])
    return dict(zip(wanted, out, strict=True))


def finish_kernel(
    index, tokens, grad_one, f_own, f_cross, x_own, x_cross, in_two, out_two, early_two, early_all, second_two, second_all, late_two, final_two, lat,
    layer_out, input_grad, latent_grad, g_rquery, g_rkey, g_rvalue, g_rout, g_wquery, g_wkey, g_wvalue, g_wout,
    g_in, g_out,
):
    wide = jnp.float32
    column = final_two.shape[2]
    rows, width = grad_one.shape

    def both(own, cross):
        return (own[...].astype(wide).reshape(rows, width)) + cross[...].astype(wide).reshape(rows, width)

    layer_out[...] = both(f_own, f_cross).astype(jnp.bfloat16)
    normed, scale = norm_parts(tokens[0].astype(wide))
    input_grad[...] = grad_one[...] + norm_vjp(normed, scale, both(x_own, x_cross))
    latent_grad[...] = lat[...]

    def total(ref):
        kept = ref[0].astype(wide)
        for s in range(1, ref.shape[0]):
            kept = kept + ref[s].astype(wide)
        return kept

    g_in[...] = total(in_two)
    g_out[...] = total(out_two)
    g_rquery[...] = total(final_two)
    late = total(late_two)
    g_rkey[...] = late[:, :column]
    g_rvalue[...] = late[:, column:]
    g_wquery[...] = total(early_two)[:, :column]
    second = total(second_two)
    g_wkey[...] = second[:, :column]
    g_wvalue[...] = second[:, column : 2 * column]

    @pl.when(pl.program_id(0) == 0)
    def _():
        g_wout[...] = total(early_all)[:, column:].T
        g_rout[...] = total(second_all)[:, 2 * column :].T


def finish(d, tokens, m):
    steps = 2 if d.share % 32 == 0 else 1
    rows, share, parts = d.quarter // steps, d.share // steps, d.chunks // steps
    head = lax.axis_index("head")
    index = jnp.stack([head, head // 2]).astype(jnp.int32)
    half = pl.BlockSpec((parts, None, SUB, d.width), lambda i, at: (i, at[1], 0, 0))
    cross = pl.BlockSpec((parts, SUB, d.width), lambda i, at: (i, 0, 0))
    strip = pl.BlockSpec((rows, d.width), lambda i, at: (i, 0))
    whole = pl.BlockSpec((d.owned // d.head_count, d.width), lambda i, at: (0, 0))

    def slots(columns):
        return pl.BlockSpec((d.outer, share, columns), lambda i, at: (0, i, 0))

    def part(columns):
        return pl.BlockSpec((share, columns), lambda i, at: (i, 0))

    wide, column = jnp.float32, d.column
    grads = [column] * 8 + [d.hidden] * 2
    turned = (column, d.share)
    return pl.pallas_call(
        finish_kernel,
        out_shape=[
            jax.ShapeDtypeStruct((d.quarter, d.width), jnp.bfloat16),
            jax.ShapeDtypeStruct((d.quarter, d.width), wide),
            jax.ShapeDtypeStruct((d.owned // d.head_count, d.width), wide),
            *[jax.ShapeDtypeStruct(turned if k in (3, 7) else (d.share, columns), wide) for k, columns in enumerate(grads)],
        ],
        grid_spec=pltpu.PrefetchScalarGridSpec(
            num_scalar_prefetch=1,
            grid=(steps,),
            in_specs=[
                pl.BlockSpec((1, rows, d.width), lambda i, at: (at[0], i, 0)),
                strip,
                half,
                cross,
                half,
                cross,
                slots(d.hidden),
                slots(d.hidden),
                slots(2 * column),
                pl.BlockSpec((d.outer, d.share, 2 * column), lambda i, at: (0, 0, 0)),
                slots(3 * column),
                pl.BlockSpec((d.outer, d.share, 3 * column), lambda i, at: (0, 0, 0)),
                slots(2 * column),
                slots(column),
                whole,
            ],
            out_specs=[
                strip,
                strip,
                whole,
                *[
                    pl.BlockSpec(turned, lambda i, at: (0, 0)) if k in (3, 7) else part(columns)
                    for k, columns in enumerate(grads)
                ],
            ],
        ),
        compiler_params=pltpu.CompilerParams(vmem_limit_bytes=62 << 20),
        name="finish",
    )(
        index, tokens, m.grad_one, m.f_half, m.f_cross, m.x_half, m.x_cross, m.in_two, m.out_two, m.early_two,
        m.early_two, m.second_two, m.second_two, m.late_two, m.final_two, m.lat_grad,
    )


def shards(
    tokens,
    latents,
    image_groups,
    read_query,
    read_key,
    read_value,
    read_out,
    write_query,
    write_key,
    write_value,
    write_out,
    mlp_in,
    mlp_out,
    cotangent,
):
    d = SimpleNamespace(tok_count=lax.axis_size("tok"), head_count=lax.axis_size("head"))
    rows, d.width = tokens.shape
    d.owned, d.column, d.hidden, d.packed = latents.shape[0], read_query.shape[1], mlp_in.shape[1], 256
    d.heads, d.quarter, d.groups_here = d.column // HD, rows // 4, rows // GROUP
    d.chunks, d.latent_count = d.quarter // SUB, d.owned * d.tok_count
    d.block = min(512, d.latent_count)
    d.blocks, d.per = d.latent_count // d.block, d.block // d.owned
    d.outer, d.share = d.tok_count // 2, d.width // d.tok_count
    tokens = tokens.reshape(4, d.quarter, d.width)
    every, vmem = FRONT | MIDDLE | BACK, pltpu.VMEM
    inputs = dict(
        counts=(image_groups, every, pltpu.SMEM),
        tokens=(tokens, every, vmem),
        latents=(latents, FRONT | BACK, vmem),
        rquery=(read_query.T, FRONT | BACK, vmem),
        rkey=(read_key.T, FRONT | BACK, vmem),
        rvalue=(read_value.T, FRONT | BACK, vmem),
        rout=(read_out, FRONT | BACK, vmem),
        wquery=(write_query.T, FRONT | BACK, vmem),
        wkey=(write_key.T, FRONT | BACK, vmem),
        wvalue=(write_value.T, FRONT | BACK, vmem),
        write_out_hbm=(write_out, MIDDLE, pl.ANY),
        mlp_in_hbm=(mlp_in, MIDDLE, pl.ANY),
        mlp_out_hbm=(mlp_out, MIDDLE, pl.ANY),
        cotangent_hbm=(cotangent.reshape(4, d.quarter, d.width), MIDDLE, pl.ANY),
    )
    made = {}
    for number, phases in enumerate([every] if d.latent_count <= 512 else [FRONT, MIDDLE, BACK]):
        made |= run(d, number, phases, inputs, made)
    (
        layer_out, input_grad, latent_grad, g_rquery, g_rkey, g_rvalue, g_rout, g_wquery, g_wkey, g_wvalue, g_wout,
        g_in, g_out,
    ) = finish(d, tokens, SimpleNamespace(**made))
    return (
        layer_out,
        input_grad,
        latent_grad,
        g_rquery,
        g_rkey,
        g_rvalue,
        g_rout,
        g_wquery,
        g_wkey,
        g_wvalue,
        g_wout,
        g_in,
        g_out.T,
    )


def solution(mesh):
    return jax.shard_map(
        shards,
        mesh=mesh,
        in_specs=(
            P("tok", None),
            P("tok", None),
            P(),
            P(None, "head"),
            P(None, "head"),
            P(None, "head"),
            P("head", None),
            P(None, "head"),
            P(None, "head"),
            P(None, "head"),
            P("head", None),
            P(None, "head"),
            P("head", None),
            P("tok", None),
        ),
        out_specs=(
            P(("tok", "head"), None),
            P(("tok", "head"), None),
            P(("tok", "head"), None),
            P("tok", "head"),
            P("tok", "head"),
            P("tok", "head"),
            P("head", "tok"),
            P("tok", "head"),
            P("tok", "head"),
            P("tok", "head"),
            P("head", "tok"),
            P("tok", "head"),
            P("head", "tok"),
        ),
        check_vma=False,
    )
```

```python
from functools import partial
from types import SimpleNamespace

import jax
import jax.numpy as jnp
from jax import lax
from jax.experimental import pallas as pl
from jax.experimental.pallas import tpu as pltpu
from jax.sharding import PartitionSpec as P

MESH = pl.DeviceIdType.MESH
HD = 64
GROUP = 256
LPG = 8
epsilon = 1e-05
SUB = 64
SCALE = 0.125
LOG2E = 1.4426950408889634
MASKED = -1e30
GELU_A = 0.7978845608028654
GELU_B = 0.044715
LAG = 2
WRITES = 3


def nn(left, right):
    return lax.dot_general(left, right, (((1,), (0,)), ((), ())), preferred_element_type=jnp.float32)


def nt(left, right):
    return lax.dot_general(left, right, (((1,), (1,)), ((), ())), preferred_element_type=jnp.float32)


def tn(left, right):
    return lax.dot_general(left, right, (((0,), (0,)), ((), ())), preferred_element_type=jnp.float32)


def norm_parts(values):
    center = values - jnp.mean(values, axis=-1, keepdims=True)
    scale = lax.rsqrt(jnp.mean(center * center, axis=-1, keepdims=True) + epsilon)
    return center * scale, scale


def norm_vjp(normed, scale, grad):
    return scale * (
        grad
        - jnp.mean(grad, axis=-1, keepdims=True)
        - normed * jnp.mean(grad * normed, axis=-1, keepdims=True)
    )


def image_of(counts, group):
    bound = jnp.int32(0)
    image = jnp.zeros_like(group)
    for m in range(counts.shape[0]):
        bound = bound + counts[m]
        image = image + jnp.where(bound <= group, 1, 0)
    return image


def latent_row_image(counts, start, count):
    group = lax.shift_right_logical(lax.broadcasted_iota(jnp.int32, (1, count), 1) + start, 3)
    return image_of(counts, group)


def head_rows(h):
    return slice(h * HD, (h + 1) * HD)


def chunk_rows(ref, c):
    part = pl.ds(pl.multiple_of(c * SUB, SUB), SUB)
    return jnp.concatenate([ref[q, part, :] for q in range(4)], axis=0)


def greet_all(r, d):
    barrier = pltpu.get_barrier_semaphore()

    def greet(step, carry):
        peer = lax.rem(r.tok + step, d.tok_count)
        pl.semaphore_signal(barrier, inc=1, device_id=(peer, r.head), device_id_type=MESH)
        return carry

    lax.fori_loop(1, d.tok_count, greet, 0)
    for step in range(1, d.head_count):
        peer = lax.rem(r.head + step, d.head_count)
        pl.semaphore_signal(barrier, inc=1, device_id=(r.tok, peer), device_id_type=MESH)
    pl.semaphore_wait(barrier, d.tok_count + d.head_count - 2)


class Spread:
    def __init__(self, axis, tok, head, count, source, got, sems):
        self.axis, self.tok, self.head, self.count = axis, tok, head, count
        self.me = tok if axis == "tok" else head
        self.source, self.got, self.sems = source, got, sems

    def copy(self, peer, slot):
        return pltpu.make_async_remote_copy(
            src_ref=self.source(peer),
            dst_ref=self.got.at[slot],
            send_sem=self.sems.at[0, peer],
            recv_sem=self.sems.at[1, slot],
            device_id=(peer, self.head) if self.axis == "tok" else (self.tok, peer),
            device_id_type=MESH,
        )

    def start(self):
        def go(step, carry):
            self.copy(lax.rem(self.me + step, self.count), self.me).start()
            return carry

        lax.fori_loop(1, self.count, go, 0)

    def wait(self):
        def go(step, carry):
            peer = lax.rem(self.me + step, self.count)
            self.copy(peer, peer).wait()
            return carry

        lax.fori_loop(1, self.count, go, 0)


class Scatter:
    def __init__(self, r, parts, got_one, got_two, sems):
        self.head, self.mine, self.side = r.head, r.tok // 2, lax.rem(r.tok, 2)
        self.parts, self.got_one, self.got_two, self.sems = parts, got_one, got_two, sems
        self.outer = parts.shape[0]

    def first(self, block):
        return pltpu.make_async_remote_copy(
            src_ref=self.parts.at[block, 1 - self.side],
            dst_ref=self.got_one.at[block],
            send_sem=self.sems.at[0, block],
            recv_sem=self.sems.at[1, block],
            device_id=(self.mine * 2 + (1 - self.side), self.head),
            device_id_type=MESH,
        )

    def second(self, block, source):
        return pltpu.make_async_remote_copy(
            src_ref=self.got_one.at[block],
            dst_ref=self.got_two.at[source],
            send_sem=self.sems.at[2, block],
            recv_sem=self.sems.at[3, source],
            device_id=(block * 2 + self.side, self.head),
            device_id_type=MESH,
        )

    def start_block(self, k):
        self.first(lax.rem(self.mine + k + 1, self.outer)).start()

    def forward_block(self, k):
        block = lax.rem(self.mine + k + 1, self.outer)
        self.got_one[block] = self.total(block)
        self.second(block, self.mine).start()

    def start(self):
        def go(k, carry):
            self.start_block(k)
            return carry

        lax.fori_loop(0, self.outer, go, 0)

    def total(self, block):
        self.first(block).wait()
        both = self.parts[block, self.side].astype(jnp.float32) + self.got_one[block].astype(jnp.float32)
        return both.astype(jnp.bfloat16)

    def forward(self):
        def go(k, carry):
            self.forward_block(k)
            return carry

        lax.fori_loop(0, self.outer - 1, go, 0)

    def finish(self):
        self.got_two[self.mine] = self.total(self.mine)

        def go(step, carry):
            peer = lax.rem(self.mine + step, self.outer)
            self.second(peer, peer).wait()
            return carry

        lax.fori_loop(1, self.outer, go, 0)


def split_three(value):
    high = value.astype(jnp.bfloat16).astype(jnp.float32)
    rest = value - high
    middle_part = rest.astype(jnp.bfloat16).astype(jnp.float32)
    return high, middle_part, rest - middle_part


def pick_lanes(shape, columns):
    lane = lax.broadcasted_iota(jnp.int32, shape, 1)
    value = jnp.zeros(shape, jnp.float32)
    for at, column in columns:
        value = jnp.where(lane == at, column, value)
    return value


def by_head(shape, columns):
    lane = lax.broadcasted_iota(jnp.int32, shape, 1)
    value = jnp.broadcast_to(columns[-1], shape)
    for h in range(len(columns) - 2, -1, -1):
        value = jnp.where(lane < (h + 1) * HD, columns[h], value)
    return value


def add_rows(values, rows):
    count = values.shape[0] // len(rows)
    return jnp.concatenate([values[k * count : (k + 1) * count] + row for k, row in enumerate(rows)], axis=0)


def token_images(r, d, c):
    return [
        image_of(r.counts, r.tok * d.groups_here + (q * d.quarter + c * SUB) // GROUP) for q in range(4)
    ]


def spread_of(r, d, axis, source, got, sems):
    count = d.tok_count if axis == "tok" else d.head_count
    return Spread(axis, r.tok, r.head, count, source, got, sems)


def sum_slots(ref, count):
    first = ref[0].astype(jnp.float32)
    return lax.fori_loop(1, count, lambda s, kept: kept + ref[s].astype(jnp.float32), first)


def each_block(d, body, carry):
    if d.blocks == 1:
        return body(0, carry)
    return lax.fori_loop(0, d.blocks, lambda b, kept: body(b, kept), carry)


def block_at(d, b):
    start = b * d.block if d.blocks == 1 else pl.multiple_of(b * d.block, d.block)
    return start, pl.ds(start, d.block)


def keep_heads(ref, wide, heads):
    for h in range(heads):
        ref[h] = wide[:, head_rows(h)]


def chunk_core_side(r):
    return lax.rem(r.head, 2), r.head // 2


def load(r, k):
    source = (r.write_out_hbm, r.mlp_in_hbm, r.mlp_out_hbm, r.cotangent_hbm)[k]
    target = (r.write_out, r.mlp_in, r.mlp_out, r.store.at[0:4])[k]
    return pltpu.make_async_copy(source, target, r.load_sems.at[k])


def peer_of(r, across):
    core, side = chunk_core_side(r)
    return (r.tok, (1 - side) * 2 + core if across else side * 2 + 1 - core)


def middle_copy(r, kind, chunk, source, target, across):
    return pltpu.make_async_remote_copy(
        src_ref=source,
        dst_ref=target,
        send_sem=r.send_sems.at[kind, chunk],
        recv_sem=r.recv_sems.at[kind, chunk],
        device_id=peer_of(r, across),
        device_id_type=MESH,
    )


def peer_weights(r):
    return middle_copy(r, 10, 0, r.write_out, r.wo_peer, True)


def peer_grads(r):
    return middle_copy(r, 11, 0, r.wo_send, r.wo_got, True)


def finish_write_out(r):
    peer_grads(r).wait()
    total = r.acc_write[0] + r.wo_got[...].astype(jnp.float32)
    r.grad_write[...] = total.T.astype(jnp.bfloat16)


def halve(r, wide, own, send):
    core = chunk_core_side(r)[0]
    r.wide_s[...] = wide.reshape(r.wide_s.shape)
    for x in range(2):
        own[x] = r.wide_s[x, core]
        send[x] = r.wide_s[x, 1 - core].astype(jnp.bfloat16)


def front_phase(r, d, merged):
    low = jnp.bfloat16
    heads, column, chunks, owned = d.heads, d.column, d.chunks, d.owned
    latents_wide = r.latents[...].astype(jnp.float32)
    normed_lat = norm_parts(latents_wide)[0].astype(low)
    r.query_all[r.tok] = nt(normed_lat, r.rquery[...]).astype(low)
    greet_all(r, d)
    queries = spread_of(r, d, "tok", lambda peer: r.query_all.at[r.tok], r.query_all, r.query_sems)
    queries.start()
    keys = nt(normed_lat, r.rkey[...]).astype(low)
    values = nt(normed_lat, r.rvalue[...]).astype(low)
    keep_heads(r.own_key, keys, heads)
    keep_heads(r.own_value, values, heads)
    r.own_key_t[...] = keys.T
    r.own_value_t[...] = values.T

    def project(c, carry):
        normed = norm_parts(chunk_rows(r.tokens, c).astype(jnp.float32))[0].astype(low)
        r.update[c] = normed.reshape(r.update.shape[1:])
        keys = nt(normed, r.rkey[...]).astype(low)
        values = nt(normed, r.rvalue[...]).astype(low)
        keep_heads(r.read_key.at[c], keys, heads)
        keep_heads(r.read_value.at[c], values, heads)
        r.read_key_t[c] = keys.T
        r.read_value_t[c] = values.T
        return carry

    lax.fori_loop(0, chunks, project, 0)
    if merged:
        load(r, 0).wait()
        peer_weights(r).start()
    r.sums[...] = jnp.zeros_like(r.sums)
    queries.wait()

    def attend(scores, rows, values_t, here, h):
        weights = jnp.exp2(add_rows(scores * (SCALE * LOG2E), rows))
        r.sums[column + h : column + h + 1, here] += jnp.sum(weights, axis=0, keepdims=True)
        r.sums[head_rows(h), here] += nn(values_t, weights.astype(low))

    def read_block(b, carry):
        start, here = block_at(d, b)
        query = r.query_all[pl.ds(b * d.per, d.per)].reshape(d.block, column).T
        r.read_query_t[:, here] = query
        row_image = latent_row_image(r.counts, start, d.block)

        def masks(images):
            return [jnp.where(row_image == image, 0.0, MASKED) for image in images]

        def read_chunk(c, carry):
            rows = masks(token_images(r, d, c))
            for h in range(heads):
                attend(nn(r.read_key[c, h], query[head_rows(h)]), rows, r.read_value_t[c, head_rows(h)], here, h)
            return carry

        lax.fori_loop(0, chunks, read_chunk, 0)
        rows = masks([image_of(r.counts, r.tok * d.groups_here + g) for g in range(d.groups_here)])
        for h in range(heads):
            attend(nn(r.own_key[h], query[head_rows(h)]), rows, r.own_value_t[head_rows(h), :], here, h)
        total = r.sums[column : column + heads, here]
        high = total.astype(low).astype(jnp.float32)
        r.sums[column : column + heads, here] = high
        r.sums[column + heads : column + 2 * heads, here] = total - high
        r.sums_send[pl.ds(b * d.per, d.per)] = r.sums[:, here].T.astype(low).reshape(d.per, owned, d.packed)
        return carry

    each_block(d, read_block, 0)
    totals = spread_of(r, d, "tok", lambda peer: r.sums_send.at[peer], r.sums_got, r.sums_sems)
    totals.start()

    def project_query(c, carry):
        r.query_t[c] = nt(r.wquery[...], r.update[c].reshape(4 * SUB, d.width)).astype(low)
        return carry

    lax.fori_loop(0, chunks, project_query, 0)
    totals.wait()
    r.sums_got[r.tok] = r.sums_send[r.tok]
    summed = sum_slots(r.sums_got, d.tok_count)
    whole = [
        summed[:, column + h : column + h + 1] + summed[:, column + heads + h : column + heads + h + 1]
        for h in range(heads)
    ]
    mixed = summed[:, :column] / by_head((owned, column), whole)
    r.mixed[:, :column] = mixed
    r.mixed[:, column:] = pick_lanes(
        (owned, d.packed - column), [(h, -jnp.log2(whole[h])) for h in range(heads)]
    )
    r.head_parts[r.head] = nn(mixed.astype(low), r.rout[...]).astype(low)
    moved = spread_of(r, d, "head", lambda peer: r.head_parts.at[r.head], r.head_parts, r.head_sems)
    moved.start()
    moved.wait()
    latents_one = latents_wide
    for s in range(d.head_count):
        latents_one = latents_one + r.head_parts[s].astype(jnp.float32)
    r.lat_one[...] = latents_one
    normed_one = norm_parts(latents_one)[0].astype(low)
    r.pair_all[r.tok, :, :column] = nt(normed_one, r.wkey[...]).astype(low)
    r.pair_all[r.tok, :, column:] = nt(normed_one, r.wvalue[...]).astype(low)
    pairs = spread_of(r, d, "tok", lambda peer: r.pair_all.at[r.tok], r.pair_all, r.pair_sems)
    pairs.start()
    pairs.wait()

    def unpack(b, carry):
        start, here = block_at(d, b)
        wide = r.pair_all[pl.ds(b * d.per, d.per)].reshape(d.block, 2 * column)
        for h in range(heads):
            r.key[h, here, :] = wide[:, head_rows(h)]
            r.value[h, here, :] = wide[:, head_rows(heads + h)]
        turned = wide.T
        r.key_t[:, here] = turned[:column]
        r.value_t[:, here] = turned[column:]
        return carry

    each_block(d, unpack, 0)


def mlp_scatters(r):
    return (
        Scatter(r, r.parts_in, r.in_one, r.in_two, r.in_sems),
        Scatter(r, r.parts_out, r.out_one, r.out_two, r.out_sems),
    )


def cross_f(r, c):
    core, side = chunk_core_side(r)
    return pltpu.make_async_remote_copy(
        src_ref=r.f_half.at[c, 1 - side],
        dst_ref=r.f_cross.at[c],
        send_sem=r.f_sems.at[0, c],
        recv_sem=r.f_sems.at[1, c],
        device_id=(r.tok, (1 - side) * 2 + core),
        device_id_type=MESH,
    )


def middle_phase(r, d, merged):
    chunks, heads, width = d.chunks, d.heads, d.width
    core, side = chunk_core_side(r)
    other = 1 - core
    for k in range(1 if merged else 0, 4):
        load(r, k).wait()
    if not merged:
        peer_weights(r).start()
    peer_weights(r).wait()

    def copy(kind, chunk, source, target, across):
        return middle_copy(r, kind, chunk, source, target, across)

    def mixed_copy(c):
        return copy(0, c, r.mixed_t.at[c, 1 - side], r.mixed_got.at[c], True)

    def core_a(c):
        return copy(1, c, r.send_a, r.got_a.at[lax.rem(c, 2)], False)

    def core_u(c):
        return copy(2, c, r.update.at[c, side, core], r.update.at[c, side, core], False)

    def cross_u(c):
        return copy(3, c, r.update.at[c, side, core], r.update.at[c, side, core], True)

    def core_v(c):
        return copy(4, c, r.update.at[c, 1 - side, core], r.update.at[c, 1 - side, core], False)

    def core_d(c):
        return copy(5, c, r.send_d, r.got_d.at[lax.rem(c, 2)], False)

    def half_d(c, x, count):
        at = pl.multiple_of(lax.rem(c, 4) * 2 * SUB + x * SUB, SUB)
        return r.store.at[4 + c // 4, pl.ds(at, count), :]

    def cross_d(c):
        return r.store.at[6, pl.ds(pl.multiple_of(c * SUB, SUB), SUB), :]

    def cross_copy_d(c):
        return copy(6, c, half_d(c, 1 - side, SUB), cross_d(c), True)

    def core_s(c):
        half = r.narrow_s.at[lax.rem(c, 4), core]
        return copy(7, c, half, half, False)

    def core_f(c):
        return copy(8, c, r.send_f, r.got_f.at[lax.rem(c, 2)], False)

    def cross_o(c):
        return copy(9, c, r.mixed_send.at[lax.rem(c, 4)], r.grad_mixed_t.at[c, side], True)

    def latent_images(start):
        row = lax.broadcasted_iota(jnp.int32, r.latent_image.shape, 0) + start
        return image_of(r.counts, lax.shift_right_logical(row, 3))

    if d.blocks == 1:
        r.latent_image[...] = latent_images(0)

    def mask_of(c, b):
        image = r.latent_image[...] if d.blocks == 1 else latent_images(b * d.block)
        image = jnp.concatenate([image, image], axis=1)
        lane = lax.broadcasted_iota(jnp.int32, (1, 4 * SUB), 1)
        part = lax.shift_right_logical(lane, 6)
        row = part * d.quarter + c * SUB
        group = r.tok * d.groups_here + lax.shift_right_logical(row, 8)
        return jnp.where(image == image_of(r.counts, group), 0.0, MASKED)

    r.acc_in[...] = jnp.zeros_like(r.acc_in)
    r.acc_out[...] = jnp.zeros_like(r.acc_out)
    r.acc_write[...] = jnp.zeros_like(r.acc_write)
    r.grad_key[...] = jnp.zeros_like(r.grad_key)
    r.grad_value[...] = jnp.zeros_like(r.grad_value)

    def write_forward(c):
        query = r.query_t[c]

        def body(b, carry):
            here = block_at(d, b)[1]
            bias = mask_of(c, b)
            kept = []
            for h in range(heads):
                scores = nn(r.key[h, here, :], query[head_rows(h)])
                weights = jnp.exp2(scores * (SCALE * LOG2E) + bias)
                total = jnp.sum(weights, axis=0, keepdims=True)
                mixed = nn(r.value_t[head_rows(h), here], weights.astype(jnp.bfloat16))
                kept.append((carry[h][0] + total, carry[h][1] + mixed))
            return tuple(kept)

        size = 4 * SUB
        zero = (jnp.zeros((1, size), jnp.float32), jnp.zeros((HD, size), jnp.float32))
        totals = each_block(d, body, (zero,) * heads)
        mixed = jnp.concatenate([part / total for total, part in totals], axis=0)
        mixed = mixed.astype(jnp.bfloat16)
        r.mixed_t[c, 0] = mixed[:, : 2 * SUB]
        r.mixed_t[c, 1] = mixed[:, 2 * SUB :]
        mixed_copy(c).start()
        for h in range(heads):
            r.log_total[c, h : h + 1] = -jnp.log2(totals[h][0])

    def part_update(c):
        mixed_copy(c).wait()
        part = tn(r.mixed_t[c, side], r.write_out[...]) + tn(r.mixed_got[c], r.wo_peer[...])
        r.part_s[...] = part.reshape(r.part_s.shape)
        r.send_a[...] = r.part_s[other].astype(jnp.bfloat16)
        core_a(c).start()

    def own_update(c):
        core_a(c).wait()
        total = r.part_s[core] + r.got_a[lax.rem(c, 2)].astype(jnp.float32)
        r.update[c, side, core] = total.astype(jnp.bfloat16)
        cross_u(c).start()
        core_u(c).start()

    def pass_update(c):
        cross_u(c).wait()
        core_v(c).start()

    def one_rows(c):
        moved = r.update[c].reshape(4 * SUB, width).astype(jnp.float32)
        return chunk_rows(r.tokens, c).astype(jnp.float32) + moved

    def feed_forward(c):
        core_u(c).wait()
        core_v(c).wait()
        normed = norm_parts(one_rows(c))[0].astype(jnp.bfloat16)
        r.normed_s[...] = normed
        inner = nn(normed, r.mlp_in[...])
        square = inner * inner
        tanh = jnp.tanh(GELU_A * inner * (1.0 + GELU_B * square))
        half = 0.5 + 0.5 * tanh
        active = (inner * half).astype(jnp.bfloat16)
        r.act_s[...] = active
        slope = half + 0.5 * GELU_A * inner * (1.0 - tanh * tanh) * (1.0 + 3.0 * GELU_B * square)
        grad_inner = (nt(chunk_rows(r.store, c), r.mlp_out[...]) * slope).astype(jnp.bfloat16)
        r.inner_s[...] = grad_inner
        halve(r, nt(grad_inner, r.mlp_in[...]), r.own_d, r.send_d)
        core_d(c).start()
        halve(r, nn(active, r.mlp_out[...]), r.own_f, r.send_f)
        core_f(c).start()

    def finish_grad(c):
        cross_copy_d(c).wait()
        grad = half_d(c, side, SUB)[...].astype(jnp.float32) + cross_d(c)[...].astype(jnp.float32)
        part = pl.ds(pl.multiple_of(c * SUB, SUB), SUB)
        rows = r.tokens[r.head, part, :].astype(jnp.float32) + r.update[c, side, core].astype(jnp.float32)
        normed, scale = norm_parts(rows)
        wide = r.store[r.head, part, :].astype(jnp.float32) + norm_vjp(normed, scale, grad)
        r.grad_one[part, :] = wide
        r.narrow_s[lax.rem(c, 4), core] = wide.astype(jnp.bfloat16)
        core_s(c).start()

    def send_mixed_grad(c):
        core_s(c).wait()
        narrow = r.narrow_s[lax.rem(c, 4)].reshape(2 * SUB, width)
        r.mixed_send[lax.rem(c, 4)] = nt(r.wo_peer[...], narrow).astype(jnp.bfloat16)
        cross_o(c).start()
        r.grad_mixed_t[c, side] = nt(r.write_out[...], narrow).astype(jnp.bfloat16)
        r.acc_write[0] += nn(r.mixed_t[c, side], narrow)
        r.acc_write[1] += nn(r.mixed_got[c], narrow)

    def cross_grad(c):
        slot = lax.rem(c, 2)
        core_d(c).wait()
        total = (r.own_d[...] + r.got_d[slot].astype(jnp.float32)).astype(jnp.bfloat16)
        half_d(c, 0, 2 * SUB)[...] = total.reshape(2 * SUB, width)

    def keep_forward(c):
        slot = lax.rem(c, 2)
        core_f(c).wait()
        total = r.own_f[...] + r.got_f[slot].astype(jnp.float32)
        r.f_half[c] = total.astype(jnp.bfloat16)
        part = pl.ds(pl.multiple_of(c * SUB, SUB), SUB)
        mine = jnp.where(side == 0, total[0], total[1]) + r.update[c, side, core].astype(jnp.float32)
        r.f_half[c, side] = (mine + r.tokens[r.head, part, :].astype(jnp.float32)).astype(jnp.bfloat16)

    def weight_grads(c):
        r.acc_in[...] += tn(r.normed_s[...], r.inner_s[...])
        r.acc_out[...] += tn(chunk_rows(r.store, c), r.act_s[...])

    def write_backward(c):
        cross_o(c).wait()
        mixed = jnp.concatenate([r.mixed_t[c, 0], r.mixed_t[c, 1]], axis=1)
        grad_mixed = jnp.concatenate([r.grad_mixed_t[c, 0], r.grad_mixed_t[c, 1]], axis=1)
        query = r.query_t[c]
        product = grad_mixed.astype(jnp.float32) * mixed.astype(jnp.float32)

        def body(b, carry):
            here = block_at(d, b)[1]
            bias = mask_of(c, b)
            kept = []
            for h in range(heads):
                rows = head_rows(h)
                scores = nn(r.key[h, here, :], query[rows])
                weights = jnp.exp2(scores * (SCALE * LOG2E) + (bias + r.log_total[c, h : h + 1]))
                grad_weights = nn(r.value[h, here, :], grad_mixed[rows])
                delta = jnp.sum(product[rows], axis=0, keepdims=True)
                grad_scores = (weights * (grad_weights - delta)).astype(jnp.bfloat16)
                r.grad_key[h, here, :] += nt(grad_scores, query[rows])
                r.grad_value[h, here, :] += nt(weights.astype(jnp.bfloat16), grad_mixed[rows])
                kept.append(carry[h] + nn(r.key_t[rows, here], grad_scores))
            return tuple(kept)

        zero = jnp.zeros((HD, 4 * SUB), jnp.float32)
        grads = each_block(d, body, (zero,) * heads)
        r.grad_query_t[c] = (jnp.concatenate(grads, axis=0) * SCALE).astype(jnp.bfloat16)

    def between(first, i, last):
        return pl.when(jnp.logical_and(i >= first, i < last))

    def step(i, carry):
        @between(3, i, chunks + 3)
        def _():
            pass_update(i - 3)

        def write(c, carry):
            write_forward(c)
            return carry

        lax.fori_loop(jnp.minimum(WRITES * i, chunks), jnp.minimum(WRITES * (i + 1), chunks), write, 0)

        @between(1, i, chunks + 1)
        def _():
            part_update(i - 1)

        @pl.when(i >= 4)
        def _():
            weight_grads(i - 4)
            keep_forward(i - 4)
            cross_grad(i - 4)

        @between(1, i, chunks + 1)
        def _():
            own_update(i - 1)

        @pl.when(i > chunks)
        def _():
            cross_copy_d(i - chunks - 1).start()

        @between(3, i, chunks + 3)
        def _():
            feed_forward(i - 3)

        return carry

    ahead = 3
    lax.fori_loop(0, chunks + 4, step, 0)
    put_parts(d, r.parts_in, 0, r.acc_in)
    put_parts(d, r.parts_out, 0, r.acc_out)
    by_in, by_out = mlp_scatters(r) if merged else (None, None)

    def back_step(c, carry):
        @pl.when(c < chunks)
        def _():
            finish_grad(c)

        @pl.when(c + ahead < chunks)
        def _():
            cross_copy_d(c + ahead).start()

        if merged:
            trickle(by_in, c)
            trickle(by_out, c - d.outer)

        @between(1, c, chunks + 1)
        def _():
            send_mixed_grad(c - 1)

        @pl.when(c >= 3)
        def _():
            write_backward(c - 3)

        return carry

    lax.fori_loop(0, chunks + 3, back_step, 0)
    r.wo_send[...] = r.acc_write[1].astype(jnp.bfloat16)
    peer_grads(r).start()
    def pack(b, carry):
        here = block_at(d, b)[1]
        there = pl.ds(b * d.per, d.per)
        both = [r.grad_key[h, here, :] * SCALE for h in range(heads)]
        both += [r.grad_value[h, here, :] for h in range(heads)]
        wide = jnp.concatenate(both, axis=1).astype(jnp.bfloat16)
        r.grad_pairs[there] = wide.reshape(d.per, d.owned, 2 * d.column)
        return carry

    each_block(d, pack, 0)
    if not merged:
        finish_write_out(r)


def trickle(scatter, k):
    pl.when(jnp.logical_and(k >= 0, k < scatter.outer))(partial(scatter.start_block, k))
    pl.when(jnp.logical_and(k >= LAG, k < LAG + scatter.outer - 1))(partial(scatter.forward_block, k - LAG))


def put_parts(d, ref, at, value):
    width = value.shape[1]
    for b in range(d.tok_count):
        rows = slice(b * d.share, (b + 1) * d.share)
        ref[b // 2, b % 2, :, at : at + width] = value[rows, :].astype(jnp.bfloat16)


def back_phase(r, d, merged):
    chunks, heads, width, column, owned = d.chunks, d.heads, d.width, d.column, d.owned
    low, wide = jnp.bfloat16, jnp.float32
    core, side = chunk_core_side(r)
    other = 1 - core
    pairs = spread_of(r, d, "tok", lambda peer: r.grad_pairs.at[peer], r.got_pairs, r.pairs_sems)
    pairs.start()
    by_in, by_out = mlp_scatters(r)
    early = Scatter(r, r.parts_early, r.early_one, r.early_two, r.early_sems)
    later = Scatter(r, r.parts_second, r.second_one, r.second_two, r.second_sems)
    late = Scatter(r, r.parts_late, r.late_one, r.late_two, r.late_sems)
    final = Scatter(r, r.parts_final, r.final_one, r.final_two, r.final_sems)
    if not merged:
        by_in.start()
        by_out.start()
    first_f = chunks // 2
    for c in range(first_f):
        cross_f(r, c).start()
    r.acc_in[...] = jnp.zeros_like(r.acc_in)
    r.acc_out[...] = jnp.zeros_like(r.acc_out)
    at_key, at_value = slice(0, column), slice(256, 256 + column)

    def plain_weights(key, h, here, masks):
        scores = nn(key, r.read_query_t[head_rows(h), here]) * (SCALE * LOG2E)
        return jnp.exp2(add_rows(scores, masks))

    def masks_of(b, images):
        start, here = block_at(d, b)
        row_image = latent_row_image(r.counts, start, d.block)
        return [jnp.where(row_image == image, 0.0, MASKED) for image in images]

    def keep_weights(first, last):
        def keep(c, carry):
            masks = masks_of(0, token_images(r, d, c))
            top, low_rows = slice(0, 4 * SUB), slice(4 * SUB, 8 * SUB)
            for h in range(heads):
                weights = plain_weights(r.read_key[c, h], h, slice(0, d.block), masks).astype(low)
                if h == 0:
                    r.store[c, top, 0:512] = weights
                elif h == 1:
                    r.store[c, top, 512:768] = weights[:, 0:256]
                    r.store[c, low_rows, 0:256] = weights[:, 256:512]
                else:
                    r.store[c, low_rows, 256:768] = weights
            return carry

        if keeps_weights(d):
            lax.fori_loop(first, last, keep, 0)

    def kept_weights(c, h):
        top, low_rows = slice(0, 4 * SUB), slice(4 * SUB, 8 * SUB)
        if h == 0:
            return r.store[c, top, 0:512]
        if h == 1:
            return jnp.concatenate([r.store[c, top, 512:768], r.store[c, low_rows, 0:256]], axis=1)
        return r.store[c, low_rows, 256:768]

    def query_weights(c, carry):
        normed = norm_parts(chunk_rows(r.tokens, c).astype(wide))[0].astype(low)
        r.update[c] = normed.reshape(r.update.shape[1:])
        r.acc_in[:, :column] += tn(normed, r.grad_query_t[c].T)
        return carry

    lax.fori_loop(0, chunks, query_weights, 0)
    put_parts(d, r.parts_early, 0, r.acc_in[:, :column])
    keep_weights(0, chunks // 2)
    if merged:
        finish_write_out(r)
    put_parts(d, r.parts_early, column, r.grad_write)
    pairs.wait()
    early.start()
    if not merged:
        by_in.forward()
        by_out.forward()
    r.got_pairs[r.tok] = r.grad_pairs[r.tok]
    summed = sum_slots(r.got_pairs, d.tok_count).astype(low)
    grad_key, grad_value = summed[:, :column], summed[:, column:]
    r.head_parts[r.head] = (nn(grad_key, r.wkey[...]) + nn(grad_value, r.wvalue[...])).astype(low)
    moved = spread_of(r, d, "head", lambda peer: r.head_parts.at[r.head], r.head_parts, r.heads_sems)
    moved.start()
    keep_weights(chunks // 2, 3 * chunks // 4)
    normed_one, scale_one = norm_parts(r.lat_one[...])
    put_parts(d, r.parts_second, 0, tn(normed_one.astype(low), summed))
    moved.wait()
    grad_lat_one = norm_vjp(normed_one, scale_one, sum_slots(r.head_parts, d.head_count))
    r.grad_own[...] = grad_lat_one
    narrow = grad_lat_one.astype(low)
    grad_mixed = nt(narrow, r.rout[...]).astype(low)
    mixed = r.mixed[:, :column]
    product = grad_mixed.astype(wide) * mixed
    extra = []
    for h in range(heads):
        delta = jnp.sum(product[:, head_rows(h)], axis=1, keepdims=True)
        logs = r.mixed[:, column + h : column + h + 1]
        for k, (first, second) in enumerate(zip(split_three(delta), split_three(logs), strict=True)):
            extra.append((3 * h + k, first))
            extra.append((3 * (heads + h) + k, second))
    r.output_all[r.tok, :, :column] = grad_mixed
    r.output_all[r.tok, :, column:] = pick_lanes((owned, d.packed - column), extra).astype(low)
    outputs = spread_of(r, d, "tok", lambda peer: r.output_all.at[r.tok], r.output_all, r.output_sems)
    outputs.start()
    put_parts(d, r.parts_second, 2 * column, tn(narrow, mixed.astype(low)))
    r.query_sum[...] = jnp.zeros_like(r.query_sum)
    keep_weights(3 * chunks // 4, chunks)
    outputs.wait()
    early.forward()

    def turn(b, carry):
        here = block_at(d, b)[1]
        turned = r.output_all[pl.ds(b * d.per, d.per)].reshape(d.block, d.packed).astype(wide).T
        def joined(k):
            at = column + 3 * k
            return turned[at : at + 1] + turned[at + 1 : at + 2] + turned[at + 2 : at + 3]

        for h in range(heads):
            inverse = jnp.exp2(joined(heads + h))
            r.output_t[head_rows(h), here] = (turned[head_rows(h)] * inverse).astype(low)
            r.rows[h : h + 1, here] = joined(h) * inverse
        return carry

    each_block(d, turn, 0)

    def key_grads(count, weights_of, value_of, key_t_of, images):
        def body(b, carry):
            here = block_at(d, b)[1]
            masks = masks_of(b, images)
            kept = []
            for h in range(heads):
                hr = head_rows(h)
                query, output = r.read_query_t[hr, here], r.output_t[hr, here]
                weights = weights_of(h, here, masks)
                grad_weights = nn(value_of(h), output) - r.rows[h : h + 1, here]
                grad_scores = (weights.astype(wide) * grad_weights).astype(low)
                r.query_sum[hr, here] += nn(key_t_of(h), grad_scores)
                kept.append(
                    (carry[h][0] + nt(grad_scores, query), carry[h][1] + nt(weights.astype(low), output))
                )
            return tuple(kept)

        zero = jnp.zeros((count, HD), wide)
        grads = each_block(d, body, ((zero, zero),) * heads)
        keys = jnp.concatenate([grads[h][0] for h in range(heads)], axis=1) * SCALE
        values = jnp.concatenate([grads[h][1] for h in range(heads)], axis=1)
        return keys.astype(low), values.astype(low)

    def core_copy(c):
        slot = lax.rem(c, 2)
        return pltpu.make_async_remote_copy(
            src_ref=r.send_f,
            dst_ref=r.got_f.at[slot],
            send_sem=r.core_sems.at[0, slot],
            recv_sem=r.core_sems.at[1, slot],
            device_id=(r.tok, side * 2 + other),
            device_id_type=MESH,
        )

    def cross_copy(c):
        return pltpu.make_async_remote_copy(
            src_ref=r.x_half.at[c, 1 - side],
            dst_ref=r.x_cross.at[c],
            send_sem=r.x_sems.at[0, c],
            recv_sem=r.x_sems.at[1, c],
            device_id=(r.tok, (1 - side) * 2 + core),
            device_id_type=MESH,
        )

    def compute(c):
        def weights_of(h, here, masks):
            return kept_weights(c, h) if keeps_weights(d) else plain_weights(r.read_key[c, h], h, here, masks)

        dk, dv = key_grads(
            4 * SUB,
            weights_of,
            lambda h: r.read_value[c, h],
            lambda h: r.read_key_t[c, head_rows(h), :],
            token_images(r, d, c),
        )
        moved = nn(dk, r.rkey[...]) + nn(dv, r.rvalue[...]) + tn(r.grad_query_t[c], r.wquery[...])
        halve(r, moved, r.own_f, r.send_f)
        core_copy(c).start()
        normed = r.update[c].reshape(4 * SUB, width)
        r.acc_out[:, at_key] += tn(normed, dk)
        r.acc_out[:, at_value] += tn(normed, dv)

    def cross(c):
        core_copy(c).wait()
        total = r.own_f[...] + r.got_f[lax.rem(c, 2)].astype(wide)
        r.x_half[c] = total.astype(low)
        cross_copy(c).start()

    def step(c, carry):
        @pl.when(c >= 1)
        def _():
            cross(c - 1)

        @pl.when(c >= first_f)
        def _():
            cross_f(r, c).start()

        compute(c)
        if few:
            trickle(later, c)
        return carry

    few = d.outer + LAG <= chunks
    if not few:
        later.start()
        later.forward()
    lax.fori_loop(0, chunks // 2, step, 0)
    lax.fori_loop(chunks // 2, chunks, step, 0)
    own_dk, own_dv = key_grads(
        owned,
        lambda h, here, masks: plain_weights(r.own_key[h], h, here, masks),
        lambda h: r.own_value[h],
        lambda h: r.own_key_t[head_rows(h), :],
        [image_of(r.counts, r.tok * d.groups_here + g) for g in range(d.groups_here)],
    )

    def turn_query(b, carry):
        here = block_at(d, b)[1]
        turned = (r.query_sum[:, here] * SCALE).T.astype(low)
        r.query_send[pl.ds(b * d.per, d.per)] = turned.reshape(d.per, owned, column)
        return carry

    each_block(d, turn_query, 0)
    queries = spread_of(r, d, "tok", lambda peer: r.query_send.at[peer], r.query_got, r.back_query_sems)
    queries.start()
    cross(chunks - 1)
    normed_lat, scale_lat = norm_parts(r.latents[...].astype(wide))
    narrow_lat = normed_lat.astype(low)
    put_parts(d, r.parts_late, 0, r.acc_out[:, at_key] + tn(narrow_lat, own_dk))
    put_parts(d, r.parts_late, column, r.acc_out[:, at_value] + tn(narrow_lat, own_dv))
    late.start()
    queries.wait()
    r.query_got[r.tok] = r.query_send[r.tok]
    grad_query = sum_slots(r.query_got, d.tok_count).astype(low)
    lat_total = nn(grad_query, r.rquery[...]) + nn(own_dk, r.rkey[...]) + nn(own_dv, r.rvalue[...])
    r.lat_parts[...] = lat_total.astype(low).reshape(r.lat_parts.shape)
    lats = spread_of(r, d, "head", lambda peer: r.lat_parts.at[peer], r.lat_got, r.lat_sems)
    lats.start()
    put_parts(d, r.parts_final, 0, tn(narrow_lat, grad_query))
    final.start()
    late.forward()
    by_in.finish()
    final.forward()
    lats.wait()
    r.lat_got[r.head] = r.lat_parts[r.head]
    total = sum_slots(r.lat_got, d.head_count)
    count = owned // d.head_count
    mine = pl.ds(pl.multiple_of(r.head * count, count), count)
    normed, scale = norm_parts(r.latents[mine, :].astype(wide))
    r.lat_grad[...] = r.grad_own[mine, :] + norm_vjp(normed, scale, total)
    by_out.finish()
    early.finish()
    later.finish()

    def wait_cross(c, carry):
        cross_copy(c).wait()
        cross_f(r, c).wait()
        return carry

    lax.fori_loop(0, chunks, wait_cross, 0)
    late.finish()
    final.finish()


FRONT, MIDDLE, BACK = 1, 2, 4
OWN, CARRY, OUT = 0, 1, 2


def keeps_weights(d):
    return d.blocks == 1 and d.heads * d.block == 2 * d.width and d.chunks == 8 and d.quarter == 8 * SUB


def buffers(d):
    low, wide = jnp.bfloat16, jnp.float32
    size, half = 4 * SUB, (2, SUB, d.width)
    n, h = d.tok_count, d.head_count
    front, middle, back = FRONT, MIDDLE, BACK
    every = front | middle | back
    by_chunk = (d.chunks, d.column, size)
    by_head, by_column = (d.heads, d.latent_count, HD), (d.column, d.latent_count)
    key_heads, own_heads = (d.chunks, d.heads, size, HD), (d.heads, d.owned, HD)
    pairs, queries, wide_rows = (n, d.owned, 2 * d.column), (n, d.owned, d.column), (n, d.owned, d.packed)
    halves, quarters = (d.chunks, 2, SUB, d.width), (d.chunks, SUB, d.width)
    tok_sems, head_sems, sum_sems = (2, n), (2, h), (4, d.outer)

    def slots(columns):
        return (d.outer, d.share, columns)

    def parts(columns):
        return (d.outer, 2, d.share, columns)

    return dict(
        query_t=(by_chunk, low, front | middle, CARRY),
        key=(by_head, low, front | middle, CARRY),
        value=(by_head, low, front | middle, CARRY),
        key_t=(by_column, low, front | middle, CARRY),
        value_t=(by_column, low, front | middle, CARRY),
        read_key=(key_heads, low, front | back, CARRY),
        read_value=(key_heads, low, front | back, CARRY),
        read_key_t=(by_chunk, low, front | back, CARRY),
        read_value_t=(by_chunk, low, front, OWN),
        own_key=(own_heads, low, front | back, CARRY),
        own_value=(own_heads, low, front | back, CARRY),
        own_key_t=((d.column, d.owned), low, front | back, CARRY),
        own_value_t=((d.column, d.owned), low, front, OWN),
        read_query_t=(by_column, low, front | back, CARRY),
        lat_one=((d.owned, d.width), wide, front | back, CARRY),
        mixed=((d.owned, d.packed), wide, front | back, CARRY),
        update=((d.chunks, 2, 2, SUB, d.width), low, every, OWN),
        query_all=(queries, low, front, OWN),
        sums=((d.packed, d.latent_count), wide, front, OWN),
        sums_send=(wide_rows, low, front, OWN),
        sums_got=(wide_rows, low, front, OWN),
        head_parts=((h, d.owned, d.width), low, front | back, OWN),
        pair_all=(pairs, low, front, OWN),
        query_sems=(tok_sems, None, front, OWN),
        sums_sems=(tok_sems, None, front, OWN),
        head_sems=(head_sems, None, front, OWN),
        pair_sems=(tok_sems, None, front, OWN),
        grad_one=((d.quarter, d.width), wide, middle, OUT),
        grad_query_t=(by_chunk, low, middle | back, CARRY),
        grad_pairs=(pairs, low, middle | back, CARRY),
        parts_in=(parts(d.hidden), low, middle | back, CARRY),
        parts_out=(parts(d.hidden), low, middle | back, CARRY),
        grad_write=((d.width, d.column), low, middle | back, CARRY),
        f_half=(halves, low, middle | back, OUT),
        write_out=((d.column, d.width), low, middle, OWN),
        mlp_in=((d.width, d.hidden), low, middle, OWN),
        mlp_out=((d.hidden, d.width), low, middle, OWN),
        store=((8, d.quarter, d.width), low, middle | back if keeps_weights(d) else middle, OWN),
        mixed_t=((d.chunks, 2, d.column, 2 * SUB), low, middle, OWN),
        log_total=((d.chunks, 8, size), wide, middle, OWN),
        send_a=((SUB, d.width), low, middle, OWN),
        got_a=(half, low, middle, OWN),
        part_s=(half, wide, middle, OWN),
        mixed_got=((d.chunks, d.column, 2 * SUB), low, middle, OWN),
        grad_mixed_t=((d.chunks, 2, d.column, 2 * SUB), low, middle, OWN),
        mixed_send=((4, d.column, 2 * SUB), low, middle, OWN),
        narrow_s=((4, *half), low, middle, OWN),
        wo_peer=((d.column, d.width), low, middle, OWN),
        wo_send=((d.column, d.width), low, middle, OWN),
        wo_got=((d.column, d.width), low, middle, OWN),
        own_d=(half, wide, middle, OWN),
        send_d=(half, low, middle, OWN),
        got_d=((2, *half), low, middle, OWN),
        own_f=(half, wide, middle | back, OWN),
        send_f=(half, low, middle | back, OWN),
        got_f=((2, *half), low, middle | back, OWN),
        acc_in=((d.width, d.hidden), wide, middle | back, OWN),
        acc_out=((d.width, d.hidden), wide, middle | back, OWN),
        acc_write=((2, d.column, d.width), wide, middle, OWN),
        normed_s=((size, d.width), low, middle, OWN),
        act_s=((size, d.hidden), low, middle, OWN),
        inner_s=((size, d.hidden), low, middle, OWN),
        wide_s=((2, *half), wide, middle | back, OWN),
        latent_image=((d.block, 128), jnp.int32, middle, OWN),
        grad_key=(by_head, wide, middle, OWN),
        grad_value=(by_head, wide, middle, OWN),
        send_sems=((12, d.chunks), None, middle, OWN),
        recv_sems=((12, d.chunks), None, middle, OWN),
        load_sems=((4,), None, middle, OWN),
        f_cross=(quarters, low, back, OUT),
        x_half=(halves, low, back, OUT),
        x_cross=(quarters, low, back, OUT),
        in_two=(slots(d.hidden), low, back, OUT),
        out_two=(slots(d.hidden), low, back, OUT),
        early_two=(slots(2 * d.column), low, back, OUT),
        second_two=(slots(3 * d.column), low, back, OUT),
        late_two=(slots(2 * d.column), low, back, OUT),
        final_two=(slots(d.column), low, back, OUT),
        lat_grad=((d.owned // h, d.width), wide, back, OUT),
        in_one=(slots(d.hidden), low, back, OWN),
        out_one=(slots(d.hidden), low, back, OWN),
        early_one=(slots(2 * d.column), low, back, OWN),
        second_one=(slots(3 * d.column), low, back, OWN),
        late_one=(slots(2 * d.column), low, back, OWN),
        final_one=(slots(d.column), low, back, OWN),
        parts_early=(parts(2 * d.column), low, back, OWN),
        parts_second=(parts(3 * d.column), low, back, OWN),
        parts_late=(parts(2 * d.column), low, back, OWN),
        parts_final=(parts(d.column), low, back, OWN),
        got_pairs=(pairs, low, back, OWN),
        output_all=(wide_rows, low, back, OWN),
        output_t=(by_column, low, back, OWN),
        rows=((8, d.latent_count), wide, back, OWN),
        grad_own=((d.owned, d.width), wide, back, OWN),
        query_sum=(by_column, wide, back, OWN),
        query_send=(queries, low, back, OWN),
        query_got=(queries, low, back, OWN),
        lat_parts=((h, d.owned // h, d.width), low, back, OWN),
        lat_got=((h, d.owned // h, d.width), low, back, OWN),
        in_sems=(sum_sems, None, back, OWN),
        out_sems=(sum_sems, None, back, OWN),
        early_sems=(sum_sems, None, back, OWN),
        second_sems=(sum_sems, None, back, OWN),
        late_sems=(sum_sems, None, back, OWN),
        final_sems=(sum_sems, None, back, OWN),
        pairs_sems=(tok_sems, None, back, OWN),
        heads_sems=(head_sems, None, back, OWN),
        output_sems=(tok_sems, None, back, OWN),
        back_query_sems=(tok_sems, None, back, OWN),
        lat_sems=(head_sems, None, back, OWN),
        core_sems=((2, 2), None, back, OWN),
        x_sems=((2, d.chunks), None, back, OWN),
        f_sems=((2, d.chunks), None, back, OWN),
    )


def run(d, number, phases, inputs, made):
    table = buffers(d)
    later = (FRONT | MIDDLE | BACK) & ~(2 * phases - 1) if phases != FRONT | MIDDLE | BACK else 0
    given = {x: (array, memory) for x, (array, uses, memory) in inputs.items() if uses & phases}
    given |= {x: (made[x], pltpu.VMEM) for x in made if table[x][2] & phases}
    wanted, inside = [], []
    for x, (shape, kind, uses, keep) in table.items():
        if x in given or not uses & phases:
            continue
        (wanted if keep == OUT or (keep == CARRY and uses & later) else inside).append(x)
    names = [*given, *wanted, *inside]
    merged = phases == FRONT | MIDDLE | BACK

    def kernel(*refs):
        r = SimpleNamespace(**dict(zip(names, refs, strict=True)))
        r.tok, r.head = lax.axis_index("tok"), lax.axis_index("head")
        if phases & MIDDLE:
            for k in range(4):
                load(r, k).start()
        if not phases & FRONT:
            greet_all(r, d)
        if phases & FRONT:
            front_phase(r, d, merged)
        if phases & MIDDLE:
            middle_phase(r, d, merged)
        if phases & BACK:
            back_phase(r, d, merged)

    def scratch(x):
        shape, kind = table[x][:2]
        return pltpu.SemaphoreType.DMA(shape) if kind is None else pltpu.VMEM(shape, kind)

    out = pl.pallas_call(
        kernel,
        out_shape=[jax.ShapeDtypeStruct(*table[x][:2]) for x in wanted],
        in_specs=[pl.BlockSpec(memory_space=memory) for array, memory in given.values()],
        out_specs=[pl.BlockSpec(memory_space=pltpu.VMEM) for x in wanted],
        scratch_shapes=[scratch(x) for x in inside],
        compiler_params=pltpu.CompilerParams(
            collective_id=number, has_side_effects=True, vmem_limit_bytes=127 << 19
        ),
        name="phases%d" % phases,
    )(*[array for array, memory in given.values()])
    return dict(zip(wanted, out, strict=True))


def finish_kernel(
    index, tokens, grad_one, f_own, f_cross, x_own, x_cross, in_two, out_two, early_two, early_all, second_two, second_all, late_two, final_two, lat,
    layer_out, input_grad, latent_grad, g_rquery, g_rkey, g_rvalue, g_rout, g_wquery, g_wkey, g_wvalue, g_wout,
    g_in, g_out,
):
    wide = jnp.float32
    column = final_two.shape[2]
    rows, width = grad_one.shape

    def both(own, cross):
        return (own[...].astype(wide).reshape(rows, width)) + cross[...].astype(wide).reshape(rows, width)

    layer_out[...] = both(f_own, f_cross).astype(jnp.bfloat16)
    normed, scale = norm_parts(tokens[0].astype(wide))
    input_grad[...] = grad_one[...] + norm_vjp(normed, scale, both(x_own, x_cross))
    latent_grad[...] = lat[...]

    def total(ref):
        kept = ref[0].astype(wide)
        for s in range(1, ref.shape[0]):
            kept = kept + ref[s].astype(wide)
        return kept

    g_in[...] = total(in_two)
    g_out[...] = total(out_two)
    g_rquery[...] = total(final_two)
    late = total(late_two)
    g_rkey[...] = late[:, :column]
    g_rvalue[...] = late[:, column:]
    g_wquery[...] = total(early_two)[:, :column]
    second = total(second_two)
    g_wkey[...] = second[:, :column]
    g_wvalue[...] = second[:, column : 2 * column]

    @pl.when(pl.program_id(0) == 0)
    def _():
        g_wout[...] = total(early_all)[:, column:].T
        g_rout[...] = total(second_all)[:, 2 * column :].T


def finish(d, tokens, m):
    steps = 2 if d.share % 32 == 0 else 1
    rows, share, parts = d.quarter // steps, d.share // steps, d.chunks // steps
    head = lax.axis_index("head")
    index = jnp.stack([head, head // 2]).astype(jnp.int32)
    half = pl.BlockSpec((parts, None, SUB, d.width), lambda i, at: (i, at[1], 0, 0))
    cross = pl.BlockSpec((parts, SUB, d.width), lambda i, at: (i, 0, 0))
    strip = pl.BlockSpec((rows, d.width), lambda i, at: (i, 0))
    whole = pl.BlockSpec((d.owned // d.head_count, d.width), lambda i, at: (0, 0))

    def slots(columns):
        return pl.BlockSpec((d.outer, share, columns), lambda i, at: (0, i, 0))

    def part(columns):
        return pl.BlockSpec((share, columns), lambda i, at: (i, 0))

    wide, column = jnp.float32, d.column
    grads = [column] * 8 + [d.hidden] * 2
    turned = (column, d.share)
    return pl.pallas_call(
        finish_kernel,
        out_shape=[
            jax.ShapeDtypeStruct((d.quarter, d.width), jnp.bfloat16),
            jax.ShapeDtypeStruct((d.quarter, d.width), wide),
            jax.ShapeDtypeStruct((d.owned // d.head_count, d.width), wide),
            *[jax.ShapeDtypeStruct(turned if k in (3, 7) else (d.share, columns), wide) for k, columns in enumerate(grads)],
        ],
        grid_spec=pltpu.PrefetchScalarGridSpec(
            num_scalar_prefetch=1,
            grid=(steps,),
            in_specs=[
                pl.BlockSpec((1, rows, d.width), lambda i, at: (at[0], i, 0)),
                strip,
                half,
                cross,
                half,
                cross,
                slots(d.hidden),
                slots(d.hidden),
                slots(2 * column),
                pl.BlockSpec((d.outer, d.share, 2 * column), lambda i, at: (0, 0, 0)),
                slots(3 * column),
                pl.BlockSpec((d.outer, d.share, 3 * column), lambda i, at: (0, 0, 0)),
                slots(2 * column),
                slots(column),
                whole,
            ],
            out_specs=[
                strip,
                strip,
                whole,
                *[
                    pl.BlockSpec(turned, lambda i, at: (0, 0)) if k in (3, 7) else part(columns)
                    for k, columns in enumerate(grads)
                ],
            ],
        ),
        compiler_params=pltpu.CompilerParams(vmem_limit_bytes=62 << 20),
        name="finish",
    )(
        index, tokens, m.grad_one, m.f_half, m.f_cross, m.x_half, m.x_cross, m.in_two, m.out_two, m.early_two,
        m.early_two, m.second_two, m.second_two, m.late_two, m.final_two, m.lat_grad,
    )


def shards(
    tokens,
    latents,
    image_groups,
    read_query,
    read_key,
    read_value,
    read_out,
    write_query,
    write_key,
    write_value,
    write_out,
    mlp_in,
    mlp_out,
    cotangent,
):
    d = SimpleNamespace(tok_count=lax.axis_size("tok"), head_count=lax.axis_size("head"))
    rows, d.width = tokens.shape
    d.owned, d.column, d.hidden, d.packed = latents.shape[0], read_query.shape[1], mlp_in.shape[1], 256
    d.heads, d.quarter, d.groups_here = d.column // HD, rows // 4, rows // GROUP
    d.chunks, d.latent_count = d.quarter // SUB, d.owned * d.tok_count
    d.block = min(512, d.latent_count)
    d.blocks, d.per = d.latent_count // d.block, d.block // d.owned
    d.outer, d.share = d.tok_count // 2, d.width // d.tok_count
    tokens = tokens.reshape(4, d.quarter, d.width)
    every, vmem = FRONT | MIDDLE | BACK, pltpu.VMEM
    inputs = dict(
        counts=(image_groups, every, pltpu.SMEM),
        tokens=(tokens, every, vmem),
        latents=(latents, FRONT | BACK, vmem),
        rquery=(read_query.T, FRONT | BACK, vmem),
        rkey=(read_key.T, FRONT | BACK, vmem),
        rvalue=(read_value.T, FRONT | BACK, vmem),
        rout=(read_out, FRONT | BACK, vmem),
        wquery=(write_query.T, FRONT | BACK, vmem),
        wkey=(write_key.T, FRONT | BACK, vmem),
        wvalue=(write_value.T, FRONT | BACK, vmem),
        write_out_hbm=(write_out, MIDDLE, pl.ANY),
        mlp_in_hbm=(mlp_in, MIDDLE, pl.ANY),
        mlp_out_hbm=(mlp_out, MIDDLE, pl.ANY),
        cotangent_hbm=(cotangent.reshape(4, d.quarter, d.width), MIDDLE, pl.ANY),
    )
    made = {}
    for number, phases in enumerate([every] if d.latent_count <= 512 else [FRONT, MIDDLE, BACK]):
        made |= run(d, number, phases, inputs, made)
    (
        layer_out, input_grad, latent_grad, g_rquery, g_rkey, g_rvalue, g_rout, g_wquery, g_wkey, g_wvalue, g_wout,
        g_in, g_out,
    ) = finish(d, tokens, SimpleNamespace(**made))
    return (
        layer_out,
        input_grad,
        latent_grad,
        g_rquery,
        g_rkey,
        g_rvalue,
        g_rout,
        g_wquery,
        g_wkey,
        g_wvalue,
        g_wout,
        g_in,
        g_out.T,
    )


def solution(mesh):
    return jax.shard_map(
        shards,
        mesh=mesh,
        in_specs=(
            P("tok", None),
            P("tok", None),
            P(),
            P(None, "head"),
            P(None, "head"),
            P(None, "head"),
            P("head", None),
            P(None, "head"),
            P(None, "head"),
            P(None, "head"),
            P("head", None),
            P(None, "head"),
            P("head", None),
            P("tok", None),
        ),
        out_specs=(
            P(("tok", "head"), None),
            P(("tok", "head"), None),
            P(("tok", "head"), None),
            P("tok", "head"),
            P("tok", "head"),
            P("tok", "head"),
            P("head", "tok"),
            P("tok", "head"),
            P("tok", "head"),
            P("tok", "head"),
            P("head", "tok"),
            P("tok", "head"),
            P("head", "tok"),
        ),
        check_vma=False,
    )
```

```python
from functools import partial
from types import SimpleNamespace

import jax
import jax.numpy as jnp
from jax import lax
from jax.experimental import pallas as pl
from jax.experimental.pallas import tpu as pltpu
from jax.sharding import PartitionSpec as P

MESH = pl.DeviceIdType.MESH
HD = 64
GROUP = 256
LPG = 8
epsilon = 1e-05
SUB = 64
SCALE = 0.125
LOG2E = 1.4426950408889634
MASKED = -1e30
GELU_A = 0.7978845608028654
GELU_B = 0.044715
LAG = 2
WRITES = 3


def nn(left, right):
    return lax.dot_general(left, right, (((1,), (0,)), ((), ())), preferred_element_type=jnp.float32)


def nt(left, right):
    return lax.dot_general(left, right, (((1,), (1,)), ((), ())), preferred_element_type=jnp.float32)


def tn(left, right):
    return lax.dot_general(left, right, (((0,), (0,)), ((), ())), preferred_element_type=jnp.float32)


def norm_parts(values):
    center = values - jnp.mean(values, axis=-1, keepdims=True)
    scale = lax.rsqrt(jnp.mean(center * center, axis=-1, keepdims=True) + epsilon)
    return center * scale, scale


def norm_vjp(normed, scale, grad):
    return scale * (
        grad
        - jnp.mean(grad, axis=-1, keepdims=True)
        - normed * jnp.mean(grad * normed, axis=-1, keepdims=True)
    )


def image_of(counts, group):
    bound = jnp.int32(0)
    image = jnp.zeros_like(group)
    for m in range(counts.shape[0]):
        bound = bound + counts[m]
        image = image + jnp.where(bound <= group, 1, 0)
    return image


def latent_row_image(counts, start, count):
    group = lax.shift_right_logical(lax.broadcasted_iota(jnp.int32, (1, count), 1) + start, 3)
    return image_of(counts, group)


def head_rows(h):
    return slice(h * HD, (h + 1) * HD)


def chunk_rows(ref, c):
    part = pl.ds(pl.multiple_of(c * SUB, SUB), SUB)
    return jnp.concatenate([ref[q, part, :] for q in range(4)], axis=0)


def greet_all(r, d):
    barrier = pltpu.get_barrier_semaphore()

    def greet(step, carry):
        peer = lax.rem(r.tok + step, d.tok_count)
        pl.semaphore_signal(barrier, inc=1, device_id=(peer, r.head), device_id_type=MESH)
        return carry

    lax.fori_loop(1, d.tok_count, greet, 0)
    for step in range(1, d.head_count):
        peer = lax.rem(r.head + step, d.head_count)
        pl.semaphore_signal(barrier, inc=1, device_id=(r.tok, peer), device_id_type=MESH)
    pl.semaphore_wait(barrier, d.tok_count + d.head_count - 2)


class Spread:
    def __init__(self, axis, tok, head, count, source, got, sems):
        self.axis, self.tok, self.head, self.count = axis, tok, head, count
        self.me = tok if axis == "tok" else head
        self.source, self.got, self.sems = source, got, sems

    def copy(self, peer, slot):
        return pltpu.make_async_remote_copy(
            src_ref=self.source(peer),
            dst_ref=self.got.at[slot],
            send_sem=self.sems.at[0, peer],
            recv_sem=self.sems.at[1, slot],
            device_id=(peer, self.head) if self.axis == "tok" else (self.tok, peer),
            device_id_type=MESH,
        )

    def start(self):
        def go(step, carry):
            self.copy(lax.rem(self.me + step, self.count), self.me).start()
            return carry

        lax.fori_loop(1, self.count, go, 0)

    def wait(self):
        def go(step, carry):
            peer = lax.rem(self.me + step, self.count)
            self.copy(peer, peer).wait()
            return carry

        lax.fori_loop(1, self.count, go, 0)


class Scatter:
    def __init__(self, r, parts, got_one, got_two, sems):
        self.head, self.mine, self.side = r.head, r.tok // 2, lax.rem(r.tok, 2)
        self.parts, self.got_one, self.got_two, self.sems = parts, got_one, got_two, sems
        self.outer = parts.shape[0]

    def first(self, block):
        return pltpu.make_async_remote_copy(
            src_ref=self.parts.at[block, 1 - self.side],
            dst_ref=self.got_one.at[block],
            send_sem=self.sems.at[0, block],
            recv_sem=self.sems.at[1, block],
            device_id=(self.mine * 2 + (1 - self.side), self.head),
            device_id_type=MESH,
        )

    def second(self, block, source):
        return pltpu.make_async_remote_copy(
            src_ref=self.got_one.at[block],
            dst_ref=self.got_two.at[source],
            send_sem=self.sems.at[2, block],
            recv_sem=self.sems.at[3, source],
            device_id=(block * 2 + self.side, self.head),
            device_id_type=MESH,
        )

    def start_block(self, k):
        self.first(lax.rem(self.mine + k + 1, self.outer)).start()

    def forward_block(self, k):
        block = lax.rem(self.mine + k + 1, self.outer)
        self.got_one[block] = self.total(block)
        self.second(block, self.mine).start()

    def start(self):
        def go(k, carry):
            self.start_block(k)
            return carry

        lax.fori_loop(0, self.outer, go, 0)

    def total(self, block):
        self.first(block).wait()
        both = self.parts[block, self.side].astype(jnp.float32) + self.got_one[block].astype(jnp.float32)
        return both.astype(jnp.bfloat16)

    def forward(self):
        def go(k, carry):
            self.forward_block(k)
            return carry

        lax.fori_loop(0, self.outer - 1, go, 0)

    def finish(self):
        self.got_two[self.mine] = self.total(self.mine)

        def go(step, carry):
            peer = lax.rem(self.mine + step, self.outer)
            self.second(peer, peer).wait()
            return carry

        lax.fori_loop(1, self.outer, go, 0)


def split_three(value):
    high = value.astype(jnp.bfloat16).astype(jnp.float32)
    rest = value - high
    middle_part = rest.astype(jnp.bfloat16).astype(jnp.float32)
    return high, middle_part, rest - middle_part


def pick_lanes(shape, columns):
    lane = lax.broadcasted_iota(jnp.int32, shape, 1)
    value = jnp.zeros(shape, jnp.float32)
    for at, column in columns:
        value = jnp.where(lane == at, column, value)
    return value


def by_head(shape, columns):
    lane = lax.broadcasted_iota(jnp.int32, shape, 1)
    value = jnp.broadcast_to(columns[-1], shape)
    for h in range(len(columns) - 2, -1, -1):
        value = jnp.where(lane < (h + 1) * HD, columns[h], value)
    return value


def add_rows(values, rows):
    count = values.shape[0] // len(rows)
    return jnp.concatenate([values[k * count : (k + 1) * count] + row for k, row in enumerate(rows)], axis=0)


def token_images(r, d, c):
    return [
        image_of(r.counts, r.tok * d.groups_here + (q * d.quarter + c * SUB) // GROUP) for q in range(4)
    ]


def spread_of(r, d, axis, source, got, sems):
    count = d.tok_count if axis == "tok" else d.head_count
    return Spread(axis, r.tok, r.head, count, source, got, sems)


def sum_slots(ref, count):
    first = ref[0].astype(jnp.float32)
    return lax.fori_loop(1, count, lambda s, kept: kept + ref[s].astype(jnp.float32), first)


def each_block(d, body, carry):
    if d.blocks == 1:
        return body(0, carry)
    return lax.fori_loop(0, d.blocks, lambda b, kept: body(b, kept), carry)


def block_at(d, b):
    start = b * d.block if d.blocks == 1 else pl.multiple_of(b * d.block, d.block)
    return start, pl.ds(start, d.block)


def keep_heads(ref, wide, heads):
    for h in range(heads):
        ref[h] = wide[:, head_rows(h)]


def chunk_core_side(r):
    return lax.rem(r.head, 2), r.head // 2


def load(r, k):
    source = (r.write_out_hbm, r.mlp_in_hbm, r.mlp_out_hbm, r.cotangent_hbm)[k]
    target = (r.write_out, r.mlp_in, r.mlp_out, r.store.at[0:4])[k]
    return pltpu.make_async_copy(source, target, r.load_sems.at[k])


def peer_of(r, across):
    core, side = chunk_core_side(r)
    return (r.tok, (1 - side) * 2 + core if across else side * 2 + 1 - core)


def middle_copy(r, kind, chunk, source, target, across):
    return pltpu.make_async_remote_copy(
        src_ref=source,
        dst_ref=target,
        send_sem=r.send_sems.at[kind, chunk],
        recv_sem=r.recv_sems.at[kind, chunk],
        device_id=peer_of(r, across),
        device_id_type=MESH,
    )


def peer_weights(r):
    return middle_copy(r, 10, 0, r.write_out, r.wo_peer, True)


def peer_grads(r):
    return middle_copy(r, 11, 0, r.wo_send, r.wo_got, True)


def finish_write_out(r):
    peer_grads(r).wait()
    total = r.acc_write[0] + r.wo_got[...].astype(jnp.float32)
    r.grad_write[...] = total.T.astype(jnp.bfloat16)


def halve(r, wide, own, send):
    core = chunk_core_side(r)[0]
    r.wide_s[...] = wide.reshape(r.wide_s.shape)
    for x in range(2):
        own[x] = r.wide_s[x, core]
        send[x] = r.wide_s[x, 1 - core].astype(jnp.bfloat16)


def front_phase(r, d, merged):
    low = jnp.bfloat16
    heads, column, chunks, owned = d.heads, d.column, d.chunks, d.owned
    latents_wide = r.latents[...].astype(jnp.float32)
    normed_lat = norm_parts(latents_wide)[0].astype(low)
    r.query_all[r.tok] = nt(normed_lat, r.rquery[...]).astype(low)
    greet_all(r, d)
    queries = spread_of(r, d, "tok", lambda peer: r.query_all.at[r.tok], r.query_all, r.query_sems)
    queries.start()
    for copy in r.pending:
        copy.wait()
    keys = nt(normed_lat, r.rkey[...]).astype(low)
    values = nt(normed_lat, r.rvalue[...]).astype(low)
    keep_heads(r.own_key, keys, heads)
    keep_heads(r.own_value, values, heads)
    r.own_key_t[...] = keys.T
    r.own_value_t[...] = values.T

    def project(c, carry):
        normed = norm_parts(chunk_rows(r.tokens, c).astype(jnp.float32))[0].astype(low)
        r.update[c] = normed.reshape(r.update.shape[1:])
        keys = nt(normed, r.rkey[...]).astype(low)
        values = nt(normed, r.rvalue[...]).astype(low)
        keep_heads(r.read_key.at[c], keys, heads)
        keep_heads(r.read_value.at[c], values, heads)
        r.read_key_t[c] = keys.T
        r.read_value_t[c] = values.T
        return carry

    lax.fori_loop(0, chunks, project, 0)
    if merged:
        load(r, 0).wait()
        peer_weights(r).start()
    r.sums[...] = jnp.zeros_like(r.sums)
    queries.wait()

    def attend(scores, rows, values_t, here, h):
        weights = jnp.exp2(add_rows(scores * (SCALE * LOG2E), rows))
        r.sums[column + h : column + h + 1, here] += jnp.sum(weights, axis=0, keepdims=True)
        r.sums[head_rows(h), here] += nn(values_t, weights.astype(low))

    def read_block(b, carry):
        start, here = block_at(d, b)
        query = r.query_all[pl.ds(b * d.per, d.per)].reshape(d.block, column).T
        r.read_query_t[:, here] = query
        row_image = latent_row_image(r.counts, start, d.block)

        def masks(images):
            return [jnp.where(row_image == image, 0.0, MASKED) for image in images]

        def read_chunk(c, carry):
            rows = masks(token_images(r, d, c))
            for h in range(heads):
                attend(nn(r.read_key[c, h], query[head_rows(h)]), rows, r.read_value_t[c, head_rows(h)], here, h)
            return carry

        lax.fori_loop(0, chunks, read_chunk, 0)
        rows = masks([image_of(r.counts, r.tok * d.groups_here + g) for g in range(d.groups_here)])
        for h in range(heads):
            attend(nn(r.own_key[h], query[head_rows(h)]), rows, r.own_value_t[head_rows(h), :], here, h)
        total = r.sums[column : column + heads, here]
        high = total.astype(low).astype(jnp.float32)
        r.sums[column : column + heads, here] = high
        r.sums[column + heads : column + 2 * heads, here] = total - high
        r.sums_send[pl.ds(b * d.per, d.per)] = r.sums[:, here].T.astype(low).reshape(d.per, owned, d.packed)
        return carry

    each_block(d, read_block, 0)
    totals = spread_of(r, d, "tok", lambda peer: r.sums_send.at[peer], r.sums_got, r.sums_sems)
    totals.start()

    def project_query(c, carry):
        r.query_t[c] = nt(r.wquery[...], r.update[c].reshape(4 * SUB, d.width)).astype(low)
        return carry

    lax.fori_loop(0, chunks, project_query, 0)
    totals.wait()
    r.sums_got[r.tok] = r.sums_send[r.tok]
    summed = sum_slots(r.sums_got, d.tok_count)
    whole = [
        summed[:, column + h : column + h + 1] + summed[:, column + heads + h : column + heads + h + 1]
        for h in range(heads)
    ]
    mixed = summed[:, :column] / by_head((owned, column), whole)
    r.mixed[:, :column] = mixed
    r.mixed[:, column:] = pick_lanes(
        (owned, d.packed - column), [(h, -jnp.log2(whole[h])) for h in range(heads)]
    )
    r.head_parts[r.head] = nn(mixed.astype(low), r.rout[...]).astype(low)
    moved = spread_of(r, d, "head", lambda peer: r.head_parts.at[r.head], r.head_parts, r.head_sems)
    moved.start()
    moved.wait()
    latents_one = latents_wide
    for s in range(d.head_count):
        latents_one = latents_one + r.head_parts[s].astype(jnp.float32)
    r.lat_one[...] = latents_one
    normed_one = norm_parts(latents_one)[0].astype(low)
    r.pair_all[r.tok, :, :column] = nt(normed_one, r.wkey[...]).astype(low)
    r.pair_all[r.tok, :, column:] = nt(normed_one, r.wvalue[...]).astype(low)
    pairs = spread_of(r, d, "tok", lambda peer: r.pair_all.at[r.tok], r.pair_all, r.pair_sems)
    pairs.start()
    pairs.wait()

    def unpack(b, carry):
        start, here = block_at(d, b)
        wide = r.pair_all[pl.ds(b * d.per, d.per)].reshape(d.block, 2 * column)
        for h in range(heads):
            r.key[h, here, :] = wide[:, head_rows(h)]
            r.value[h, here, :] = wide[:, head_rows(heads + h)]
        turned = wide.T
        r.key_t[:, here] = turned[:column]
        r.value_t[:, here] = turned[column:]
        return carry

    each_block(d, unpack, 0)


def mlp_scatters(r):
    return (
        Scatter(r, r.parts_in, r.in_one, r.in_two, r.in_sems),
        Scatter(r, r.parts_out, r.out_one, r.out_two, r.out_sems),
    )


def cross_f(r, c):
    core, side = chunk_core_side(r)
    return pltpu.make_async_remote_copy(
        src_ref=r.f_half.at[c, 1 - side],
        dst_ref=r.f_cross.at[c],
        send_sem=r.f_sems.at[0, c],
        recv_sem=r.f_sems.at[1, c],
        device_id=(r.tok, (1 - side) * 2 + core),
        device_id_type=MESH,
    )


def middle_phase(r, d, merged):
    chunks, heads, width = d.chunks, d.heads, d.width
    core, side = chunk_core_side(r)
    other = 1 - core
    for k in range(1 if merged else 0, 4):
        load(r, k).wait()
    if not merged:
        peer_weights(r).start()
    peer_weights(r).wait()

    def copy(kind, chunk, source, target, across):
        return middle_copy(r, kind, chunk, source, target, across)

    def mixed_copy(c):
        return copy(0, c, r.mixed_t.at[c, 1 - side], r.mixed_got.at[c], True)

    def core_a(c):
        return copy(1, c, r.send_a, r.got_a.at[lax.rem(c, 2)], False)

    def core_u(c):
        return copy(2, c, r.update.at[c, side, core], r.update.at[c, side, core], False)

    def cross_u(c):
        return copy(3, c, r.update.at[c, side, core], r.update.at[c, side, core], True)

    def core_v(c):
        return copy(4, c, r.update.at[c, 1 - side, core], r.update.at[c, 1 - side, core], False)

    def core_d(c):
        return copy(5, c, r.send_d, r.got_d.at[lax.rem(c, 2)], False)

    def half_d(c, x, count):
        at = pl.multiple_of(lax.rem(c, 4) * 2 * SUB + x * SUB, SUB)
        return r.store.at[4 + c // 4, pl.ds(at, count), :]

    def cross_d(c):
        return r.store.at[6, pl.ds(pl.multiple_of(c * SUB, SUB), SUB), :]

    def cross_copy_d(c):
        return copy(6, c, half_d(c, 1 - side, SUB), cross_d(c), True)

    def core_s(c):
        half = r.narrow_s.at[lax.rem(c, 4), core]
        return copy(7, c, half, half, False)

    def core_f(c):
        return copy(8, c, r.send_f, r.got_f.at[lax.rem(c, 2)], False)

    def cross_o(c):
        return copy(9, c, r.mixed_send.at[lax.rem(c, 4)], r.grad_mixed_t.at[c, side], True)

    def latent_images(start):
        row = lax.broadcasted_iota(jnp.int32, r.latent_image.shape, 0) + start
        return image_of(r.counts, lax.shift_right_logical(row, 3))

    if d.blocks == 1:
        r.latent_image[...] = latent_images(0)

    def mask_of(c, b):
        image = r.latent_image[...] if d.blocks == 1 else latent_images(b * d.block)
        image = jnp.concatenate([image, image], axis=1)
        lane = lax.broadcasted_iota(jnp.int32, (1, 4 * SUB), 1)
        part = lax.shift_right_logical(lane, 6)
        row = part * d.quarter + c * SUB
        group = r.tok * d.groups_here + lax.shift_right_logical(row, 8)
        return jnp.where(image == image_of(r.counts, group), 0.0, MASKED)

    r.acc_in[...] = jnp.zeros_like(r.acc_in)
    r.acc_out[...] = jnp.zeros_like(r.acc_out)
    r.acc_write[...] = jnp.zeros_like(r.acc_write)
    r.grad_key[...] = jnp.zeros_like(r.grad_key)
    r.grad_value[...] = jnp.zeros_like(r.grad_value)

    def write_forward(c):
        query = r.query_t[c]

        def body(b, carry):
            here = block_at(d, b)[1]
            bias = mask_of(c, b)
            kept = []
            for h in range(heads):
                scores = nn(r.key[h, here, :], query[head_rows(h)])
                weights = jnp.exp2(scores * (SCALE * LOG2E) + bias)
                total = jnp.sum(weights, axis=0, keepdims=True)
                mixed = nn(r.value_t[head_rows(h), here], weights.astype(jnp.bfloat16))
                kept.append((carry[h][0] + total, carry[h][1] + mixed))
            return tuple(kept)

        size = 4 * SUB
        zero = (jnp.zeros((1, size), jnp.float32), jnp.zeros((HD, size), jnp.float32))
        totals = each_block(d, body, (zero,) * heads)
        mixed = jnp.concatenate([part / total for total, part in totals], axis=0)
        mixed = mixed.astype(jnp.bfloat16)
        r.mixed_t[c, 0] = mixed[:, : 2 * SUB]
        r.mixed_t[c, 1] = mixed[:, 2 * SUB :]
        mixed_copy(c).start()
        for h in range(heads):
            r.log_total[c, h : h + 1] = -jnp.log2(totals[h][0])

    def part_update(c):
        mixed_copy(c).wait()
        part = tn(r.mixed_t[c, side], r.write_out[...]) + tn(r.mixed_got[c], r.wo_peer[...])
        r.part_s[...] = part.reshape(r.part_s.shape)
        r.send_a[...] = r.part_s[other].astype(jnp.bfloat16)
        core_a(c).start()

    def own_update(c):
        core_a(c).wait()
        total = r.part_s[core] + r.got_a[lax.rem(c, 2)].astype(jnp.float32)
        r.update[c, side, core] = total.astype(jnp.bfloat16)
        cross_u(c).start()
        core_u(c).start()

    def pass_update(c):
        cross_u(c).wait()
        core_v(c).start()

    def one_rows(c):
        moved = r.update[c].reshape(4 * SUB, width).astype(jnp.float32)
        return chunk_rows(r.tokens, c).astype(jnp.float32) + moved

    def feed_forward(c):
        core_u(c).wait()
        core_v(c).wait()
        normed = norm_parts(one_rows(c))[0].astype(jnp.bfloat16)
        r.normed_s[...] = normed
        inner = nn(normed, r.mlp_in[...])
        square = inner * inner
        tanh = jnp.tanh(GELU_A * inner * (1.0 + GELU_B * square))
        half = 0.5 + 0.5 * tanh
        active = (inner * half).astype(jnp.bfloat16)
        r.act_s[...] = active
        slope = half + 0.5 * GELU_A * inner * (1.0 - tanh * tanh) * (1.0 + 3.0 * GELU_B * square)
        grad_inner = (nt(chunk_rows(r.store, c), r.mlp_out[...]) * slope).astype(jnp.bfloat16)
        r.inner_s[...] = grad_inner
        halve(r, nt(grad_inner, r.mlp_in[...]), r.own_d, r.send_d)
        core_d(c).start()
        halve(r, nn(active, r.mlp_out[...]), r.own_f, r.send_f)
        core_f(c).start()

    def finish_grad(c):
        cross_copy_d(c).wait()
        grad = half_d(c, side, SUB)[...].astype(jnp.float32) + cross_d(c)[...].astype(jnp.float32)
        part = pl.ds(pl.multiple_of(c * SUB, SUB), SUB)
        rows = r.tokens[r.head, part, :].astype(jnp.float32) + r.update[c, side, core].astype(jnp.float32)
        normed, scale = norm_parts(rows)
        wide = r.store[r.head, part, :].astype(jnp.float32) + norm_vjp(normed, scale, grad)
        r.grad_one[part, :] = wide
        r.narrow_s[lax.rem(c, 4), core] = wide.astype(jnp.bfloat16)
        core_s(c).start()

    def send_mixed_grad(c):
        core_s(c).wait()
        narrow = r.narrow_s[lax.rem(c, 4)].reshape(2 * SUB, width)
        r.mixed_send[lax.rem(c, 4)] = nt(r.wo_peer[...], narrow).astype(jnp.bfloat16)
        cross_o(c).start()
        r.grad_mixed_t[c, side] = nt(r.write_out[...], narrow).astype(jnp.bfloat16)
        r.acc_write[0] += nn(r.mixed_t[c, side], narrow)
        r.acc_write[1] += nn(r.mixed_got[c], narrow)

    def cross_grad(c):
        slot = lax.rem(c, 2)
        core_d(c).wait()
        total = (r.own_d[...] + r.got_d[slot].astype(jnp.float32)).astype(jnp.bfloat16)
        half_d(c, 0, 2 * SUB)[...] = total.reshape(2 * SUB, width)

    def keep_forward(c):
        slot = lax.rem(c, 2)
        core_f(c).wait()
        total = r.own_f[...] + r.got_f[slot].astype(jnp.float32)
        r.f_half[c] = total.astype(jnp.bfloat16)
        part = pl.ds(pl.multiple_of(c * SUB, SUB), SUB)
        mine = jnp.where(side == 0, total[0], total[1]) + r.update[c, side, core].astype(jnp.float32)
        r.f_half[c, side] = (mine + r.tokens[r.head, part, :].astype(jnp.float32)).astype(jnp.bfloat16)

    def weight_grads(c):
        r.acc_in[...] += tn(r.normed_s[...], r.inner_s[...])
        r.acc_out[...] += tn(chunk_rows(r.store, c), r.act_s[...])

    def write_backward(c):
        cross_o(c).wait()
        mixed = jnp.concatenate([r.mixed_t[c, 0], r.mixed_t[c, 1]], axis=1)
        grad_mixed = jnp.concatenate([r.grad_mixed_t[c, 0], r.grad_mixed_t[c, 1]], axis=1)
        query = r.query_t[c]
        product = grad_mixed.astype(jnp.float32) * mixed.astype(jnp.float32)

        def body(b, carry):
            here = block_at(d, b)[1]
            bias = mask_of(c, b)
            kept = []
            for h in range(heads):
                rows = head_rows(h)
                scores = nn(r.key[h, here, :], query[rows])
                weights = jnp.exp2(scores * (SCALE * LOG2E) + (bias + r.log_total[c, h : h + 1]))
                grad_weights = nn(r.value[h, here, :], grad_mixed[rows])
                delta = jnp.sum(product[rows], axis=0, keepdims=True)
                grad_scores = (weights * (grad_weights - delta)).astype(jnp.bfloat16)
                r.grad_key[h, here, :] += nt(grad_scores, query[rows])
                r.grad_value[h, here, :] += nt(weights.astype(jnp.bfloat16), grad_mixed[rows])
                kept.append(carry[h] + nn(r.key_t[rows, here], grad_scores))
            return tuple(kept)

        zero = jnp.zeros((HD, 4 * SUB), jnp.float32)
        grads = each_block(d, body, (zero,) * heads)
        r.grad_query_t[c] = (jnp.concatenate(grads, axis=0) * SCALE).astype(jnp.bfloat16)

    def between(first, i, last):
        return pl.when(jnp.logical_and(i >= first, i < last))

    def step(i, carry):
        @between(3, i, chunks + 3)
        def _():
            pass_update(i - 3)

        def write(c, carry):
            write_forward(c)
            return carry

        lax.fori_loop(jnp.minimum(WRITES * i, chunks), jnp.minimum(WRITES * (i + 1), chunks), write, 0)

        @between(1, i, chunks + 1)
        def _():
            part_update(i - 1)

        @pl.when(i >= 4)
        def _():
            weight_grads(i - 4)
            keep_forward(i - 4)
            cross_grad(i - 4)

        @between(1, i, chunks + 1)
        def _():
            own_update(i - 1)

        @pl.when(i > chunks)
        def _():
            cross_copy_d(i - chunks - 1).start()

        @between(3, i, chunks + 3)
        def _():
            feed_forward(i - 3)

        return carry

    ahead = 3
    lax.fori_loop(0, chunks + 4, step, 0)
    put_parts(d, r.parts_in, 0, r.acc_in)
    put_parts(d, r.parts_out, 0, r.acc_out)
    by_in, by_out = mlp_scatters(r) if merged else (None, None)

    def back_step(c, carry):
        @pl.when(c < chunks)
        def _():
            finish_grad(c)

        @pl.when(c + ahead < chunks)
        def _():
            cross_copy_d(c + ahead).start()

        if merged:
            trickle(by_in, c)
            trickle(by_out, c - d.outer)

        @between(1, c, chunks + 1)
        def _():
            send_mixed_grad(c - 1)

        @pl.when(c >= 3)
        def _():
            write_backward(c - 3)

        return carry

    lax.fori_loop(0, chunks + 3, back_step, 0)
    r.wo_send[...] = r.acc_write[1].astype(jnp.bfloat16)
    peer_grads(r).start()
    def pack(b, carry):
        here = block_at(d, b)[1]
        there = pl.ds(b * d.per, d.per)
        both = [r.grad_key[h, here, :] * SCALE for h in range(heads)]
        both += [r.grad_value[h, here, :] for h in range(heads)]
        wide = jnp.concatenate(both, axis=1).astype(jnp.bfloat16)
        r.grad_pairs[there] = wide.reshape(d.per, d.owned, 2 * d.column)
        return carry

    each_block(d, pack, 0)
    if not merged:
        finish_write_out(r)


def trickle(scatter, k):
    pl.when(jnp.logical_and(k >= 0, k < scatter.outer))(partial(scatter.start_block, k))
    pl.when(jnp.logical_and(k >= LAG, k < LAG + scatter.outer - 1))(partial(scatter.forward_block, k - LAG))


def put_parts(d, ref, at, value):
    width = value.shape[1]
    for b in range(d.tok_count):
        rows = slice(b * d.share, (b + 1) * d.share)
        ref[b // 2, b % 2, :, at : at + width] = value[rows, :].astype(jnp.bfloat16)


def back_phase(r, d, merged):
    chunks, heads, width, column, owned = d.chunks, d.heads, d.width, d.column, d.owned
    low, wide = jnp.bfloat16, jnp.float32
    core, side = chunk_core_side(r)
    other = 1 - core
    pairs = spread_of(r, d, "tok", lambda peer: r.grad_pairs.at[peer], r.got_pairs, r.pairs_sems)
    pairs.start()
    by_in, by_out = mlp_scatters(r)
    early = Scatter(r, r.parts_early, r.early_one, r.early_two, r.early_sems)
    later = Scatter(r, r.parts_second, r.second_one, r.second_two, r.second_sems)
    late = Scatter(r, r.parts_late, r.late_one, r.late_two, r.late_sems)
    final = Scatter(r, r.parts_final, r.final_one, r.final_two, r.final_sems)
    if not merged:
        by_in.start()
        by_out.start()
    first_f = chunks // 2
    for c in range(first_f):
        cross_f(r, c).start()
    r.acc_in[...] = jnp.zeros_like(r.acc_in)
    r.acc_out[...] = jnp.zeros_like(r.acc_out)
    at_key, at_value = slice(0, column), slice(256, 256 + column)

    def plain_weights(key, h, here, masks):
        scores = nn(key, r.read_query_t[head_rows(h), here]) * (SCALE * LOG2E)
        return jnp.exp2(add_rows(scores, masks))

    def masks_of(b, images):
        start, here = block_at(d, b)
        row_image = latent_row_image(r.counts, start, d.block)
        return [jnp.where(row_image == image, 0.0, MASKED) for image in images]

    def keep_weights(first, last):
        def keep(c, carry):
            masks = masks_of(0, token_images(r, d, c))
            top, low_rows = slice(0, 4 * SUB), slice(4 * SUB, 8 * SUB)
            for h in range(heads):
                weights = plain_weights(r.read_key[c, h], h, slice(0, d.block), masks).astype(low)
                if h == 0:
                    r.store[c, top, 0:512] = weights
                elif h == 1:
                    r.store[c, top, 512:768] = weights[:, 0:256]
                    r.store[c, low_rows, 0:256] = weights[:, 256:512]
                else:
                    r.store[c, low_rows, 256:768] = weights
            return carry

        if keeps_weights(d):
            lax.fori_loop(first, last, keep, 0)

    def kept_weights(c, h):
        top, low_rows = slice(0, 4 * SUB), slice(4 * SUB, 8 * SUB)
        if h == 0:
            return r.store[c, top, 0:512]
        if h == 1:
            return jnp.concatenate([r.store[c, top, 512:768], r.store[c, low_rows, 0:256]], axis=1)
        return r.store[c, low_rows, 256:768]

    def query_weights(c, carry):
        normed = norm_parts(chunk_rows(r.tokens, c).astype(wide))[0].astype(low)
        r.update[c] = normed.reshape(r.update.shape[1:])
        r.acc_in[:, :column] += tn(normed, r.grad_query_t[c].T)
        return carry

    lax.fori_loop(0, chunks, query_weights, 0)
    put_parts(d, r.parts_early, 0, r.acc_in[:, :column])
    keep_weights(0, chunks // 2)
    if merged:
        finish_write_out(r)
    put_parts(d, r.parts_early, column, r.grad_write)
    pairs.wait()
    early.start()
    if not merged:
        by_in.forward()
        by_out.forward()
    r.got_pairs[r.tok] = r.grad_pairs[r.tok]
    summed = sum_slots(r.got_pairs, d.tok_count).astype(low)
    grad_key, grad_value = summed[:, :column], summed[:, column:]
    r.head_parts[r.head] = (nn(grad_key, r.wkey[...]) + nn(grad_value, r.wvalue[...])).astype(low)
    moved = spread_of(r, d, "head", lambda peer: r.head_parts.at[r.head], r.head_parts, r.heads_sems)
    moved.start()
    keep_weights(chunks // 2, 3 * chunks // 4)
    normed_one, scale_one = norm_parts(r.lat_one[...])
    put_parts(d, r.parts_second, 0, tn(normed_one.astype(low), summed))
    moved.wait()
    grad_lat_one = norm_vjp(normed_one, scale_one, sum_slots(r.head_parts, d.head_count))
    r.grad_own[...] = grad_lat_one
    narrow = grad_lat_one.astype(low)
    grad_mixed = nt(narrow, r.rout[...]).astype(low)
    mixed = r.mixed[:, :column]
    product = grad_mixed.astype(wide) * mixed
    extra = []
    for h in range(heads):
        delta = jnp.sum(product[:, head_rows(h)], axis=1, keepdims=True)
        logs = r.mixed[:, column + h : column + h + 1]
        for k, (first, second) in enumerate(zip(split_three(delta), split_three(logs), strict=True)):
            extra.append((3 * h + k, first))
            extra.append((3 * (heads + h) + k, second))
    r.output_all[r.tok, :, :column] = grad_mixed
    r.output_all[r.tok, :, column:] = pick_lanes((owned, d.packed - column), extra).astype(low)
    outputs = spread_of(r, d, "tok", lambda peer: r.output_all.at[r.tok], r.output_all, r.output_sems)
    outputs.start()
    put_parts(d, r.parts_second, 2 * column, tn(narrow, mixed.astype(low)))
    r.query_sum[...] = jnp.zeros_like(r.query_sum)
    keep_weights(3 * chunks // 4, chunks)
    outputs.wait()
    early.forward()

    def turn(b, carry):
        here = block_at(d, b)[1]
        turned = r.output_all[pl.ds(b * d.per, d.per)].reshape(d.block, d.packed).astype(wide).T
        def joined(k):
            at = column + 3 * k
            return turned[at : at + 1] + turned[at + 1 : at + 2] + turned[at + 2 : at + 3]

        for h in range(heads):
            inverse = jnp.exp2(joined(heads + h))
            r.output_t[head_rows(h), here] = (turned[head_rows(h)] * inverse).astype(low)
            r.rows[h : h + 1, here] = joined(h) * inverse
        return carry

    each_block(d, turn, 0)

    def key_grads(count, weights_of, value_of, key_t_of, images):
        def body(b, carry):
            here = block_at(d, b)[1]
            masks = masks_of(b, images)
            kept = []
            for h in range(heads):
                hr = head_rows(h)
                query, output = r.read_query_t[hr, here], r.output_t[hr, here]
                weights = weights_of(h, here, masks)
                grad_weights = nn(value_of(h), output) - r.rows[h : h + 1, here]
                grad_scores = (weights.astype(wide) * grad_weights).astype(low)
                r.query_sum[hr, here] += nn(key_t_of(h), grad_scores)
                kept.append(
                    (carry[h][0] + nt(grad_scores, query), carry[h][1] + nt(weights.astype(low), output))
                )
            return tuple(kept)

        zero = jnp.zeros((count, HD), wide)
        grads = each_block(d, body, ((zero, zero),) * heads)
        keys = jnp.concatenate([grads[h][0] for h in range(heads)], axis=1) * SCALE
        values = jnp.concatenate([grads[h][1] for h in range(heads)], axis=1)
        return keys.astype(low), values.astype(low)

    def core_copy(c):
        slot = lax.rem(c, 2)
        return pltpu.make_async_remote_copy(
            src_ref=r.send_f,
            dst_ref=r.got_f.at[slot],
            send_sem=r.core_sems.at[0, slot],
            recv_sem=r.core_sems.at[1, slot],
            device_id=(r.tok, side * 2 + other),
            device_id_type=MESH,
        )

    def cross_copy(c):
        return pltpu.make_async_remote_copy(
            src_ref=r.x_half.at[c, 1 - side],
            dst_ref=r.x_cross.at[c],
            send_sem=r.x_sems.at[0, c],
            recv_sem=r.x_sems.at[1, c],
            device_id=(r.tok, (1 - side) * 2 + core),
            device_id_type=MESH,
        )

    def compute(c):
        def weights_of(h, here, masks):
            return kept_weights(c, h) if keeps_weights(d) else plain_weights(r.read_key[c, h], h, here, masks)

        dk, dv = key_grads(
            4 * SUB,
            weights_of,
            lambda h: r.read_value[c, h],
            lambda h: r.read_key_t[c, head_rows(h), :],
            token_images(r, d, c),
        )
        moved = nn(dk, r.rkey[...]) + nn(dv, r.rvalue[...]) + tn(r.grad_query_t[c], r.wquery[...])
        halve(r, moved, r.own_f, r.send_f)
        core_copy(c).start()
        normed = r.update[c].reshape(4 * SUB, width)
        r.acc_out[:, at_key] += tn(normed, dk)
        r.acc_out[:, at_value] += tn(normed, dv)

    def cross(c):
        core_copy(c).wait()
        total = r.own_f[...] + r.got_f[lax.rem(c, 2)].astype(wide)
        r.x_half[c] = total.astype(low)
        cross_copy(c).start()

    def step(c, carry):
        @pl.when(c >= 1)
        def _():
            cross(c - 1)

        @pl.when(c >= first_f)
        def _():
            cross_f(r, c).start()

        compute(c)
        if few:
            trickle(later, c)
        return carry

    few = d.outer + LAG <= chunks
    if not few:
        later.start()
        later.forward()
    lax.fori_loop(0, chunks // 2, step, 0)
    lax.fori_loop(chunks // 2, chunks, step, 0)
    own_dk, own_dv = key_grads(
        owned,
        lambda h, here, masks: plain_weights(r.own_key[h], h, here, masks),
        lambda h: r.own_value[h],
        lambda h: r.own_key_t[head_rows(h), :],
        [image_of(r.counts, r.tok * d.groups_here + g) for g in range(d.groups_here)],
    )

    def turn_query(b, carry):
        here = block_at(d, b)[1]
        turned = (r.query_sum[:, here] * SCALE).T.astype(low)
        r.query_send[pl.ds(b * d.per, d.per)] = turned.reshape(d.per, owned, column)
        return carry

    each_block(d, turn_query, 0)
    queries = spread_of(r, d, "tok", lambda peer: r.query_send.at[peer], r.query_got, r.back_query_sems)
    queries.start()
    cross(chunks - 1)
    normed_lat, scale_lat = norm_parts(r.latents[...].astype(wide))
    narrow_lat = normed_lat.astype(low)
    put_parts(d, r.parts_late, 0, r.acc_out[:, at_key] + tn(narrow_lat, own_dk))
    put_parts(d, r.parts_late, column, r.acc_out[:, at_value] + tn(narrow_lat, own_dv))
    late.start()
    queries.wait()
    r.query_got[r.tok] = r.query_send[r.tok]
    grad_query = sum_slots(r.query_got, d.tok_count).astype(low)
    lat_total = nn(grad_query, r.rquery[...]) + nn(own_dk, r.rkey[...]) + nn(own_dv, r.rvalue[...])
    r.lat_parts[...] = lat_total.astype(low).reshape(r.lat_parts.shape)
    lats = spread_of(r, d, "head", lambda peer: r.lat_parts.at[peer], r.lat_got, r.lat_sems)
    lats.start()
    put_parts(d, r.parts_final, 0, tn(narrow_lat, grad_query))
    final.start()
    late.forward()
    by_in.finish()
    final.forward()
    lats.wait()
    r.lat_got[r.head] = r.lat_parts[r.head]
    total = sum_slots(r.lat_got, d.head_count)
    count = owned // d.head_count
    mine = pl.ds(pl.multiple_of(r.head * count, count), count)
    normed, scale = norm_parts(r.latents[mine, :].astype(wide))
    r.lat_grad[...] = r.grad_own[mine, :] + norm_vjp(normed, scale, total)
    by_out.finish()
    early.finish()
    later.finish()

    def wait_cross(c, carry):
        cross_copy(c).wait()
        cross_f(r, c).wait()
        return carry

    lax.fori_loop(0, chunks, wait_cross, 0)
    late.finish()
    final.finish()


FRONT, MIDDLE, BACK = 1, 2, 4
OWN, CARRY, OUT = 0, 1, 2


def keeps_weights(d):
    return d.blocks == 1 and d.heads * d.block == 2 * d.width and d.chunks == 8 and d.quarter == 8 * SUB


def buffers(d):
    low, wide = jnp.bfloat16, jnp.float32
    size, half = 4 * SUB, (2, SUB, d.width)
    n, h = d.tok_count, d.head_count
    front, middle, back = FRONT, MIDDLE, BACK
    every = front | middle | back
    by_chunk = (d.chunks, d.column, size)
    by_head, by_column = (d.heads, d.latent_count, HD), (d.column, d.latent_count)
    key_heads, own_heads = (d.chunks, d.heads, size, HD), (d.heads, d.owned, HD)
    pairs, queries, wide_rows = (n, d.owned, 2 * d.column), (n, d.owned, d.column), (n, d.owned, d.packed)
    halves, quarters = (d.chunks, 2, SUB, d.width), (d.chunks, SUB, d.width)
    tok_sems, head_sems, sum_sems = (2, n), (2, h), (4, d.outer)

    def slots(columns):
        return (d.outer, d.share, columns)

    def parts(columns):
        return (d.outer, 2, d.share, columns)

    return dict(
        query_t=(by_chunk, low, front | middle, CARRY),
        key=(by_head, low, front | middle, CARRY),
        value=(by_head, low, front | middle, CARRY),
        key_t=(by_column, low, front | middle, CARRY),
        value_t=(by_column, low, front | middle, CARRY),
        read_key=(key_heads, low, front | back, CARRY),
        read_value=(key_heads, low, front | back, CARRY),
        read_key_t=(by_chunk, low, front | back, CARRY),
        read_value_t=(by_chunk, low, front, OWN),
        own_key=(own_heads, low, front | back, CARRY),
        own_value=(own_heads, low, front | back, CARRY),
        own_key_t=((d.column, d.owned), low, front | back, CARRY),
        own_value_t=((d.column, d.owned), low, front, OWN),
        read_query_t=(by_column, low, front | back, CARRY),
        lat_one=((d.owned, d.width), wide, front | back, CARRY),
        mixed=((d.owned, d.packed), wide, front | back, CARRY),
        update=((d.chunks, 2, 2, SUB, d.width), low, every, OWN),
        query_all=(queries, low, front, OWN),
        sums=((d.packed, d.latent_count), wide, front, OWN),
        sums_send=(wide_rows, low, front, OWN),
        sums_got=(wide_rows, low, front, OWN),
        head_parts=((h, d.owned, d.width), low, front | back, OWN),
        pair_all=(pairs, low, front, OWN),
        query_sems=(tok_sems, None, front, OWN),
        sums_sems=(tok_sems, None, front, OWN),
        head_sems=(head_sems, None, front, OWN),
        pair_sems=(tok_sems, None, front, OWN),
        grad_one=((d.quarter, d.width), wide, middle, OUT),
        grad_query_t=(by_chunk, low, middle | back, CARRY),
        grad_pairs=(pairs, low, middle | back, CARRY),
        parts_in=(parts(d.hidden), low, middle | back, CARRY),
        parts_out=(parts(d.hidden), low, middle | back, CARRY),
        grad_write=((d.width, d.column), low, middle | back, CARRY),
        f_half=(halves, low, middle | back, OUT),
        write_out=((d.column, d.width), low, middle, OWN),
        mlp_in=((d.width, d.hidden), low, middle, OWN),
        mlp_out=((d.hidden, d.width), low, middle, OWN),
        store=((8, d.quarter, d.width), low, middle | back if keeps_weights(d) else middle, OWN),
        mixed_t=((d.chunks, 2, d.column, 2 * SUB), low, middle, OWN),
        log_total=((d.chunks, 8, size), wide, middle, OWN),
        send_a=((SUB, d.width), low, middle, OWN),
        got_a=(half, low, middle, OWN),
        part_s=(half, wide, middle, OWN),
        mixed_got=((d.chunks, d.column, 2 * SUB), low, middle, OWN),
        grad_mixed_t=((d.chunks, 2, d.column, 2 * SUB), low, middle, OWN),
        mixed_send=((4, d.column, 2 * SUB), low, middle, OWN),
        narrow_s=((4, *half), low, middle, OWN),
        wo_peer=((d.column, d.width), low, middle, OWN),
        wo_send=((d.column, d.width), low, middle, OWN),
        wo_got=((d.column, d.width), low, middle, OWN),
        own_d=(half, wide, middle, OWN),
        send_d=(half, low, middle, OWN),
        got_d=((2, *half), low, middle, OWN),
        own_f=(half, wide, middle | back, OWN),
        send_f=(half, low, middle | back, OWN),
        got_f=((2, *half), low, middle | back, OWN),
        acc_in=((d.width, d.hidden), wide, middle | back, OWN),
        acc_out=((d.width, d.hidden), wide, middle | back, OWN),
        acc_write=((2, d.column, d.width), wide, middle, OWN),
        normed_s=((size, d.width), low, middle, OWN),
        act_s=((size, d.hidden), low, middle, OWN),
        inner_s=((size, d.hidden), low, middle, OWN),
        wide_s=((2, *half), wide, middle | back, OWN),
        latent_image=((d.block, 128), jnp.int32, middle, OWN),
        grad_key=(by_head, wide, middle, OWN),
        grad_value=(by_head, wide, middle, OWN),
        send_sems=((12, d.chunks), None, middle, OWN),
        recv_sems=((12, d.chunks), None, middle, OWN),
        load_sems=((4,), None, middle, OWN),
        f_cross=(quarters, low, back, OUT),
        x_half=(halves, low, back, OUT),
        x_cross=(quarters, low, back, OUT),
        in_two=(slots(d.hidden), low, back, OUT),
        out_two=(slots(d.hidden), low, back, OUT),
        early_two=(slots(2 * d.column), low, back, OUT),
        second_two=(slots(3 * d.column), low, back, OUT),
        late_two=(slots(2 * d.column), low, back, OUT),
        final_two=(slots(d.column), low, back, OUT),
        lat_grad=((d.owned // h, d.width), wide, back, OUT),
        in_one=(slots(d.hidden), low, back, OWN),
        out_one=(slots(d.hidden), low, back, OWN),
        early_one=(slots(2 * d.column), low, back, OWN),
        second_one=(slots(3 * d.column), low, back, OWN),
        late_one=(slots(2 * d.column), low, back, OWN),
        final_one=(slots(d.column), low, back, OWN),
        parts_early=(parts(2 * d.column), low, back, OWN),
        parts_second=(parts(3 * d.column), low, back, OWN),
        parts_late=(parts(2 * d.column), low, back, OWN),
        parts_final=(parts(d.column), low, back, OWN),
        got_pairs=(pairs, low, back, OWN),
        output_all=(wide_rows, low, back, OWN),
        output_t=(by_column, low, back, OWN),
        rows=((8, d.latent_count), wide, back, OWN),
        grad_own=((d.owned, d.width), wide, back, OWN),
        query_sum=(by_column, wide, back, OWN),
        query_send=(queries, low, back, OWN),
        query_got=(queries, low, back, OWN),
        lat_parts=((h, d.owned // h, d.width), low, back, OWN),
        lat_got=((h, d.owned // h, d.width), low, back, OWN),
        in_sems=(sum_sems, None, back, OWN),
        out_sems=(sum_sems, None, back, OWN),
        early_sems=(sum_sems, None, back, OWN),
        second_sems=(sum_sems, None, back, OWN),
        late_sems=(sum_sems, None, back, OWN),
        final_sems=(sum_sems, None, back, OWN),
        pairs_sems=(tok_sems, None, back, OWN),
        heads_sems=(head_sems, None, back, OWN),
        output_sems=(tok_sems, None, back, OWN),
        back_query_sems=(tok_sems, None, back, OWN),
        lat_sems=(head_sems, None, back, OWN),
        core_sems=((2, 2), None, back, OWN),
        x_sems=((2, d.chunks), None, back, OWN),
        f_sems=((2, d.chunks), None, back, OWN),
    )


def run(d, number, phases, inputs, made):
    table = buffers(d)
    later = (FRONT | MIDDLE | BACK) & ~(2 * phases - 1) if phases != FRONT | MIDDLE | BACK else 0
    given = {x: (array, memory) for x, (array, uses, memory) in inputs.items() if uses & phases}
    given |= {x: (made[x], pltpu.VMEM) for x in made if table[x][2] & phases}
    wanted, inside = [], []
    for x, (shape, kind, uses, keep) in table.items():
        if x in given or not uses & phases:
            continue
        (wanted if keep == OUT or (keep == CARRY and uses & later) else inside).append(x)
    names = [*given, *wanted, *inside]
    merged = phases == FRONT | MIDDLE | BACK
    first = ("counts", "latents", "rquery")
    loaded = [x for x, (array, memory) in given.items() if merged and memory == pltpu.VMEM and x not in first]
    given = {x: (array, pl.ANY if x in loaded else memory) for x, (array, memory) in given.items()}

    def kernel(*refs):
        found = dict(zip(names, refs[: len(names)], strict=True))
        targets = refs[len(names) :]
        pending = [
            pltpu.make_async_copy(found[x], targets[k], targets[-1].at[k]) for k, x in enumerate(loaded)
        ]
        found |= dict(zip(loaded, targets))
        r = SimpleNamespace(**found, pending=pending)
        for copy in pending:
            copy.start()
        r.tok, r.head = lax.axis_index("tok"), lax.axis_index("head")
        if phases & MIDDLE:
            for k in range(4):
                load(r, k).start()
        if not phases & FRONT:
            greet_all(r, d)
        if phases & FRONT:
            front_phase(r, d, merged)
        if phases & MIDDLE:
            middle_phase(r, d, merged)
        if phases & BACK:
            back_phase(r, d, merged)

    def scratch(x):
        shape, kind = table[x][:2]
        return pltpu.SemaphoreType.DMA(shape) if kind is None else pltpu.VMEM(shape, kind)

    out = pl.pallas_call(
        kernel,
        out_shape=[jax.ShapeDtypeStruct(*table[x][:2]) for x in wanted],
        in_specs=[pl.BlockSpec(memory_space=memory) for array, memory in given.values()],
        out_specs=[pl.BlockSpec(memory_space=pltpu.VMEM) for x in wanted],
        scratch_shapes=[scratch(x) for x in inside]
        + [pltpu.VMEM(given[x][0].shape, given[x][0].dtype) for x in loaded]
        + [pltpu.SemaphoreType.DMA((len(loaded),))] * min(1, len(loaded)),
        compiler_params=pltpu.CompilerParams(
            collective_id=number, has_side_effects=True, vmem_limit_bytes=127 << 19
        ),
        name="phases%d" % phases,
    )(*[array for array, memory in given.values()])
    return dict(zip(wanted, out, strict=True))


def finish_kernel(
    index, tokens, grad_one, f_own, f_cross, x_own, x_cross, in_two, out_two, early_two, early_all, second_two, second_all, late_two, final_two, lat,
    layer_out, input_grad, latent_grad, g_rquery, g_rkey, g_rvalue, g_rout, g_wquery, g_wkey, g_wvalue, g_wout,
    g_in, g_out,
):
    wide = jnp.float32
    column = final_two.shape[2]
    rows, width = grad_one.shape

    def both(own, cross):
        return (own[...].astype(wide).reshape(rows, width)) + cross[...].astype(wide).reshape(rows, width)

    layer_out[...] = both(f_own, f_cross).astype(jnp.bfloat16)
    normed, scale = norm_parts(tokens[0].astype(wide))
    input_grad[...] = grad_one[...] + norm_vjp(normed, scale, both(x_own, x_cross))
    latent_grad[...] = lat[...]

    def total(ref):
        kept = ref[0].astype(wide)
        for s in range(1, ref.shape[0]):
            kept = kept + ref[s].astype(wide)
        return kept

    g_in[...] = total(in_two)
    g_out[...] = total(out_two)
    g_rquery[...] = total(final_two)
    late = total(late_two)
    g_rkey[...] = late[:, :column]
    g_rvalue[...] = late[:, column:]
    g_wquery[...] = total(early_two)[:, :column]
    second = total(second_two)
    g_wkey[...] = second[:, :column]
    g_wvalue[...] = second[:, column : 2 * column]

    @pl.when(pl.program_id(0) == 0)
    def _():
        g_wout[...] = total(early_all)[:, column:].T
        g_rout[...] = total(second_all)[:, 2 * column :].T


def finish(d, tokens, m):
    steps = 2 if d.share % 32 == 0 else 1
    rows, share, parts = d.quarter // steps, d.share // steps, d.chunks // steps
    head = lax.axis_index("head")
    index = jnp.stack([head, head // 2]).astype(jnp.int32)
    half = pl.BlockSpec((parts, None, SUB, d.width), lambda i, at: (i, at[1], 0, 0))
    cross = pl.BlockSpec((parts, SUB, d.width), lambda i, at: (i, 0, 0))
    strip = pl.BlockSpec((rows, d.width), lambda i, at: (i, 0))
    whole = pl.BlockSpec((d.owned // d.head_count, d.width), lambda i, at: (0, 0))

    def slots(columns):
        return pl.BlockSpec((d.outer, share, columns), lambda i, at: (0, i, 0))

    def part(columns):
        return pl.BlockSpec((share, columns), lambda i, at: (i, 0))

    wide, column = jnp.float32, d.column
    grads = [column] * 8 + [d.hidden] * 2
    turned = (column, d.share)
    return pl.pallas_call(
        finish_kernel,
        out_shape=[
            jax.ShapeDtypeStruct((d.quarter, d.width), jnp.bfloat16),
            jax.ShapeDtypeStruct((d.quarter, d.width), wide),
            jax.ShapeDtypeStruct((d.owned // d.head_count, d.width), wide),
            *[jax.ShapeDtypeStruct(turned if k in (3, 7) else (d.share, columns), wide) for k, columns in enumerate(grads)],
        ],
        grid_spec=pltpu.PrefetchScalarGridSpec(
            num_scalar_prefetch=1,
            grid=(steps,),
            in_specs=[
                pl.BlockSpec((1, rows, d.width), lambda i, at: (at[0], i, 0)),
                strip,
                half,
                cross,
                half,
                cross,
                slots(d.hidden),
                slots(d.hidden),
                slots(2 * column),
                pl.BlockSpec((d.outer, d.share, 2 * column), lambda i, at: (0, 0, 0)),
                slots(3 * column),
                pl.BlockSpec((d.outer, d.share, 3 * column), lambda i, at: (0, 0, 0)),
                slots(2 * column),
                slots(column),
                whole,
            ],
            out_specs=[
                strip,
                strip,
                whole,
                *[
                    pl.BlockSpec(turned, lambda i, at: (0, 0)) if k in (3, 7) else part(columns)
                    for k, columns in enumerate(grads)
                ],
            ],
        ),
        compiler_params=pltpu.CompilerParams(vmem_limit_bytes=62 << 20),
        name="finish",
    )(
        index, tokens, m.grad_one, m.f_half, m.f_cross, m.x_half, m.x_cross, m.in_two, m.out_two, m.early_two,
        m.early_two, m.second_two, m.second_two, m.late_two, m.final_two, m.lat_grad,
    )


def shards(
    tokens,
    latents,
    image_groups,
    read_query,
    read_key,
    read_value,
    read_out,
    write_query,
    write_key,
    write_value,
    write_out,
    mlp_in,
    mlp_out,
    cotangent,
):
    d = SimpleNamespace(tok_count=lax.axis_size("tok"), head_count=lax.axis_size("head"))
    rows, d.width = tokens.shape
    d.owned, d.column, d.hidden, d.packed = latents.shape[0], read_query.shape[1], mlp_in.shape[1], 256
    d.heads, d.quarter, d.groups_here = d.column // HD, rows // 4, rows // GROUP
    d.chunks, d.latent_count = d.quarter // SUB, d.owned * d.tok_count
    d.block = min(512, d.latent_count)
    d.blocks, d.per = d.latent_count // d.block, d.block // d.owned
    d.outer, d.share = d.tok_count // 2, d.width // d.tok_count
    tokens = tokens.reshape(4, d.quarter, d.width)
    every, vmem = FRONT | MIDDLE | BACK, pltpu.VMEM
    inputs = dict(
        counts=(image_groups, every, pltpu.SMEM),
        tokens=(tokens, every, vmem),
        latents=(latents, FRONT | BACK, vmem),
        rquery=(read_query.T, FRONT | BACK, vmem),
        rkey=(read_key.T, FRONT | BACK, vmem),
        rvalue=(read_value.T, FRONT | BACK, vmem),
        rout=(read_out, FRONT | BACK, vmem),
        wquery=(write_query.T, FRONT | BACK, vmem),
        wkey=(write_key.T, FRONT | BACK, vmem),
        wvalue=(write_value.T, FRONT | BACK, vmem),
        write_out_hbm=(write_out, MIDDLE, pl.ANY),
        mlp_in_hbm=(mlp_in, MIDDLE, pl.ANY),
        mlp_out_hbm=(mlp_out, MIDDLE, pl.ANY),
        cotangent_hbm=(cotangent.reshape(4, d.quarter, d.width), MIDDLE, pl.ANY),
    )
    made = {}
    for number, phases in enumerate([every] if d.latent_count <= 512 else [FRONT, MIDDLE, BACK]):
        made |= run(d, number, phases, inputs, made)
    (
        layer_out, input_grad, latent_grad, g_rquery, g_rkey, g_rvalue, g_rout, g_wquery, g_wkey, g_wvalue, g_wout,
        g_in, g_out,
    ) = finish(d, tokens, SimpleNamespace(**made))
    return (
        layer_out,
        input_grad,
        latent_grad,
        g_rquery,
        g_rkey,
        g_rvalue,
        g_rout,
        g_wquery,
        g_wkey,
        g_wvalue,
        g_wout,
        g_in,
        g_out.T,
    )


def solution(mesh):
    return jax.shard_map(
        shards,
        mesh=mesh,
        in_specs=(
            P("tok", None),
            P("tok", None),
            P(),
            P(None, "head"),
            P(None, "head"),
            P(None, "head"),
            P("head", None),
            P(None, "head"),
            P(None, "head"),
            P(None, "head"),
            P("head", None),
            P(None, "head"),
            P("head", None),
            P("tok", None),
        ),
        out_specs=(
            P(("tok", "head"), None),
            P(("tok", "head"), None),
            P(("tok", "head"), None),
            P("tok", "head"),
            P("tok", "head"),
            P("tok", "head"),
            P("head", "tok"),
            P("tok", "head"),
            P("tok", "head"),
            P("tok", "head"),
            P("head", "tok"),
            P("tok", "head"),
            P("head", "tok"),
        ),
        check_vma=False,
    )
```
